256 devices in a mesh: dp: 16 (over z, y_lo), seq: 16 (over y_hi, x, core).
Axes of the slice: x: 4, y: 4 (y_hi: 2, y_lo: 2; y = y_hi * 2 + y_lo), z: 8, core: 2. Of those that a mesh axis runs over, the one named last changes fastest.
Arguments:
- query_proj: bfloat16 [16, 2048, 1536], P('dp', 'seq'), may hold values from -8 to 8
- key_proj: bfloat16 [16, 2048, 1536], P('dp', 'seq'), may hold values from -8 to 8
- value_proj: bfloat16 [16, 2048, 1536], P('dp', 'seq'), may hold values from -6 to 6
- residual: bfloat16 [16, 2048, 1536], P('dp', 'seq'), may hold values from -3 to 3
- lengths: int32 [16], P('dp'), may hold values from 512 to 2048, as said below
- out_weight: bfloat16 [1536, 1536], replicated, may hold values from -0.15625 to 0.15625
- conv_kernel: float32 [31, 1536], replicated, may hold values from -1 to 1
- cotangent: bfloat16 [16, 2048, 1536], P('dp', 'seq'), may hold values from -6 to 6
Outputs:
- block_out: bfloat16 [16, 2048, 1536], P('dp', 'seq')
- query_grad: bfloat16 [16, 2048, 1536], P('dp', 'seq')
- key_grad: bfloat16 [16, 2048, 1536], P('dp', 'seq')
- value_grad: bfloat16 [16, 2048, 1536], P('dp', 'seq')
- weight_grad: float32 [1536, 1536], P('seq')
- kernel_grad: float32 [31, 1536], replicated
The draws below stay inside these ranges and needn't reach their ends.
Inputs may be any that keep to these rules, and one draw needn't show every extreme that they name: Frames lengths[b] and later of utterance b are padding.
All inputs are finite; a program needn't handle non-finite values.
Results may differ from the reference program's by a relative error of at most 0.028.
Values may be sent and summed in bfloat16 or wider, within the bound.
No kernel may reach another device: no remote copies, remote signals or barrier semaphores. Data moves between devices by JAX's collectives and lax.ppermute only.
A program may use at most 128 MiB of HBM per device.

```python
import math
import jax
import jax.numpy as jnp
from jax import lax

D = 1536
HEADS = 16
KERNEL = 31
HALF = 15
BATCH = 16
FRAMES = 2048


def draw_query_proj(key, part):
    key = jax.random.fold_in(key, 1)
    values = 1.5 * jax.random.truncated_normal(key, -5.0, 5.0, (BATCH, FRAMES, D))
    return values.astype(jnp.float32).astype(jnp.bfloat16)


def draw_key_proj(key, part):
    key = jax.random.fold_in(key, 2)
    values = 1.5 * jax.random.truncated_normal(key, -5.0, 5.0, (BATCH, FRAMES, D))
    return values.astype(jnp.float32).astype(jnp.bfloat16)


def draw_lengths(key, part):
    key = jax.random.fold_in(key, 3)
    values = jax.random.randint(key, (BATCH,), FRAMES // 4, FRAMES + 1, dtype=jnp.int32)
    return values.at[0].set(FRAMES).astype(jnp.int32)


def steps_of(rng, shape, pieces, smallest, high):
    factor_of = 1.0
    for axis_at, blocks in pieces:
        heights = jax.random.uniform(jax.random.fold_in(jax.random.fold_in(rng, 6), axis_at), (blocks,), jnp.float32, smallest / len(pieces), high / len(pieces))
        factor_of = factor_of * jnp.repeat(jnp.exp(heights), shape[axis_at] // blocks).reshape((-1,) + (1,) * (len(shape) - 1 - axis_at))
    return factor_of


def normal_values(rng, extent, scale, reach, pieces=(), kind=jnp.bfloat16):
    level = steps_of(rng, extent, pieces, -0.22, 0.18) if pieces else 1.0
    values = jax.random.normal(rng, extent, jnp.float32) * scale * level
    return jnp.minimum(jnp.maximum(values, -reach), reach).astype(kind)


def setup_inputs(seed: int = 0) -> dict:
    splits = jax.random.split(jax.random.key(seed), 9)
    return {
        "query_proj": draw_query_proj(jax.random.fold_in(splits[8], 71), 0),
        "key_proj": draw_key_proj(jax.random.fold_in(splits[8], 71), 0),
        "value_proj": normal_values(splits[2], (BATCH, FRAMES, D), 1.0, 6.0, ((0, 16), (1, 16))),
        "residual": normal_values(splits[3], (BATCH, FRAMES, D), 0.5, 3.0, ((0, 16), (1, 16))),
        "lengths": draw_lengths(jax.random.fold_in(splits[8], 71), 0),
        "out_weight": normal_values(splits[5], (D, D), D ** -0.5, 0.15625),
        "conv_kernel": normal_values(splits[6], (KERNEL, D), KERNEL ** -0.5, 1.0, (), jnp.float32),
        "cotangent": normal_values(splits[7], (BATCH, FRAMES, D), 1.0, 6.0, ((0, 16), (1, 16))),
    }


def probabilities(query_rows, key_rows, length):
    head_size = D // HEADS
    score_scale = 1.0 / math.sqrt(head_size)
    query_heads = query_rows.astype(jnp.float32).reshape(FRAMES, HEADS, head_size)
    key_heads = key_rows.astype(jnp.float32).reshape(FRAMES, HEADS, head_size)
    scores = jnp.einsum('qhd,khd->hqk', query_heads, key_heads) * score_scale
    valid_keys = jnp.arange(FRAMES, dtype=jnp.int32) < length
    scores = jnp.where(valid_keys[None, None, :], scores, -jnp.inf)
    shifted = jnp.exp(scores - lax.optimization_barrier(jnp.max(scores, axis=-1, keepdims=True)))
    return shifted / lax.optimization_barrier(jnp.sum(shifted, axis=-1, keepdims=True))

def reference(query_proj, key_proj, value_proj, residual, lengths, out_weight, conv_kernel, cotangent):
    head_size = D // HEADS
    score_scale = 1.0 / math.sqrt(head_size)

    def forward_one(inputs):
        query_rows, key_rows, value_rows, length = inputs
        weights = lax.optimization_barrier(probabilities(query_rows, key_rows, length).astype(jnp.bfloat16))
        value_heads = value_rows.astype(jnp.float32).reshape(FRAMES, HEADS, head_size)
        mixed = jnp.einsum('hqk,khd->qhd', weights.astype(jnp.float32), value_heads)
        return mixed.reshape(FRAMES, D).astype(jnp.bfloat16)
    attended = lax.map(forward_one, (query_proj, key_proj, value_proj, lengths))
    flat_attended = attended.reshape(BATCH * FRAMES, D)
    projected = jnp.dot(flat_attended, out_weight, preferred_element_type=jnp.float32).reshape(BATCH, FRAMES, D)
    block_in = residual.astype(jnp.float32) + projected
    positions = jnp.arange(FRAMES, dtype=jnp.int32)
    frame_mask = (positions[None, :] < lengths[:, None]).astype(jnp.float32)[:, :, None]
    masked = lax.optimization_barrier((block_in * frame_mask).astype(jnp.bfloat16))
    padded = jnp.pad(masked.astype(jnp.float32), ((0, 0), (HALF, HALF), (0, 0)))
    conv_out = jnp.zeros((BATCH, FRAMES, D), jnp.float32)
    for offset in range(KERNEL):
        conv_out = conv_out + conv_kernel[offset] * padded[:, offset:offset + FRAMES]
    gate_value = jax.nn.sigmoid(conv_out)
    block_out = (block_in + conv_out * gate_value).astype(jnp.bfloat16)
    silu_slope = gate_value * (1.0 + conv_out * (1.0 - gate_value))
    conv_grad = lax.optimization_barrier((cotangent.astype(jnp.float32) * silu_slope).astype(jnp.bfloat16))
    grad_float = conv_grad.astype(jnp.float32)
    grad_pad = jnp.pad(grad_float, ((0, 0), (HALF, HALF), (0, 0)))
    masked_grad = jnp.zeros((BATCH, FRAMES, D), jnp.float32)
    kernel_rows = []
    for offset in range(KERNEL):
        first_row = 2 * HALF - offset
        masked_grad = masked_grad + conv_kernel[offset] * grad_pad[:, first_row:first_row + FRAMES]
        kernel_rows.append(lax.optimization_barrier(jnp.sum(grad_float * padded[:, offset:offset + FRAMES], axis=(0, 1))))
    kernel_grad = jnp.stack(kernel_rows) / BATCH
    block_grad = (cotangent.astype(jnp.float32) + frame_mask * masked_grad).astype(jnp.bfloat16)
    flat_grad = block_grad.reshape(BATCH * FRAMES, D)
    weight_grad = jnp.dot(flat_attended.T, flat_grad, preferred_element_type=jnp.float32) / BATCH
    mixed_grad = jnp.dot(flat_grad, out_weight.T, preferred_element_type=jnp.float32).astype(jnp.bfloat16)
    mixed_grad = mixed_grad.reshape(BATCH, FRAMES, D)

    def backward_one(inputs):
        query_rows, key_rows, value_rows, grad_rows, length = inputs
        weights = probabilities(query_rows, key_rows, length)
        rounded = lax.optimization_barrier(weights.astype(jnp.bfloat16)).astype(jnp.float32)
        query_heads = query_rows.astype(jnp.float32).reshape(FRAMES, HEADS, head_size)
        key_heads = key_rows.astype(jnp.float32).reshape(FRAMES, HEADS, head_size)
        value_heads = value_rows.astype(jnp.float32).reshape(FRAMES, HEADS, head_size)
        grad_heads = grad_rows.astype(jnp.float32).reshape(FRAMES, HEADS, head_size)
        value_out = jnp.einsum('hqk,qhd->khd', rounded, grad_heads)
        slope = jnp.einsum('qhd,khd->hqk', grad_heads, value_heads)
        centre = lax.optimization_barrier(jnp.sum(weights * slope, axis=-1, keepdims=True))
        score_grad = lax.optimization_barrier((weights * (slope - centre) * score_scale).astype(jnp.bfloat16))
        score_grad = score_grad.astype(jnp.float32)
        query_out = jnp.einsum('hqk,khd->qhd', score_grad, key_heads)
        key_out = jnp.einsum('hqk,qhd->khd', score_grad, query_heads)
        return (query_out.reshape(FRAMES, D).astype(jnp.bfloat16), key_out.reshape(FRAMES, D).astype(jnp.bfloat16), value_out.reshape(FRAMES, D).astype(jnp.bfloat16))
    query_grad, key_grad, value_grad = lax.map(backward_one, (query_proj, key_proj, value_proj, mixed_grad, lengths))
    return (block_out, query_grad, key_grad, value_grad, weight_grad, kernel_grad)
```

```python
import math

import jax
import jax.numpy as jnp
from jax import lax
from jax.experimental import pallas as pl
from jax.experimental.pallas import tpu as pltpu
from jax.sharding import PartitionSpec as P

HEADS = 16
HEAD = 96
LANES = 128
TAPS = 31
HALF = 15
HALO = 32
QT = 512
KT = 256
BF = jnp.bfloat16
F32 = jnp.float32
MIB = 2**20


def params(mib):
    return pltpu.CompilerParams(vmem_limit_bytes=mib * MIB)


def cost(flops, moved):
    return pl.CostEstimate(flops=int(flops), bytes_accessed=int(moved), transcendentals=0)


def lane_iota(shape):
    return lax.broadcasted_iota(jnp.int32, shape, len(shape) - 1)


def row_iota(shape):
    return lax.broadcasted_iota(jnp.int32, shape, 0)


def dot(a, b):
    return jnp.dot(a, b, preferred_element_type=F32)


def pre_kernel(q_ref, k_ref, v_ref, o_ref):
    for part, ref in enumerate((q_ref, k_ref, v_ref)):
        turned = ref[...].T
        for h in range(HEADS):
            o_ref[h, part * HEAD : (part + 1) * HEAD, :] = turned[h * HEAD : (h + 1) * HEAD, :]


def pre(q, k, v):
    return pl.pallas_call(
        pre_kernel,
        out_shape=jax.ShapeDtypeStruct((HEADS, 3 * HEAD, LANES), BF),
        compiler_params=params(32),
        cost_estimate=cost(1e6, 3e6),
        name="pre",
    )(q, k, v)


def fwd_kernel(len_ref, x_ref, e_ref, o_ref, inv_ref, pay_ref, kaug, vaug, sbuf):
    step = pl.program_id(0)
    blocks = x_ref.shape[0]
    scale = math.log2(math.e) / math.sqrt(HEAD)

    @pl.when(step == 0)
    def _():
        length = len_ref[0]
        for j in range(blocks):
            rows = pl.ds(j * LANES, LANES)
            bias = jnp.where(j * LANES + lane_iota((32, LANES)) < length, 0.0, -1e30)
            bias = jnp.where(row_iota((32, LANES)) == 0, bias, 0.0)
            turned = jnp.concatenate([x_ref[j, HEAD : 2 * HEAD, :], bias.astype(BF)], axis=0).T
            kaug[rows, 0:LANES] = turned
            kaug[rows, LANES : 2 * LANES] = turned
            vaug[0:HEAD, rows] = x_ref[j, 2 * HEAD : 3 * HEAD, :]
            vaug[HEAD : HEAD + 16, rows] = jnp.where(row_iota((16, LANES)) == 0, 1.0, 0.0).astype(BF)

    per = QT // LANES
    qt = jnp.concatenate([x_ref[step * per + p, 0:HEAD, :] for p in range(per)], axis=1)
    qs = qt.astype(F32) * scale
    hi = qs.astype(BF)
    lo = (qs - hi.astype(F32)).astype(BF)
    one = jnp.where(row_iota((32, QT)) == 0, 1.0, 0.0).astype(BF)
    qaug = jnp.concatenate([hi, one, lo, jnp.zeros((32, QT), BF)], axis=0)
    tiles = kaug.shape[0] // KT
    top = None
    for t in range(tiles):
        s = dot(kaug[t * KT : (t + 1) * KT, :], qaug)
        sbuf[t * KT : (t + 1) * KT, :] = s
        part = jnp.max(s.reshape(KT // 8, 8, QT), axis=0)
        top = part if top is None else jnp.maximum(top, part)
    top = jnp.max(top, axis=0, keepdims=True)
    acc = jnp.zeros((HEAD + 16, QT), F32)
    for t in range(tiles):
        e = jnp.exp2(sbuf[t * KT : (t + 1) * KT, :] - top).astype(BF)
        e_ref[0, t * KT : (t + 1) * KT, :] = e
        acc = acc + dot(vaug[:, t * KT : (t + 1) * KT], e)
    inv = 1.0 / acc[HEAD : HEAD + 1, :]
    out = acc[0:HEAD, :] * inv
    o_ref[...] = out
    inv_ref[...] = jnp.broadcast_to(inv, (8, QT))
    rounded = out.astype(BF)
    for p in range(per):
        pay_ref[step * per + p, 0:HEAD, :] = rounded[:, p * LANES : (p + 1) * LANES]

    @pl.when(step == pl.num_programs(0) - 1)
    def _():
        left = lane_iota((HEAD, LANES)) < LANES // 2
        for j in range(blocks):
            after = pay_ref[min(j + 1, blocks - 1), 0:HEAD, :]
            before = pay_ref[max(j - 1, 0), 0:HEAD, :]
            pay_ref[j, HEAD : 2 * HEAD, :] = jnp.where(left, after, before)


def fwd(length, x):
    blocks = x.shape[0]
    frames = blocks * LANES
    steps = frames // QT
    return pl.pallas_call(
        fwd_kernel,
        grid=(steps,),
        out_shape=(
            jax.ShapeDtypeStruct((steps, frames, QT), BF),
            jax.ShapeDtypeStruct((HEAD, frames), F32),
            jax.ShapeDtypeStruct((8, frames), F32),
            jax.ShapeDtypeStruct((blocks, 2 * HEAD, LANES), BF),
        ),
        in_specs=[
            pl.BlockSpec(memory_space=pltpu.SMEM),
            pl.BlockSpec((blocks, 3 * HEAD, LANES), lambda i: (0, 0, 0)),
        ],
        out_specs=(
            pl.BlockSpec((1, frames, QT), lambda i: (i, 0, 0)),
            pl.BlockSpec((HEAD, QT), lambda i: (0, i)),
            pl.BlockSpec((8, QT), lambda i: (0, i)),
            pl.BlockSpec((blocks, 2 * HEAD, LANES), lambda i: (0, 0, 0)),
        ),
        scratch_shapes=[
            pltpu.VMEM((frames, 2 * LANES), BF),
            pltpu.VMEM((HEAD + 16, frames), BF),
            pltpu.VMEM((frames, QT), F32),
        ],
        compiler_params=params(40),
        cost_estimate=cost(9e9, 1e7),
        name="attend",
    )(length, x)


def conv_kernel_body(
    info_ref, att_ref, res_ref, cot_ref, left_ref, right_ref, w_ref, taps_ref,
    out_ref, pay_ref, bg_ref, send_ref, keep_ref,
    lhs, block_in, masked, cot, grad, taps_sum,
):
    rows = res_ref.shape[0]
    width = res_ref.shape[1]
    cols = width // LANES
    span = rows + 2 * HALO
    length = info_ref[0]
    first = info_ref[1]
    core = info_ref[2]
    for i in range(HEADS // 2):
        keep_ref[i] = att_ref[2 * i + core, 0:HEAD, :]
        send_ref[i] = att_ref[2 * i + 1 - core, 0:HEAD, :]
    main = jnp.concatenate([att_ref[h, 0:HEAD, :] for h in range(HEADS)], axis=0)
    halo = jnp.concatenate([att_ref[h, HEAD : 2 * HEAD, :] for h in range(HEADS)], axis=0)
    halo = halo.T
    lhs[0:HALO, :] = halo[LANES - HALO : LANES, :]
    lhs[HALO : HALO + rows, :] = main.T
    lhs[HALO + rows : span, :] = halo[0:HALO, :]
    frame = first - HALO + row_iota((span, LANES))
    valid = jnp.logical_and(frame >= 0, frame < length)
    for n in range(cols // 2):
        wide = slice(2 * n * LANES, 2 * (n + 1) * LANES)
        proj = dot(lhs[...], w_ref[:, wide])
        for m in range(2):
            c = 2 * n + m
            at = slice(c * LANES, (c + 1) * LANES)
            res = jnp.concatenate(
                [left_ref[0:HALO, at], res_ref[:, at], right_ref[0:HALO, at]], axis=0
            ).astype(F32)
            block = res + proj[:, m * LANES : (m + 1) * LANES]
            block_in[c] = block
            masked[c] = jnp.where(valid, block, 0.0).astype(BF).astype(F32)
            cot[c] = jnp.concatenate(
                [left_ref[HALO + 16 : 2 * HALO, at], cot_ref[:, at], right_ref[HALO : HALO + 16, at]],
                axis=0,
            ).astype(F32)
    mid = rows + 32

    @pl.loop(0, cols)
    def _(c):
        at = pl.ds(pl.multiple_of(c * LANES, LANES), LANES)
        acc = jnp.zeros((mid, LANES), F32)
        for r in range(TAPS):
            acc = acc + taps_ref[r : r + 1, at] * masked[c, 1 + r : 1 + r + mid, :]
        gate = jax.nn.sigmoid(acc)
        cg = (cot[c] * (gate * (1.0 + acc * (1.0 - gate)))).astype(BF).astype(F32)
        grad[...] = cg
        out_ref[:, at] = (
            block_in[c, HALO : HALO + rows, :] + (acc * gate)[16 : 16 + rows, :]
        ).astype(BF)
        own = cg[16 : 16 + rows, :]
        back = jnp.zeros((rows, LANES), F32)
        for r in range(TAPS):
            back = back + taps_ref[r : r + 1, at] * grad[31 - r : 31 - r + rows, :]
            prod = own * masked[c, 17 + r : 17 + r + rows, :]
            prod = jnp.sum(prod.reshape(rows // 8, 8, LANES), axis=0)
            taps_sum[r // 2, pl.ds((r % 2) * cols + c, 1), :] = jnp.sum(prod, axis=0, keepdims=True)
        own_valid = valid[HALO : HALO + rows, :]
        bg_ref[:, at] = (cot[c, 16 : 16 + rows, :] + jnp.where(own_valid, back, 0.0)).astype(BF)

    taps_sum[HEADS - 1, pl.ds(cols, cols), :] = jnp.zeros((cols, LANES), F32)
    taps_sum[:, pl.ds(2 * cols, 8), :] = jnp.zeros((HEADS, 8, LANES), F32)
    bg = bg_ref[...]
    for h in range(0, HEADS, 2):
        mixed = lax.dot_general(
            w_ref[h * HEAD : (h + 2) * HEAD, :], bg, (((1,), (1,)), ((), ())),
            preferred_element_type=F32,
        ).astype(BF)
        pay_ref[h, 0:HEAD, :] = mixed[0:HEAD]
        pay_ref[h + 1, 0:HEAD, :] = mixed[HEAD : 2 * HEAD]
    pay_ref[:, HEAD:LANES, :] = taps_sum[...].astype(BF)


def conv(info, att, res, cot, left, right, w, taps):
    rows, width = res.shape
    cols = width // LANES
    span = rows + 2 * HALO
    vm = pl.BlockSpec(memory_space=pltpu.VMEM)
    return pl.pallas_call(
        conv_kernel_body,
        out_shape=(
            jax.ShapeDtypeStruct((rows, width), BF),
            jax.ShapeDtypeStruct((HEADS, LANES, LANES), BF),
            jax.ShapeDtypeStruct((rows, width), BF),
            jax.ShapeDtypeStruct((HEADS // 2, HEAD, LANES), BF),
            jax.ShapeDtypeStruct((HEADS // 2, HEAD, LANES), BF),
        ),
        in_specs=[pl.BlockSpec(memory_space=pltpu.SMEM)] + [vm] * 7,
        out_specs=(vm,) * 5,
        scratch_shapes=[
            pltpu.VMEM((span, width), BF),
            pltpu.VMEM((cols, span, LANES), F32),
            pltpu.VMEM((cols, span, LANES), F32),
            pltpu.VMEM((cols, rows + 32, LANES), F32),
            pltpu.VMEM((rows + 32, LANES), F32),
            pltpu.VMEM((HEADS, 32, LANES), F32),
        ],
        compiler_params=params(40),
        cost_estimate=cost(9e9, 1e7),
        name="convolve",
    )(info, att, res, cot, left, right, w, taps)


def outer_kernel(a_ref, b_ref, g_ref, h_ref, o_ref):
    half = HEADS // 2
    lhs = jnp.concatenate(
        [a_ref[...].reshape(half * HEAD, LANES), b_ref[...].reshape(half * HEAD, LANES)], axis=1
    )
    width = g_ref.shape[1]
    for n in range(width // 256):
        at = slice(n * 256, (n + 1) * 256)
        rhs = jnp.concatenate([g_ref[:, at], h_ref[:, at]], axis=0)
        o_ref[:, :, at] = dot(lhs, rhs).astype(BF).reshape(half, HEAD, 256)


def outer(a, b, g, h):
    return pl.pallas_call(
        outer_kernel,
        out_shape=jax.ShapeDtypeStruct((HEADS // 2, HEAD, g.shape[1]), BF),
        compiler_params=params(32),
        cost_estimate=cost(1e9, 4e6),
        name="outer",
    )(a, b, g, h)


def bwd_kernel(x_ref, g_ref, e_ref, o_ref, inv_ref, pay_ref, vaug, kt, dk, dv):
    step = pl.program_id(0)
    blocks = x_ref.shape[0]
    scale = 1.0 / math.sqrt(HEAD)

    @pl.when(step == 0)
    def _():
        ones = jnp.where(row_iota((32, LANES)) < 3, 1.0, 0.0).astype(BF)
        for j in range(blocks):
            rows = pl.ds(j * LANES, LANES)
            turned = jnp.concatenate([x_ref[j, 2 * HEAD : 3 * HEAD, :], ones], axis=0).T
            vaug[rows, 0:LANES] = turned
            vaug[rows, LANES : 2 * LANES] = turned
            kt[:, rows] = x_ref[j, HEAD : 2 * HEAD, :]
        dk[...] = jnp.zeros_like(dk)
        dv[...] = jnp.zeros_like(dv)

    per = QT // LANES
    gt = jnp.concatenate([g_ref[step * per + p, 0:HEAD, :] for p in range(per)], axis=1).astype(F32)
    qt = jnp.concatenate([x_ref[step * per + p, 0:HEAD, :] for p in range(per)], axis=1)
    inv = inv_ref[0:1, :]
    centre = jnp.sum(gt * o_ref[...], axis=0, keepdims=True)
    ginv = gt * inv
    sg = ginv * scale
    hi = sg.astype(BF)
    lo = (sg - hi.astype(F32)).astype(BF)
    rest = centre * inv * (-scale)
    c0 = rest.astype(BF).astype(F32)
    c1 = (rest - c0).astype(BF).astype(F32)
    c2 = rest - c0 - c1
    at = row_iota((32, QT))
    crows = jnp.where(at == 0, c0, jnp.where(at == 1, c1, jnp.where(at == 2, c2, 0.0))).astype(BF)
    zeros = jnp.zeros((32, QT), BF)
    gaug = jnp.concatenate([hi, crows, lo, zeros], axis=0)
    gn = jnp.concatenate([ginv.astype(BF), zeros], axis=0).T
    qn = jnp.concatenate([qt, zeros], axis=0).T
    dq = jnp.zeros((HEAD, QT), F32)
    for t in range(kt.shape[1] // KT):
        rows = slice(t * KT, (t + 1) * KT)
        slope = dot(vaug[rows, :], gaug)
        e = e_ref[0, rows, :]
        ds = (e.astype(F32) * slope).astype(BF)
        dv[rows, :] += dot(e, gn)
        dk[rows, :] += dot(ds, qn)
        dq = dq + dot(kt[:, rows], ds)
    dq = dq.astype(BF)
    for p in range(per):
        pay_ref[step * per + p, 0:HEAD, :] = dq[:, p * LANES : (p + 1) * LANES]

    @pl.when(step == pl.num_programs(0) - 1)
    def _():
        total = jnp.zeros((32, LANES), F32)
        for j in range(blocks):
            total = total + g_ref[j, HEAD:LANES, :].astype(F32)
        total = total.astype(BF)
        for j in range(blocks):
            rows = pl.ds(j * LANES, LANES)
            pay_ref[j, HEAD : 2 * HEAD, :] = dk[rows, :].T[0:HEAD].astype(BF)
            pay_ref[j, 2 * HEAD : 3 * HEAD, :] = dv[rows, :].T[0:HEAD].astype(BF)
            pay_ref[j, 3 * HEAD : 3 * HEAD + 32, :] = total


def bwd(x, g, e, o, inv):
    blocks = x.shape[0]
    frames = blocks * LANES
    steps = frames // QT
    return pl.pallas_call(
        bwd_kernel,
        grid=(steps,),
        out_shape=jax.ShapeDtypeStruct((blocks, 3 * HEAD + 32, LANES), BF),
        in_specs=[
            pl.BlockSpec((blocks, 3 * HEAD, LANES), lambda i: (0, 0, 0)),
            pl.BlockSpec((blocks, LANES, LANES), lambda i: (0, 0, 0)),
            pl.BlockSpec((1, frames, QT), lambda i: (i, 0, 0)),
            pl.BlockSpec((HEAD, QT), lambda i: (0, i)),
            pl.BlockSpec((8, QT), lambda i: (0, i)),
        ],
        out_specs=pl.BlockSpec((blocks, 3 * HEAD + 32, LANES), lambda i: (0, 0, 0)),
        scratch_shapes=[
            pltpu.VMEM((frames, 2 * LANES), BF),
            pltpu.VMEM((HEAD, frames), BF),
            pltpu.VMEM((frames, LANES), F32),
            pltpu.VMEM((frames, LANES), F32),
        ],
        compiler_params=params(40),
        cost_estimate=cost(2e10, 1e7),
        name="attend_back",
    )(x, g, e, o, inv)


def post_kernel(x_ref, q_ref, k_ref, v_ref):
    for part, ref in enumerate((q_ref, k_ref, v_ref)):
        rows = slice(part * HEAD, (part + 1) * HEAD)
        ref[...] = jnp.concatenate([x_ref[h, rows, :] for h in range(HEADS)], axis=0).T


def post(x):
    shape = jax.ShapeDtypeStruct((LANES, HEADS * HEAD), BF)
    return pl.pallas_call(
        post_kernel,
        out_shape=(shape,) * 3,
        compiler_params=params(32),
        cost_estimate=cost(1e6, 3e6),
        name="post",
    )(x)


def pack_kernel(w_ref, x_ref, o_ref):
    width = w_ref.shape[2]
    cols = width // LANES
    share = (HEAD // 8) * cols // HEADS
    for d in range(HEADS):
        parts = []
        for n in range(d * share, (d + 1) * share):
            r, c = 8 * (n // cols), LANES * (n % cols)
            parts.append(
                jnp.sum(w_ref[:, r : r + 8, c : c + LANES].astype(F32), axis=0)
            )
        parts.append(x_ref[d, 3 * HEAD : 3 * HEAD + 24, :].astype(F32))
        o_ref[d] = jnp.concatenate(parts, axis=0).astype(BF)


def pack(w, x):
    return pl.pallas_call(
        pack_kernel,
        out_shape=jax.ShapeDtypeStruct((HEADS, HEAD, LANES), BF),
        compiler_params=params(32),
        cost_estimate=cost(1e6, 3e6),
        name="pack",
    )(w, x)


def total_kernel(x_ref, o_ref):
    total = jnp.sum(x_ref[...].astype(F32), axis=0) * (1.0 / x_ref.shape[0])
    o_ref[...] = jnp.broadcast_to(total.astype(BF)[None], o_ref.shape)


def total(x):
    return pl.pallas_call(
        total_kernel,
        out_shape=jax.ShapeDtypeStruct(x.shape, BF),
        compiler_params=params(32),
        cost_estimate=cost(1e6, 1e6),
        name="total",
    )(x)


def unpack_kernel(x_ref, w_ref, k_ref):
    cols = w_ref.shape[1] // LANES
    share = (HEAD // 8) * cols // HEADS
    for d in range(HEADS):
        x = x_ref[d].astype(F32)
        for i in range(share):
            n = d * share + i
            r, c = 8 * (n // cols), LANES * (n % cols)
            w_ref[r : r + 8, c : c + LANES] = x[8 * i : 8 * i + 8, :]
        for i in range(2):
            if 2 * d + i < TAPS:
                for c in range(cols):
                    k_ref[2 * d + i : 2 * d + i + 1, c * LANES : (c + 1) * LANES] = x[
                        8 * share + cols * i + c : 8 * share + cols * i + c + 1, :
                    ]


def unpack(x, width):
    return pl.pallas_call(
        unpack_kernel,
        out_shape=(
            jax.ShapeDtypeStruct((HEAD, width), F32),
            jax.ShapeDtypeStruct((TAPS, width), F32),
        ),
        compiler_params=params(32),
        cost_estimate=cost(1e6, 1e6),
        name="unpack",
    )(x)


def exchange(x, axis, groups=None):
    return lax.all_to_all(
        x, axis, split_axis=0, concat_axis=0, tiled=True, axis_index_groups=groups
    )


def shards(query_proj, key_proj, value_proj, residual, lengths, out_weight, conv_kernel, cotangent):
    rows, width = query_proj.shape[1:]
    count = lax.axis_size("seq")
    me = lax.axis_index("seq")
    res, cot = residual[0], cotangent[0]
    up = [(i, i + 1) for i in range(count - 1)]
    down = [(i + 1, i) for i in range(count - 1)]
    pairs = [(i, i ^ 1) for i in range(count)]
    same_core = [list(range(c, count, 2)) for c in range(2)]

    heads = exchange(pre(query_proj[0], key_proj[0], value_proj[0]), "seq")
    left = lax.ppermute(jnp.concatenate([res[-HALO:], cot[-HALO:]], axis=0), "seq", up)
    right = lax.ppermute(jnp.concatenate([res[:HALO], cot[:HALO]], axis=0), "seq", down)
    weights, mixed, inv, payload = fwd(lengths, heads)
    attended = exchange(payload, "seq")
    info = jnp.stack([lengths[0], me * rows, me % 2]).astype(jnp.int32)
    block_out, payload, block_grad, send, keep = conv(
        info, attended, res, cot, left, right, out_weight, conv_kernel
    )
    grads = exchange(payload, "seq")
    partner_att = lax.ppermute(send, "seq", pairs)
    partner_grad = lax.ppermute(block_grad, "seq", pairs)
    partial = outer(keep, partner_att, block_grad, partner_grad)
    partial = exchange(partial, "seq", same_core)
    payload = bwd(heads, grads, weights, mixed, inv)
    back = exchange(payload, "seq")
    query_grad, key_grad, value_grad = post(back)
    packed = exchange(pack(partial, back), "dp")
    final = exchange(total(packed), "dp")
    weight_grad, kernel_grad = unpack(final, width)
    return (
        block_out[None],
        query_grad[None],
        key_grad[None],
        value_grad[None],
        weight_grad,
        kernel_grad,
    )


def solution(mesh):
    split = P("dp", "seq", None)
    return jax.shard_map(
        shards,
        mesh=mesh,
        in_specs=(split, split, split, split, P("dp"), P(), P(), split),
        out_specs=(split, split, split, split, P("seq", None), P()),
        check_vma=False,
    )
```

```python
import math

import jax
import jax.numpy as jnp
from jax import lax
from jax.experimental import pallas as pl
from jax.experimental.pallas import tpu as pltpu
from jax.sharding import PartitionSpec as P

HEADS = 16
HEAD = 96
LANES = 128
TAPS = 31
HALF = 15
HALO = 32
QT = 512
KT = 256
BF = jnp.bfloat16
F32 = jnp.float32
MIB = 2**20


def params(mib):
    return pltpu.CompilerParams(vmem_limit_bytes=mib * MIB)


def cost(flops, moved):
    return pl.CostEstimate(flops=int(flops), bytes_accessed=int(moved), transcendentals=0)


def lane_iota(shape):
    return lax.broadcasted_iota(jnp.int32, shape, len(shape) - 1)


def row_iota(shape):
    return lax.broadcasted_iota(jnp.int32, shape, 0)


def dot(a, b):
    return jnp.dot(a, b, preferred_element_type=F32)


def pre_kernel(q_hbm, k_hbm, v_hbm, res_hbm, cot_hbm, o_ref, up_ref, down_ref, buf, sems):
    rows = q_hbm.shape[0]
    loads = [
        pltpu.make_async_copy(ref, buf.at[i], sems.at[i])
        for i, ref in enumerate((q_hbm, k_hbm, v_hbm))
    ]
    edges = [
        pltpu.make_async_copy(ref.at[pl.ds(lo, HALO)], out.at[pl.ds(at, HALO)], sems.at[n])
        for n, ref, lo, out, at in (
            (3, res_hbm, rows - HALO, up_ref, 0),
            (4, cot_hbm, rows - HALO, up_ref, HALO),
            (5, res_hbm, 0, down_ref, 0),
            (6, cot_hbm, 0, down_ref, HALO),
        )
    ]
    for copy in loads + edges:
        copy.start()
    for part, copy in enumerate(loads):
        copy.wait()
        turned = buf[part].T
        for h in range(HEADS):
            o_ref[h, part * HEAD : (part + 1) * HEAD, :] = turned[h * HEAD : (h + 1) * HEAD, :]
    for copy in edges:
        copy.wait()


def pre(q, k, v, res, cot):
    edge = jax.ShapeDtypeStruct((2 * HALO, q.shape[1]), BF)
    return pl.pallas_call(
        pre_kernel,
        out_shape=(jax.ShapeDtypeStruct((HEADS, 3 * HEAD, LANES), BF), edge, edge),
        in_specs=[pl.BlockSpec(memory_space=pltpu.HBM)] * 5,
        scratch_shapes=[pltpu.VMEM((3,) + q.shape, BF), pltpu.SemaphoreType.DMA((7,))],
        compiler_params=params(8),
        cost_estimate=cost(1e6, 3e6),
        name="pre",
    )(q, k, v, res, cot)


def fwd_kernel(len_ref, x_ref, e_ref, o_ref, inv_ref, pay_ref, kaug, vaug, sbuf):
    step = pl.program_id(0)
    blocks = x_ref.shape[0]
    scale = math.log2(math.e) / math.sqrt(HEAD)

    @pl.when(step == 0)
    def _():
        length = len_ref[0]
        for j in range(blocks):
            rows = pl.ds(j * LANES, LANES)
            bias = jnp.where(j * LANES + lane_iota((32, LANES)) < length, 0.0, -1e30)
            bias = jnp.where(row_iota((32, LANES)) == 0, bias, 0.0)
            turned = jnp.concatenate([x_ref[j, HEAD : 2 * HEAD, :], bias.astype(BF)], axis=0).T
            kaug[rows, 0:LANES] = turned
            kaug[rows, LANES : 2 * LANES] = turned
            vaug[0:HEAD, rows] = x_ref[j, 2 * HEAD : 3 * HEAD, :]
            vaug[HEAD : HEAD + 16, rows] = jnp.where(row_iota((16, LANES)) == 0, 1.0, 0.0).astype(BF)

    per = QT // LANES
    qt = jnp.concatenate([x_ref[step * per + p, 0:HEAD, :] for p in range(per)], axis=1)
    qs = qt.astype(F32) * scale
    hi = qs.astype(BF)
    lo = (qs - hi.astype(F32)).astype(BF)
    one = jnp.where(row_iota((32, QT)) == 0, 1.0, 0.0).astype(BF)
    qaug = jnp.concatenate([hi, one, lo, jnp.zeros((32, QT), BF)], axis=0)
    tiles = kaug.shape[0] // KT
    top = None
    for t in range(tiles):
        s = dot(kaug[t * KT : (t + 1) * KT, :], qaug)
        sbuf[t * KT : (t + 1) * KT, :] = s
        part = jnp.max(s.reshape(KT // 8, 8, QT), axis=0)
        top = part if top is None else jnp.maximum(top, part)
    top = jnp.max(top, axis=0, keepdims=True)
    acc = jnp.zeros((HEAD + 16, QT), F32)
    for t in range(tiles):
        e = jnp.exp2(sbuf[t * KT : (t + 1) * KT, :] - top).astype(BF)
        e_ref[0, t * KT : (t + 1) * KT, :] = e
        acc = acc + dot(vaug[:, t * KT : (t + 1) * KT], e)
    inv = 1.0 / acc[HEAD : HEAD + 1, :]
    out = acc[0:HEAD, :] * inv
    o_ref[...] = out
    inv_ref[...] = jnp.broadcast_to(inv, (8, QT))
    rounded = out.astype(BF)
    for p in range(per):
        pay_ref[step * per + p, 0:HEAD, :] = rounded[:, p * LANES : (p + 1) * LANES]

    @pl.when(step == pl.num_programs(0) - 1)
    def _():
        low = HEAD // 2
        lane = lane_iota((low, LANES))
        left = lane < LANES // 2
        outer_lanes = jnp.logical_or(lane < HALO, lane >= LANES - HALO)
        for j in range(blocks):
            after = pay_ref[min(j + 1, blocks - 1), 0:HEAD, :].astype(F32)
            before = pay_ref[max(j - 1, 0), 0:HEAD, :].astype(F32)
            first = jnp.where(left, after[0:low], before[0:low])
            second = jnp.where(left, after[low:HEAD], before[low:HEAD])
            second = pltpu.roll(second, LANES // 2, 1)
            pay_ref[j, HEAD : HEAD + low, :] = jnp.where(outer_lanes, first, second).astype(BF)


def fwd(length, x):
    blocks = x.shape[0]
    frames = blocks * LANES
    steps = frames // QT
    return pl.pallas_call(
        fwd_kernel,
        grid=(steps,),
        out_shape=(
            pltpu.HBM((steps, frames, QT), BF),
            pltpu.HBM((HEAD, frames), F32),
            jax.ShapeDtypeStruct((8, frames), F32),
            jax.ShapeDtypeStruct((blocks, HEAD + HEAD // 2, LANES), BF),
        ),
        in_specs=[
            pl.BlockSpec(memory_space=pltpu.SMEM),
            pl.BlockSpec((blocks, 3 * HEAD, LANES), lambda i: (0, 0, 0)),
        ],
        out_specs=(
            pl.BlockSpec((1, frames, QT), lambda i: (i, 0, 0)),
            pl.BlockSpec((HEAD, QT), lambda i: (0, i)),
            pl.BlockSpec((8, QT), lambda i: (0, i)),
            pl.BlockSpec((blocks, HEAD + HEAD // 2, LANES), lambda i: (0, 0, 0)),
        ),
        scratch_shapes=[
            pltpu.VMEM((frames, 2 * LANES), BF),
            pltpu.VMEM((HEAD + 16, frames), BF),
            pltpu.VMEM((frames, QT), F32),
        ],
        compiler_params=params(20),
        cost_estimate=cost(9e9, 1e7),
        name="attend",
    )(length, x)


def conv_kernel_body(
    info_ref, att_ref, res_hbm, cot_hbm, left_hbm, right_hbm, w_hbm, taps_hbm,
    out_ref, pay_ref, keep_ref, send_ref,
    lhs, block_in, masked, cot, grad, taps_sum, bg_ref,
    res_ref, cot_ref, left_ref, right_ref, weight, taps_ref, sems,
):
    rows, width = res_ref.shape
    cols = width // LANES
    span = rows + 2 * HALO
    length = info_ref[0]
    first = info_ref[1]
    zbit = info_ref[3]
    loads = [
        pltpu.make_async_copy(
            w_hbm.at[:, pl.ds(2 * n * LANES, 2 * LANES)],
            weight.at[:, pl.ds(2 * n * LANES, 2 * LANES)],
            sems.at[n],
        )
        for n in range(cols // 2)
    ]
    small = [
        pltpu.make_async_copy(src, dst, sems.at[cols // 2 + n])
        for n, (src, dst) in enumerate(
            (
                (res_hbm, res_ref),
                (cot_hbm, cot_ref),
                (left_hbm, left_ref),
                (right_hbm, right_ref),
                (taps_hbm, taps_ref),
            )
        )
    ]
    for load in small[0:4] + loads + small[4:]:
        load.start()
    main = jnp.concatenate([att_ref[h, 0:HEAD, :] for h in range(HEADS)], axis=0)
    packed = [att_ref[h, HEAD : HEAD + HEAD // 2, :].astype(F32) for h in range(HEADS)]
    halo = jnp.concatenate(
        [part for p in packed for part in (p, pltpu.roll(p, LANES // 2, 1))], axis=0
    ).astype(BF)
    halo = halo.T
    lhs[0:HALO, :] = halo[LANES - HALO : LANES, :]
    lhs[HALO : HALO + rows, :] = main.T
    lhs[HALO + rows : span, :] = halo[0:HALO, :]
    frame = first - HALO + row_iota((span, LANES))
    valid = jnp.logical_and(frame >= 0, frame < length)
    for load in small[0:4]:
        load.wait()
    for n in range(cols // 2):
        wide = slice(2 * n * LANES, 2 * (n + 1) * LANES)
        loads[n].wait()
        proj = dot(lhs[...], weight[:, wide])
        for m in range(2):
            c = 2 * n + m
            at = slice(c * LANES, (c + 1) * LANES)
            res = jnp.concatenate(
                [left_ref[0:HALO, at], res_ref[:, at], right_ref[0:HALO, at]], axis=0
            ).astype(F32)
            block = res + proj[:, m * LANES : (m + 1) * LANES]
            block_in[c] = block
            masked[c] = jnp.where(valid, block, 0.0).astype(BF).astype(F32)
            cot[c] = jnp.concatenate(
                [left_ref[HALO + 16 : 2 * HALO, at], cot_ref[:, at], right_ref[HALO : HALO + 16, at]],
                axis=0,
            ).astype(F32)
    mid = rows + 32
    small[4].wait()

    @pl.loop(0, cols)
    def _(c):
        at = pl.ds(pl.multiple_of(c * LANES, LANES), LANES)
        acc = jnp.zeros((mid, LANES), F32)
        for r in range(TAPS):
            acc = acc + taps_ref[r : r + 1, at] * masked[c, 1 + r : 1 + r + mid, :]
        gate = jax.nn.sigmoid(acc)
        cg = (cot[c] * (gate * (1.0 + acc * (1.0 - gate)))).astype(BF).astype(F32)
        grad[...] = cg
        out_ref[:, at] = (
            block_in[c, HALO : HALO + rows, :] + (acc * gate)[16 : 16 + rows, :]
        ).astype(BF)
        own = cg[16 : 16 + rows, :]
        back = jnp.zeros((rows, LANES), F32)
        for r in range(TAPS):
            back = back + taps_ref[r : r + 1, at] * grad[31 - r : 31 - r + rows, :]
            prod = own * masked[c, 17 + r : 17 + r + rows, :]
            prod = jnp.sum(prod.reshape(rows // 8, 8, LANES), axis=0)
            taps_sum[r // 2, pl.ds((r % 2) * cols + c, 1), :] = jnp.sum(prod, axis=0, keepdims=True)
        own_valid = valid[HALO : HALO + rows, :]
        bg_ref[:, at] = (cot[c, 16 : 16 + rows, :] + jnp.where(own_valid, back, 0.0)).astype(BF)

    taps_sum[HEADS - 1, pl.ds(cols, cols), :] = jnp.zeros((cols, LANES), F32)
    taps_sum[:, pl.ds(2 * cols, 8), :] = jnp.zeros((HEADS, 8, LANES), F32)
    half = width // 2
    keep_ref[...] = bg_ref[:, pl.ds(pl.multiple_of(zbit * half, LANES), half)]
    send_ref[...] = bg_ref[:, pl.ds(pl.multiple_of((1 - zbit) * half, LANES), half)]
    bg = bg_ref[...]
    for h in range(0, HEADS, 2):
        mixed = lax.dot_general(
            weight[h * HEAD : (h + 2) * HEAD, :], bg, (((1,), (1,)), ((), ())),
            preferred_element_type=F32,
        ).astype(BF)
        pay_ref[h, 0:HEAD, :] = mixed[0:HEAD]
        pay_ref[h + 1, 0:HEAD, :] = mixed[HEAD : 2 * HEAD]
    pay_ref[:, HEAD:LANES, :] = taps_sum[...].astype(BF)


def conv(info, att, res, cot, left, right, w, taps):
    rows, width = res.shape
    cols = width // LANES
    span = rows + 2 * HALO
    vm = pl.BlockSpec()
    return pl.pallas_call(
        conv_kernel_body,
        out_shape=(
            jax.ShapeDtypeStruct((rows, width), BF),
            pltpu.HBM((HEADS, LANES, LANES), BF),
            pltpu.HBM((rows, width // 2), BF),
            pltpu.HBM((rows, width // 2), BF),
        ),
        in_specs=[pl.BlockSpec(memory_space=pltpu.SMEM)]
        + [vm]
        + [pl.BlockSpec(memory_space=pl.ANY)] * 6,
        out_specs=(vm,) * 4,
        scratch_shapes=[
            pltpu.VMEM((span, width), BF),
            pltpu.VMEM((cols, span, LANES), F32),
            pltpu.VMEM((cols, span, LANES), F32),
            pltpu.VMEM((cols, rows + 32, LANES), F32),
            pltpu.VMEM((rows + 32, LANES), F32),
            pltpu.VMEM((HEADS, 32, LANES), F32),
            pltpu.VMEM((rows, width), BF),
            pltpu.VMEM((rows, width), BF),
            pltpu.VMEM((rows, width), BF),
            pltpu.VMEM((2 * HALO, width), BF),
            pltpu.VMEM((2 * HALO, width), BF),
            pltpu.VMEM((width, width), BF),
            pltpu.VMEM((TAPS, width), F32),
            pltpu.SemaphoreType.DMA((cols // 2 + 5,)),
        ],
        compiler_params=params(20),
        cost_estimate=cost(9e9, 1e7),
        name="convolve",
    )(info, att, res, cot, left, right, w, taps)


def outer_kernel(info_ref, g_ref, *refs):
    o_ref = refs[-1]
    taps = jnp.sum(g_ref[:, HEAD:LANES, :].astype(F32), axis=0).astype(BF)
    core = info_ref[2]
    tall, wide = refs[0:4], refs[4:8]
    part = wide[0].shape[1] // 2
    at = pl.ds(pl.multiple_of(core * part, LANES), part)
    rhs = jnp.concatenate([ref[:, at] for ref in wide], axis=0)
    below = part // LANES * HEAD
    for h in range(HEADS):
        o_ref[h, below : below + 32, :] = taps
    for h in range(0, HEADS, 4):
        lhs = jnp.concatenate(
            [
                jnp.concatenate([ref[g, 0:HEAD, :] for ref in tall], axis=1)
                for g in range(h, h + 4)
            ],
            axis=0,
        )
        full = dot(lhs, rhs).astype(BF)
        for g in range(4):
            for c in range(part // LANES):
                o_ref[h + g, c * HEAD : (c + 1) * HEAD, :] = full[
                    g * HEAD : (g + 1) * HEAD, c * LANES : (c + 1) * LANES
                ]


def outer(info, g, tall, wide):
    part = wide[0].shape[1] // 2
    return pl.pallas_call(
        outer_kernel,
        out_shape=jax.ShapeDtypeStruct((HEADS, part // LANES * HEAD + 32, LANES), BF),
        in_specs=[pl.BlockSpec(memory_space=pltpu.SMEM)] + [pl.BlockSpec()] * 9,
        compiler_params=params(20),
        cost_estimate=cost(1e9, 4e6),
        name="outer",
    )(info, g, *tall, *wide)


def bwd_kernel(x_ref, g_ref, e_ref, o_ref, inv_ref, pay_ref, vaug, kt, dk, dv):
    step = pl.program_id(0)
    blocks = x_ref.shape[0]
    scale = 1.0 / math.sqrt(HEAD)

    @pl.when(step == 0)
    def _():
        ones = jnp.where(row_iota((32, LANES)) < 3, 1.0, 0.0).astype(BF)
        for j in range(blocks):
            rows = pl.ds(j * LANES, LANES)
            turned = jnp.concatenate([x_ref[j, 2 * HEAD : 3 * HEAD, :], ones], axis=0).T
            vaug[rows, 0:LANES] = turned
            vaug[rows, LANES : 2 * LANES] = turned
            kt[:, rows] = x_ref[j, HEAD : 2 * HEAD, :]
        dk[...] = jnp.zeros_like(dk)
        dv[...] = jnp.zeros_like(dv)

    per = QT // LANES
    gt = jnp.concatenate([g_ref[step * per + p, 0:HEAD, :] for p in range(per)], axis=1).astype(F32)
    qt = jnp.concatenate([x_ref[step * per + p, 0:HEAD, :] for p in range(per)], axis=1)
    inv = inv_ref[0:1, :]
    centre = jnp.sum(gt * o_ref[...], axis=0, keepdims=True)
    ginv = gt * inv
    sg = ginv * scale
    hi = sg.astype(BF)
    lo = (sg - hi.astype(F32)).astype(BF)
    rest = centre * inv * (-scale)
    c0 = rest.astype(BF).astype(F32)
    c1 = (rest - c0).astype(BF).astype(F32)
    c2 = rest - c0 - c1
    at = row_iota((32, QT))
    crows = jnp.where(at == 0, c0, jnp.where(at == 1, c1, jnp.where(at == 2, c2, 0.0))).astype(BF)
    zeros = jnp.zeros((32, QT), BF)
    gaug = jnp.concatenate([hi, crows, lo, zeros], axis=0)
    gn = jnp.concatenate([ginv.astype(BF), zeros], axis=0).T
    qn = jnp.concatenate([qt, zeros], axis=0).T
    dq = jnp.zeros((HEAD, QT), F32)
    for t in range(kt.shape[1] // KT):
        rows = slice(t * KT, (t + 1) * KT)
        slope = dot(vaug[rows, :], gaug)
        e = e_ref[0, rows, :]
        ds = (e.astype(F32) * slope).astype(BF)
        dv[rows, :] += dot(e, gn)
        dk[rows, :] += dot(ds, qn)
        dq = dq + dot(kt[:, rows], ds)
    dq = dq.astype(BF)
    for p in range(per):
        pay_ref[step * per + p, 0:HEAD, :] = dq[:, p * LANES : (p + 1) * LANES]

    @pl.when(step == pl.num_programs(0) - 1)
    def _():
        for j in range(blocks):
            rows = pl.ds(j * LANES, LANES)
            pay_ref[j, HEAD : 2 * HEAD, :] = dk[rows, :].T[0:HEAD].astype(BF)
            pay_ref[j, 2 * HEAD : 3 * HEAD, :] = dv[rows, :].T[0:HEAD].astype(BF)


def bwd(x, g, e, o, inv):
    blocks = x.shape[0]
    frames = blocks * LANES
    steps = frames // QT
    return pl.pallas_call(
        bwd_kernel,
        grid=(steps,),
        out_shape=jax.ShapeDtypeStruct((blocks, 3 * HEAD, LANES), BF),
        in_specs=[
            pl.BlockSpec((blocks, 3 * HEAD, LANES), lambda i: (0, 0, 0)),
            pl.BlockSpec((blocks, LANES, LANES), lambda i: (0, 0, 0)),
            pl.BlockSpec((1, frames, QT), lambda i: (i, 0, 0)),
            pl.BlockSpec((HEAD, QT), lambda i: (0, i)),
            pl.BlockSpec((8, QT), lambda i: (0, i)),
        ],
        out_specs=pl.BlockSpec((blocks, 3 * HEAD, LANES), lambda i: (0, 0, 0)),
        scratch_shapes=[
            pltpu.VMEM((frames, 2 * LANES), BF),
            pltpu.VMEM((HEAD, frames), BF),
            pltpu.VMEM((frames, LANES), F32),
            pltpu.VMEM((frames, LANES), F32),
        ],
        compiler_params=params(30),
        cost_estimate=cost(2e10, 1e7),
        name="attend_back",
    )(x, g, e, o, inv)


def post_kernel(x_ref, q_ref, k_ref, v_ref):
    for part, ref in enumerate((q_ref, k_ref, v_ref)):
        rows = slice(part * HEAD, (part + 1) * HEAD)
        ref[...] = jnp.concatenate([x_ref[h, rows, :] for h in range(HEADS)], axis=0).T


def post(x):
    shape = jax.ShapeDtypeStruct((LANES, HEADS * HEAD), BF)
    return pl.pallas_call(
        post_kernel,
        out_shape=(shape,) * 3,
        compiler_params=params(12),
        cost_estimate=cost(1e6, 3e6),
        name="post",
    )(x)


GROUP = 8


def pack_kernel(x_ref, o_ref, buf):
    cols = x_ref.shape[1] // HEAD
    below = cols * HEAD
    for r in range(HEAD // 16):
        for c in range(2 * cols):
            at = (c % cols) * HEAD + 16 * r
            tiles = [x_ref[2 * i + c // cols, at : at + 16, :].astype(F32) for i in range(HEADS // 2)]
            both = sum(tiles[1:], tiles[0])
            for e in range(2):
                n = (2 * r + e) * 2 * cols + c
                buf[8 * n : 8 * n + 8, :] = both[8 * e : 8 * e + 8, :]
    share = buf.shape[0] // GROUP
    for j in range(GROUP):
        taps = [x_ref[2 * j + e, below : below + 32, :].astype(F32)[0:24] for e in range(2)]
        rest = jnp.zeros((o_ref.shape[1] - share - 48, LANES), F32)
        o_ref[j] = jnp.concatenate(
            [buf[share * j : share * (j + 1), :]] + taps + [rest], axis=0
        ).astype(BF)


def pack(x):
    units = x.shape[1] // HEAD * HEAD * 2
    return pl.pallas_call(
        pack_kernel,
        out_shape=jax.ShapeDtypeStruct((GROUP, LANES, LANES), BF),
        scratch_shapes=[pltpu.VMEM((units, LANES), F32)],
        compiler_params=params(12),
        cost_estimate=cost(1e6, 3e6),
        name="pack",
    )(x)


def total_kernel(x_ref, o_ref):
    total = jnp.sum(x_ref[...].astype(F32), axis=0) * (1.0 / o_ref.shape[0])
    o_ref[...] = jnp.broadcast_to(total.astype(BF)[None], o_ref.shape)


def total(x, batch):
    return pl.pallas_call(
        total_kernel,
        out_shape=jax.ShapeDtypeStruct((batch,) + x.shape[1:], BF),
        compiler_params=params(12),
        cost_estimate=cost(1e6, 1e6),
        name="total",
    )(x)


def unpack_kernel(x_ref, w_ref, k_ref):
    width = w_ref.shape[1]
    cols = width // LANES
    share = HEAD // 8 * cols // 2 // GROUP
    for z in range(2):
        for j in range(GROUP):
            x = x_ref[4 * (j // 2) + 2 * z + j % 2].astype(F32)
            for i in range(share):
                n = j * share + i
                r, c = 8 * (n // (cols // 2)), width // 2 * z + LANES * (n % (cols // 2))
                w_ref[r : r + 8, c : c + LANES] = x[8 * i : 8 * i + 8, :]
    for j in range(GROUP):
        x = x_ref[4 * (j // 2) + j % 2].astype(F32) + x_ref[4 * (j // 2) + 2 + j % 2].astype(F32)
        for i in range(4):
            if 4 * j + i < TAPS:
                for c in range(cols):
                    at = 8 * share + cols * i + c
                    k_ref[4 * j + i : 4 * j + i + 1, c * LANES : (c + 1) * LANES] = x[at : at + 1, :]


def unpack(x, width):
    return pl.pallas_call(
        unpack_kernel,
        out_shape=(
            jax.ShapeDtypeStruct((HEAD, width), F32),
            jax.ShapeDtypeStruct((TAPS, width), F32),
        ),
        compiler_params=params(12),
        cost_estimate=cost(1e6, 1e6),
        name="unpack",
    )(x)


def in_hbm(x):
    return pltpu.with_memory_space_constraint(x, pltpu.HBM)


def exchange(x, axis, groups=None):
    return lax.all_to_all(
        x, axis, split_axis=0, concat_axis=0, tiled=True, axis_index_groups=groups
    )


def shards(query_proj, key_proj, value_proj, residual, lengths, out_weight, conv_kernel, cotangent):
    rows, width = query_proj.shape[1:]
    count = lax.axis_size("seq")
    me = lax.axis_index("seq")
    res, cot = residual[0], cotangent[0]
    up = [(i, i + 1) for i in range(count - 1)]
    down = [(i + 1, i) for i in range(count - 1)]
    cores = [(i, i ^ 1) for i in range(count)]
    batch = lax.axis_size("dp")
    depth = lax.axis_index("dp")
    levels = [(i, i ^ 2) for i in range(batch)]
    same_level = [[i for i in range(batch) if (i // 2) % 2 == z] for z in range(2)]
    query, key, value, res, cot, out_weight, conv_kernel = (
        in_hbm(x)
        for x in (query_proj[0], key_proj[0], value_proj[0], res, cot, out_weight, conv_kernel)
    )
    payload, edge_up, edge_down = pre(query, key, value, res, cot)
    heads = exchange(payload, "seq")
    left = lax.ppermute(edge_up, "seq", up)
    right = lax.ppermute(edge_down, "seq", down)
    heads, left, right = lax.optimization_barrier((heads, left, right))
    weights, mixed, inv, payload = fwd(lengths, heads)
    attended = exchange(payload, "seq")
    att_level = lax.ppermute(attended, "dp", levels)
    att_core = lax.ppermute(attended, "seq", cores)
    info = jnp.stack([lengths[0], me * rows, me % 2, depth // 2 % 2]).astype(jnp.int32)
    block_out, payload, keep, send = conv(
        info, attended, res, cot, in_hbm(left), in_hbm(right), out_weight, conv_kernel
    )
    att_level, payload = lax.optimization_barrier((att_level, payload))
    att_both = lax.ppermute(att_level, "seq", cores)
    grads = exchange(payload, "seq")
    level = lax.ppermute(send, "dp", levels)
    partner = lax.ppermute(keep, "seq", cores)
    both = lax.ppermute(level, "seq", cores)
    partial = outer(
        info, grads, (attended, att_core, att_level, att_both), (keep, partner, level, both)
    )
    partial = exchange(partial, "seq")
    payload = bwd(heads, grads, in_hbm(weights), in_hbm(mixed), inv)
    payload, partial = lax.optimization_barrier((payload, partial))
    back = exchange(payload, "seq")
    query_grad, key_grad, value_grad = post(back)
    packed = exchange(pack(partial), "dp", same_level)
    final = exchange(total(packed, batch), "dp")
    weight_grad, kernel_grad = unpack(final, width)
    return (
        block_out[None],
        query_grad[None],
        key_grad[None],
        value_grad[None],
        weight_grad,
        kernel_grad,
    )


def solution(mesh):
    split = P("dp", "seq", None)
    return jax.shard_map(
        shards,
        mesh=mesh,
        in_specs=(split, split, split, split, P("dp"), P(), P(), split),
        out_specs=(split, split, split, split, P("seq", None), P()),
        check_vma=False,
    )
```

```python
import math

import jax
import jax.numpy as jnp
from jax import lax
from jax.experimental import pallas as pl
from jax.experimental.pallas import tpu as pltpu
from jax.sharding import PartitionSpec as P

HEADS = 16
HEAD = 96
LANES = 128
TAPS = 31
HALF = 15
HALO = 32
QT = 512
KT = 256
BF = jnp.bfloat16
F32 = jnp.float32
MIB = 2**20


def params(mib):
    return pltpu.CompilerParams(vmem_limit_bytes=mib * MIB)


def cost(flops, moved):
    return pl.CostEstimate(flops=int(flops), bytes_accessed=int(moved), transcendentals=0)


def lane_iota(shape):
    return lax.broadcasted_iota(jnp.int32, shape, len(shape) - 1)


def row_iota(shape):
    return lax.broadcasted_iota(jnp.int32, shape, 0)


def dot(a, b):
    return jnp.dot(a, b, preferred_element_type=F32)


def pre_kernel(q_hbm, k_hbm, v_hbm, res_hbm, cot_hbm, o_ref, up_ref, down_ref, buf, sems):
    rows = q_hbm.shape[0]
    loads = [
        pltpu.make_async_copy(ref, buf.at[i], sems.at[i])
        for i, ref in enumerate((q_hbm, k_hbm, v_hbm))
    ]
    edges = [
        pltpu.make_async_copy(ref.at[pl.ds(lo, HALO)], out.at[pl.ds(at, HALO)], sems.at[n])
        for n, ref, lo, out, at in (
            (3, res_hbm, rows - HALO, up_ref, 0),
            (4, cot_hbm, rows - HALO, up_ref, HALO),
            (5, res_hbm, 0, down_ref, 0),
            (6, cot_hbm, 0, down_ref, HALO),
        )
    ]
    for copy in loads + edges:
        copy.start()
    for part, copy in enumerate(loads):
        copy.wait()
        turned = buf[part].T
        for h in range(HEADS):
            o_ref[h, part * HEAD : (part + 1) * HEAD, :] = turned[h * HEAD : (h + 1) * HEAD, :]
    for copy in edges:
        copy.wait()


def pre(q, k, v, res, cot):
    edge = jax.ShapeDtypeStruct((2 * HALO, q.shape[1]), BF)
    return pl.pallas_call(
        pre_kernel,
        out_shape=(jax.ShapeDtypeStruct((HEADS, 3 * HEAD, LANES), BF), edge, edge),
        in_specs=[pl.BlockSpec(memory_space=pltpu.HBM)] * 5,
        scratch_shapes=[pltpu.VMEM((3,) + q.shape, BF), pltpu.SemaphoreType.DMA((7,))],
        compiler_params=params(8),
        cost_estimate=cost(1e6, 3e6),
        name="pre",
    )(q, k, v, res, cot)


def fwd_kernel(len_ref, x_ref, e_ref, o_ref, inv_ref, pay_ref, kaug, vaug, sbuf):
    step = pl.program_id(0)
    blocks = x_ref.shape[0]
    scale = math.log2(math.e) / math.sqrt(HEAD)

    @pl.when(step == 0)
    def _():
        length = len_ref[0]
        for j in range(blocks):
            rows = pl.ds(j * LANES, LANES)
            bias = jnp.where(j * LANES + lane_iota((32, LANES)) < length, 0.0, -1e30)
            bias = jnp.where(row_iota((32, LANES)) == 0, bias, 0.0)
            turned = jnp.concatenate([x_ref[j, HEAD : 2 * HEAD, :], bias.astype(BF)], axis=0).T
            kaug[rows, 0:LANES] = turned
            kaug[rows, LANES : 2 * LANES] = turned
            vaug[0:HEAD, rows] = x_ref[j, 2 * HEAD : 3 * HEAD, :]
            vaug[HEAD : HEAD + 16, rows] = jnp.where(row_iota((16, LANES)) == 0, 1.0, 0.0).astype(BF)

    per = QT // LANES
    qt = jnp.concatenate([x_ref[step * per + p, 0:HEAD, :] for p in range(per)], axis=1)
    qs = qt.astype(F32) * scale
    hi = qs.astype(BF)
    lo = (qs - hi.astype(F32)).astype(BF)
    one = jnp.where(row_iota((32, QT)) == 0, 1.0, 0.0).astype(BF)
    qaug = jnp.concatenate([hi, one, lo, jnp.zeros((32, QT), BF)], axis=0)
    tiles = kaug.shape[0] // KT
    top = None
    for t in range(tiles):
        s = dot(kaug[t * KT : (t + 1) * KT, :], qaug)
        sbuf[t * KT : (t + 1) * KT, :] = s
        part = jnp.max(s.reshape(KT // 8, 8, QT), axis=0)
        top = part if top is None else jnp.maximum(top, part)
    top = jnp.max(top, axis=0, keepdims=True)
    acc = jnp.zeros((HEAD + 16, QT), F32)
    for t in range(tiles):
        e = jnp.exp2(sbuf[t * KT : (t + 1) * KT, :] - top).astype(BF)
        e_ref[0, t * KT : (t + 1) * KT, :] = e
        acc = acc + dot(vaug[:, t * KT : (t + 1) * KT], e)
    inv = 1.0 / acc[HEAD : HEAD + 1, :]
    out = acc[0:HEAD, :] * inv
    o_ref[...] = out
    inv_ref[...] = jnp.broadcast_to(inv, (8, QT))
    rounded = out.astype(BF)
    for p in range(per):
        pay_ref[step * per + p, 0:HEAD, :] = rounded[:, p * LANES : (p + 1) * LANES]

    @pl.when(step == pl.num_programs(0) - 1)
    def _():
        low = HEAD // 2
        lane = lane_iota((low, LANES))
        left = lane < LANES // 2
        outer_lanes = jnp.logical_or(lane < HALO, lane >= LANES - HALO)
        for j in range(blocks):
            after = pay_ref[min(j + 1, blocks - 1), 0:HEAD, :].astype(F32)
            before = pay_ref[max(j - 1, 0), 0:HEAD, :].astype(F32)
            first = jnp.where(left, after[0:low], before[0:low])
            second = jnp.where(left, after[low:HEAD], before[low:HEAD])
            second = pltpu.roll(second, LANES // 2, 1)
            pay_ref[j, HEAD : HEAD + low, :] = jnp.where(outer_lanes, first, second).astype(BF)


def fwd(length, x):
    blocks = x.shape[0]
    frames = blocks * LANES
    steps = frames // QT
    return pl.pallas_call(
        fwd_kernel,
        grid=(steps,),
        out_shape=(
            pltpu.HBM((steps, frames, QT), BF),
            pltpu.HBM((HEAD, frames), F32),
            jax.ShapeDtypeStruct((8, frames), F32),
            jax.ShapeDtypeStruct((blocks, HEAD + HEAD // 2, LANES), BF),
        ),
        in_specs=[
            pl.BlockSpec(memory_space=pltpu.SMEM),
            pl.BlockSpec((blocks, 3 * HEAD, LANES), lambda i: (0, 0, 0)),
        ],
        out_specs=(
            pl.BlockSpec((1, frames, QT), lambda i: (i, 0, 0)),
            pl.BlockSpec((HEAD, QT), lambda i: (0, i)),
            pl.BlockSpec((8, QT), lambda i: (0, i)),
            pl.BlockSpec((blocks, HEAD + HEAD // 2, LANES), lambda i: (0, 0, 0)),
        ),
        scratch_shapes=[
            pltpu.VMEM((frames, 2 * LANES), BF),
            pltpu.VMEM((HEAD + 16, frames), BF),
            pltpu.VMEM((frames, QT), F32),
        ],
        compiler_params=params(20),
        cost_estimate=cost(9e9, 1e7),
        name="attend",
    )(length, x)


def conv_kernel_body(
    info_ref, att_ref, res_hbm, cot_hbm, left_hbm, right_hbm, w_hbm, taps_hbm,
    out_ref, pay_ref, keep_ref, send_ref,
    lhs, block_in, masked, cot, grad, taps_sum, bg_ref,
    res_ref, cot_ref, left_ref, right_ref, weight, taps_ref, proj, sems,
):
    rows, width = res_ref.shape
    cols = width // LANES
    span = rows + 2 * HALO
    length = info_ref[0]
    first = info_ref[1]
    zbit = info_ref[3]
    pieces = cols // 2
    wide = 2 * LANES

    def chunk(n):
        at = pl.ds(pl.multiple_of(n * wide, wide), wide)
        return pltpu.make_async_copy(w_hbm.at[:, at], weight.at[:, at], sems.at[n])

    small = [
        pltpu.make_async_copy(src, dst, sems.at[pieces + n])
        for n, (src, dst) in enumerate(
            (
                (res_hbm, res_ref),
                (cot_hbm, cot_ref),
                (left_hbm, left_ref),
                (right_hbm, right_ref),
                (taps_hbm, taps_ref),
            )
        )
    ]
    chunk(0).start()
    for load in small:
        load.start()
    for n in range(1, pieces):
        chunk(n).start()
    main = jnp.concatenate([att_ref[h, 0:HEAD, :] for h in range(HEADS)], axis=0)
    packed = [att_ref[h, HEAD : HEAD + HEAD // 2, :].astype(F32) for h in range(HEADS)]
    halo = jnp.concatenate(
        [part for p in packed for part in (p, pltpu.roll(p, LANES // 2, 1))], axis=0
    ).astype(BF)
    halo = halo.T
    lhs[0:HALO, :] = halo[LANES - HALO : LANES, :]
    lhs[HALO : HALO + rows, :] = main.T
    lhs[HALO + rows : span, :] = halo[0:HALO, :]
    frame = first - HALO + row_iota((span, LANES))
    valid = jnp.logical_and(frame >= 0, frame < length)
    mid = rows + 32

    def project(n):
        at = pl.ds(pl.multiple_of(n * wide, wide), wide)
        proj[...] = dot(lhs[...], weight[:, at])

    def place(n):
        for m in range(2):
            c = 2 * n + m
            at = pl.ds(pl.multiple_of(c * LANES, LANES), LANES)
            res = jnp.concatenate(
                [left_ref[0:HALO, at], res_ref[:, at], right_ref[0:HALO, at]], axis=0
            ).astype(F32)
            block = res + proj[:, m * LANES : (m + 1) * LANES]
            block_in[c] = block
            masked[c] = jnp.where(valid, block, 0.0).astype(BF).astype(F32)
            cot[c] = jnp.concatenate(
                [left_ref[HALO : 2 * HALO, at], cot_ref[:, at], right_ref[HALO : 2 * HALO, at]],
                axis=0,
            ).astype(F32)[16 : 16 + mid, :]

    for load in small:
        load.wait()
    chunk(0).wait()
    project(0)
    place(0)

    def channels(c):
        at = pl.ds(pl.multiple_of(c * LANES, LANES), LANES)
        acc = jnp.zeros((mid, LANES), F32)
        for r in range(TAPS):
            acc = acc + taps_ref[r : r + 1, at] * masked[c, 1 + r : 1 + r + mid, :]
        gate = jax.nn.sigmoid(acc)
        cg = (cot[c] * (gate * (1.0 + acc * (1.0 - gate)))).astype(BF).astype(F32)
        grad[...] = cg
        out_ref[:, at] = (
            block_in[c, HALO : HALO + rows, :] + (acc * gate)[16 : 16 + rows, :]
        ).astype(BF)
        own = cg[16 : 16 + rows, :]
        back = jnp.zeros((rows, LANES), F32)
        for r in range(TAPS):
            back = back + taps_ref[r : r + 1, at] * grad[31 - r : 31 - r + rows, :]
            prod = own * masked[c, 17 + r : 17 + r + rows, :]
            prod = jnp.sum(prod.reshape(rows // 8, 8, LANES), axis=0)
            taps_sum[r // 2, pl.ds((r % 2) * cols + c, 1), :] = jnp.sum(prod, axis=0, keepdims=True)
        own_valid = valid[HALO : HALO + rows, :]
        bg_ref[:, at] = (cot[c, 16 : 16 + rows, :] + jnp.where(own_valid, back, 0.0)).astype(BF)

    @pl.loop(0, pieces)
    def _(n):
        @pl.when(n < pieces - 1)
        def _():
            chunk(n + 1).wait()

        after = lax.rem(n + 1, pieces)
        project(after)
        channels(2 * n)
        channels(2 * n + 1)
        place(after)

    taps_sum[HEADS - 1, pl.ds(cols, cols), :] = jnp.zeros((cols, LANES), F32)
    taps_sum[:, pl.ds(2 * cols, 8), :] = jnp.zeros((HEADS, 8, LANES), F32)
    half = width // 2
    keep_ref[...] = bg_ref[:, pl.ds(pl.multiple_of(zbit * half, LANES), half)]
    send_ref[...] = bg_ref[:, pl.ds(pl.multiple_of((1 - zbit) * half, LANES), half)]
    bg = bg_ref[...]
    for h in range(0, HEADS, 2):
        mixed = lax.dot_general(
            weight[h * HEAD : (h + 2) * HEAD, :], bg, (((1,), (1,)), ((), ())),
            preferred_element_type=F32,
        ).astype(BF)
        pay_ref[h, 0:HEAD, :] = mixed[0:HEAD]
        pay_ref[h + 1, 0:HEAD, :] = mixed[HEAD : 2 * HEAD]
    pay_ref[:, HEAD:LANES, :] = taps_sum[...].astype(BF)


def conv(info, att, res, cot, left, right, w, taps):
    rows, width = res.shape
    cols = width // LANES
    span = rows + 2 * HALO
    vm = pl.BlockSpec()
    return pl.pallas_call(
        conv_kernel_body,
        out_shape=(
            jax.ShapeDtypeStruct((rows, width), BF),
            pltpu.HBM((HEADS, LANES, LANES), BF),
            pltpu.HBM((rows, width // 2), BF),
            pltpu.HBM((rows, width // 2), BF),
        ),
        in_specs=[pl.BlockSpec(memory_space=pltpu.SMEM)]
        + [vm]
        + [pl.BlockSpec(memory_space=pl.ANY)] * 6,
        out_specs=(vm,) * 4,
        scratch_shapes=[
            pltpu.VMEM((span, width), BF),
            pltpu.VMEM((cols, span, LANES), F32),
            pltpu.VMEM((cols, span, LANES), F32),
            pltpu.VMEM((cols, rows + 32, LANES), F32),
            pltpu.VMEM((rows + 32, LANES), F32),
            pltpu.VMEM((HEADS, 32, LANES), F32),
            pltpu.VMEM((rows, width), BF),
            pltpu.VMEM((rows, width), BF),
            pltpu.VMEM((rows, width), BF),
            pltpu.VMEM((2 * HALO, width), BF),
            pltpu.VMEM((2 * HALO, width), BF),
            pltpu.VMEM((width, width), BF),
            pltpu.VMEM((TAPS, width), F32),
            pltpu.VMEM((span, 2 * LANES), F32),
            pltpu.SemaphoreType.DMA((cols // 2 + 5,)),
        ],
        compiler_params=params(20),
        cost_estimate=cost(9e9, 1e7),
        name="convolve",
    )(info, att, res, cot, left, right, w, taps)


def outer_kernel(info_ref, *refs):
    o_ref = refs[-1]
    core = info_ref[2]
    tall, wide = refs[0:4], refs[4:8]
    part = wide[0].shape[1] // 2
    at = pl.ds(pl.multiple_of(core * part, LANES), part)
    rhs = jnp.concatenate([ref[:, at] for ref in wide], axis=0)
    for h in range(0, HEADS, 4):
        lhs = jnp.concatenate(
            [
                jnp.concatenate([ref[g, 0:HEAD, :] for ref in tall], axis=1)
                for g in range(h, h + 4)
            ],
            axis=0,
        )
        full = dot(lhs, rhs).astype(BF)
        for g in range(4):
            for c in range(part // LANES):
                o_ref[h + g, c * HEAD : (c + 1) * HEAD, :] = full[
                    g * HEAD : (g + 1) * HEAD, c * LANES : (c + 1) * LANES
                ]


def outer(info, tall, wide):
    part = wide[0].shape[1] // 2
    return pl.pallas_call(
        outer_kernel,
        out_shape=pltpu.HBM((HEADS, part // LANES * HEAD + 32, LANES), BF),
        in_specs=[pl.BlockSpec(memory_space=pltpu.SMEM)] + [pl.BlockSpec()] * 8,
        compiler_params=params(20),
        cost_estimate=cost(1e9, 4e6),
        name="outer",
    )(info, *tall, *wide)


def tail_kernel(g_ref, w_ref, o_ref, taps, sems):
    taps[...] = jnp.sum(g_ref[:, HEAD:LANES, :].astype(F32), axis=0).astype(BF)
    base = o_ref.shape[1] - 32
    copies = [
        pltpu.make_async_copy(taps, o_ref.at[h, pl.ds(base, 32), :], sems.at[h])
        for h in range(HEADS)
    ]
    for copy in copies:
        copy.start()
    for copy in copies:
        copy.wait()


def tail(g, w):
    return pl.pallas_call(
        tail_kernel,
        out_shape=pltpu.HBM(w.shape, BF),
        in_specs=[pl.BlockSpec(), pl.BlockSpec(memory_space=pl.ANY)],
        out_specs=pl.BlockSpec(memory_space=pl.ANY),
        scratch_shapes=[pltpu.VMEM((32, LANES), BF), pltpu.SemaphoreType.DMA((HEADS,))],
        input_output_aliases={1: 0},
        compiler_params=params(8),
        cost_estimate=cost(1e6, 1e6),
        name="tail",
    )(g, w)


def bwd_kernel(x_ref, g_ref, e_ref, o_ref, inv_ref, pay_ref, vaug, kt, dk, dv):
    step = pl.program_id(0)
    blocks = x_ref.shape[0]
    scale = 1.0 / math.sqrt(HEAD)

    @pl.when(step == 0)
    def _():
        ones = jnp.where(row_iota((32, LANES)) < 3, 1.0, 0.0).astype(BF)
        for j in range(blocks):
            rows = pl.ds(j * LANES, LANES)
            turned = jnp.concatenate([x_ref[j, 2 * HEAD : 3 * HEAD, :], ones], axis=0).T
            vaug[rows, 0:LANES] = turned
            vaug[rows, LANES : 2 * LANES] = turned
            kt[:, rows] = x_ref[j, HEAD : 2 * HEAD, :]
        dk[...] = jnp.zeros_like(dk)
        dv[...] = jnp.zeros_like(dv)

    per = QT // LANES
    gt = jnp.concatenate([g_ref[step * per + p, 0:HEAD, :] for p in range(per)], axis=1).astype(F32)
    qt = jnp.concatenate([x_ref[step * per + p, 0:HEAD, :] for p in range(per)], axis=1)
    inv = inv_ref[0:1, :]
    centre = jnp.sum(gt * o_ref[...], axis=0, keepdims=True)
    ginv = gt * inv
    sg = ginv * scale
    hi = sg.astype(BF)
    lo = (sg - hi.astype(F32)).astype(BF)
    rest = centre * inv * (-scale)
    c0 = rest.astype(BF).astype(F32)
    c1 = (rest - c0).astype(BF).astype(F32)
    c2 = rest - c0 - c1
    at = row_iota((32, QT))
    crows = jnp.where(at == 0, c0, jnp.where(at == 1, c1, jnp.where(at == 2, c2, 0.0))).astype(BF)
    zeros = jnp.zeros((32, QT), BF)
    gaug = jnp.concatenate([hi, crows, lo, zeros], axis=0)
    gn = jnp.concatenate([ginv.astype(BF), zeros], axis=0).T
    qn = jnp.concatenate([qt, zeros], axis=0).T
    dq = jnp.zeros((HEAD, QT), F32)
    for t in range(kt.shape[1] // KT):
        rows = slice(t * KT, (t + 1) * KT)
        slope = dot(vaug[rows, :], gaug)
        e = e_ref[0, rows, :]
        ds = (e.astype(F32) * slope).astype(BF)
        dv[rows, :] += dot(e, gn)
        dk[rows, :] += dot(ds, qn)
        dq = dq + dot(kt[:, rows], ds)
    dq = dq.astype(BF)
    for p in range(per):
        pay_ref[step * per + p, 0:HEAD, :] = dq[:, p * LANES : (p + 1) * LANES]

    @pl.when(step == pl.num_programs(0) - 1)
    def _():
        for j in range(blocks):
            rows = pl.ds(j * LANES, LANES)
            pay_ref[j, HEAD : 2 * HEAD, :] = dk[rows, :].T[0:HEAD].astype(BF)
            pay_ref[j, 2 * HEAD : 3 * HEAD, :] = dv[rows, :].T[0:HEAD].astype(BF)


def bwd(x, g, e, o, inv):
    blocks = x.shape[0]
    frames = blocks * LANES
    steps = frames // QT
    return pl.pallas_call(
        bwd_kernel,
        grid=(steps,),
        out_shape=pltpu.HBM((blocks, 3 * HEAD, LANES), BF),
        in_specs=[
            pl.BlockSpec((blocks, 3 * HEAD, LANES), lambda i: (0, 0, 0)),
            pl.BlockSpec((blocks, LANES, LANES), lambda i: (0, 0, 0)),
            pl.BlockSpec((1, frames, QT), lambda i: (i, 0, 0)),
            pl.BlockSpec((HEAD, QT), lambda i: (0, i)),
            pl.BlockSpec((8, QT), lambda i: (0, i)),
        ],
        out_specs=pl.BlockSpec((blocks, 3 * HEAD, LANES), lambda i: (0, 0, 0)),
        scratch_shapes=[
            pltpu.VMEM((frames, 2 * LANES), BF),
            pltpu.VMEM((HEAD, frames), BF),
            pltpu.VMEM((frames, LANES), F32),
            pltpu.VMEM((frames, LANES), F32),
        ],
        compiler_params=params(30),
        cost_estimate=cost(2e10, 1e7),
        name="attend_back",
    )(x, g, e, o, inv)


def post_kernel(x_ref, q_ref, k_ref, v_ref):
    for part, ref in enumerate((q_ref, k_ref, v_ref)):
        rows = slice(part * HEAD, (part + 1) * HEAD)
        ref[...] = jnp.concatenate([x_ref[h, rows, :] for h in range(HEADS)], axis=0).T


def post(x):
    shape = jax.ShapeDtypeStruct((LANES, HEADS * HEAD), BF)
    return pl.pallas_call(
        post_kernel,
        out_shape=(shape,) * 3,
        compiler_params=params(12),
        cost_estimate=cost(1e6, 3e6),
        name="post",
    )(x)


GROUP = 8


def pack_kernel(info_ref, x_ref, *refs):
    outs, buf = refs[:GROUP], refs[GROUP]
    cols = x_ref.shape[1] // HEAD
    below = cols * HEAD
    for r in range(HEAD // 16):
        for c in range(2 * cols):
            at = (c % cols) * HEAD + 16 * r
            tiles = [x_ref[2 * i + c // cols, at : at + 16, :].astype(F32) for i in range(HEADS // 2)]
            both = sum(tiles[1:], tiles[0])
            for e in range(2):
                n = (2 * r + e) * 2 * cols + c
                buf[8 * n : 8 * n + 8, :] = both[8 * e : 8 * e + 8, :]
    share = buf.shape[0] // GROUP
    for k in range(GROUP):
        j = jnp.bitwise_xor(info_ref[4], k)
        taps = [x_ref[2 * j + e, below : below + 32, :].astype(F32)[0:24] for e in range(2)]
        rest = jnp.zeros((outs[k].shape[0] - share - 48, LANES), F32)
        outs[k][...] = jnp.concatenate(
            [buf[pl.ds(pl.multiple_of(share * j, 8), share), :]] + taps + [rest], axis=0
        ).astype(BF)


def pack(info, x):
    units = x.shape[1] // HEAD * HEAD * 2
    return pl.pallas_call(
        pack_kernel,
        out_shape=(pltpu.HBM((LANES, LANES), BF),) * GROUP,
        in_specs=[pl.BlockSpec(memory_space=pltpu.SMEM), pl.BlockSpec()],
        scratch_shapes=[pltpu.VMEM((units, LANES), F32)],
        compiler_params=params(12),
        cost_estimate=cost(1e6, 3e6),
        name="pack",
    )(info, x)


def total_kernel(*refs):
    o_ref = refs[-1]
    total = sum([ref[...].astype(F32) for ref in refs[1:-1]], refs[0][...].astype(F32))
    total = total * (1.0 / o_ref.shape[0])
    o_ref[...] = jnp.broadcast_to(total.astype(BF)[None], o_ref.shape)


def total(xs, batch):
    return pl.pallas_call(
        total_kernel,
        out_shape=pltpu.HBM((batch,) + xs[0].shape, BF),
        compiler_params=params(12),
        cost_estimate=cost(1e6, 1e6),
        name="total",
    )(*xs)


def unpack_kernel(x_ref, w_ref, k_ref):
    width = w_ref.shape[1]
    cols = width // LANES
    share = HEAD // 8 * cols // 2 // GROUP
    for z in range(2):
        for j in range(GROUP):
            x = x_ref[4 * (j // 2) + 2 * z + j % 2].astype(F32)
            for i in range(share):
                n = j * share + i
                r, c = 8 * (n // (cols // 2)), width // 2 * z + LANES * (n % (cols // 2))
                w_ref[r : r + 8, c : c + LANES] = x[8 * i : 8 * i + 8, :]
    for j in range(GROUP):
        x = x_ref[4 * (j // 2) + j % 2].astype(F32) + x_ref[4 * (j // 2) + 2 + j % 2].astype(F32)
        for i in range(4):
            if 4 * j + i < TAPS:
                for c in range(cols):
                    at = 8 * share + cols * i + c
                    k_ref[4 * j + i : 4 * j + i + 1, c * LANES : (c + 1) * LANES] = x[at : at + 1, :]


def unpack(x, width):
    return pl.pallas_call(
        unpack_kernel,
        out_shape=(
            jax.ShapeDtypeStruct((HEAD, width), F32),
            jax.ShapeDtypeStruct((TAPS, width), F32),
        ),
        compiler_params=params(12),
        cost_estimate=cost(1e6, 1e6),
        name="unpack",
    )(x)


def in_hbm(x):
    return pltpu.with_memory_space_constraint(x, pltpu.HBM)


def exchange(x, axis, groups=None):
    return lax.all_to_all(
        x, axis, split_axis=0, concat_axis=0, tiled=True, axis_index_groups=groups
    )


def shards(query_proj, key_proj, value_proj, residual, lengths, out_weight, conv_kernel, cotangent):
    rows, width = query_proj.shape[1:]
    count = lax.axis_size("seq")
    me = lax.axis_index("seq")
    res, cot = residual[0], cotangent[0]
    up = [(i, i + 1) for i in range(count - 1)]
    down = [(i + 1, i) for i in range(count - 1)]
    cores = [(i, i ^ 1) for i in range(count)]
    batch = lax.axis_size("dp")
    depth = lax.axis_index("dp")
    levels = [(i, i ^ 2) for i in range(batch)]

    def hop(k):
        return [(i, i ^ (4 * (k // 2) + k % 2)) for i in range(batch)]

    query, key, value, res, cot, out_weight, conv_kernel = (
        in_hbm(x)
        for x in (query_proj[0], key_proj[0], value_proj[0], res, cot, out_weight, conv_kernel)
    )
    payload, edge_up, edge_down = pre(query, key, value, res, cot)
    heads = exchange(payload, "seq")
    left = lax.ppermute(edge_up, "seq", up)
    right = lax.ppermute(edge_down, "seq", down)
    heads, left, right = lax.optimization_barrier((heads, left, right))
    weights, mixed, inv, payload = fwd(lengths, heads)
    attended = exchange(payload, "seq")
    att_level = lax.ppermute(attended, "dp", levels)
    att_core = lax.ppermute(attended, "seq", cores)
    member = depth // 4 * 2 + depth % 2
    info = jnp.stack([lengths[0], me * rows, me % 2, depth // 2 % 2, member]).astype(jnp.int32)
    block_out, payload, keep, send = conv(
        info, attended, res, cot, in_hbm(left), in_hbm(right), out_weight, conv_kernel
    )
    att_level, payload = lax.optimization_barrier((att_level, payload))
    att_both = lax.ppermute(att_level, "seq", cores)
    grads = exchange(payload, "seq")
    level = lax.ppermute(send, "dp", levels)
    partner = lax.ppermute(keep, "seq", cores)
    both = lax.ppermute(level, "seq", cores)
    partial = outer(
        info, (attended, att_core, att_level, att_both), (keep, partner, level, both)
    )
    partial = exchange(tail(grads, partial), "seq")
    payload = bwd(heads, grads, in_hbm(weights), in_hbm(mixed), inv)
    payload, partial = lax.optimization_barrier((payload, partial))
    back = exchange(payload, "seq")
    packed = pack(info, partial)
    packed = [packed[0]] + [lax.ppermute(packed[k], "dp", hop(k)) for k in range(1, GROUP)]
    summed, back = lax.optimization_barrier((total(packed, batch), back))
    final = exchange(summed, "dp")
    query_grad, key_grad, value_grad = post(back)
    weight_grad, kernel_grad = unpack(final, width)
    return (
        block_out[None],
        query_grad[None],
        key_grad[None],
        value_grad[None],
        weight_grad,
        kernel_grad,
    )


def solution(mesh):
    split = P("dp", "seq", None)
    return jax.shard_map(
        shards,
        mesh=mesh,
        in_specs=(split, split, split, split, P("dp"), P(), P(), split),
        out_specs=(split, split, split, split, P("seq", None), P()),
        check_vma=False,
    )
```

```python
import math

import jax
import jax.numpy as jnp
from jax import lax
from jax.experimental import pallas as pl
from jax.experimental.pallas import tpu as pltpu
from jax.sharding import PartitionSpec as P

HEADS = 16
HEAD = 96
LANES = 128
TAPS = 31
HALF = 15
HALO = 32
QT = 512
KT = 256
BF = jnp.bfloat16
F32 = jnp.float32
MIB = 2**20


def params(mib):
    return pltpu.CompilerParams(vmem_limit_bytes=mib * MIB)


def cost(flops, moved):
    return pl.CostEstimate(flops=int(flops), bytes_accessed=int(moved), transcendentals=0)


def lane_iota(shape):
    return lax.broadcasted_iota(jnp.int32, shape, len(shape) - 1)


def row_iota(shape):
    return lax.broadcasted_iota(jnp.int32, shape, 0)


def dot(a, b):
    return jnp.dot(a, b, preferred_element_type=F32)


def pre_kernel(q_hbm, k_hbm, v_hbm, res_hbm, cot_hbm, o_ref, up_ref, down_ref, buf, sems):
    rows = q_hbm.shape[0]
    loads = [
        pltpu.make_async_copy(ref, buf.at[i], sems.at[i])
        for i, ref in enumerate((q_hbm, k_hbm, v_hbm))
    ]
    edges = [
        pltpu.make_async_copy(ref.at[pl.ds(lo, HALO)], out.at[pl.ds(at, HALO)], sems.at[n])
        for n, ref, lo, out, at in (
            (3, res_hbm, rows - HALO, up_ref, 0),
            (4, cot_hbm, rows - HALO, up_ref, HALO),
            (5, res_hbm, 0, down_ref, 0),
            (6, cot_hbm, 0, down_ref, HALO),
        )
    ]
    for copy in loads + edges:
        copy.start()
    for part, copy in enumerate(loads):
        copy.wait()
        turned = buf[part].T
        for h in range(HEADS):
            o_ref[h, part * HEAD : (part + 1) * HEAD, :] = turned[h * HEAD : (h + 1) * HEAD, :]
    for copy in edges:
        copy.wait()


def pre(q, k, v, res, cot):
    edge = jax.ShapeDtypeStruct((2 * HALO, q.shape[1]), BF)
    return pl.pallas_call(
        pre_kernel,
        out_shape=(jax.ShapeDtypeStruct((HEADS, 3 * HEAD, LANES), BF), edge, edge),
        in_specs=[pl.BlockSpec(memory_space=pltpu.HBM)] * 5,
        scratch_shapes=[pltpu.VMEM((3,) + q.shape, BF), pltpu.SemaphoreType.DMA((7,))],
        compiler_params=params(8),
        cost_estimate=cost(1e6, 3e6),
        name="pre",
    )(q, k, v, res, cot)


def fwd_kernel(len_ref, x_ref, e_hbm, o_ref, inv_ref, pay_ref, kaug, vaug, even, odd, ebuf, sems):
    blocks = x_ref.shape[0]
    frames = blocks * LANES
    scale = math.log2(math.e) / math.sqrt(HEAD)
    length = len_ref[0]
    for j in range(blocks):
        rows = slice(j * LANES, (j + 1) * LANES)
        bias = jnp.where(j * LANES + lane_iota((32, LANES)) < length, 0.0, -1e30)
        bias = jnp.where(row_iota((32, LANES)) == 0, bias, 0.0)
        turned = jnp.concatenate([x_ref[j, HEAD : 2 * HEAD, :], bias.astype(BF)], axis=0).T
        kaug[rows, 0:LANES] = turned
        kaug[rows, LANES : 2 * LANES] = turned
        vaug[0:HEAD, rows] = x_ref[j, 2 * HEAD : 3 * HEAD, :]
        vaug[HEAD : HEAD + 16, rows] = jnp.where(row_iota((16, LANES)) == 0, 1.0, 0.0).astype(BF)
    per = QT // LANES
    count = frames // QT
    tiles = frames // KT
    one = jnp.where(row_iota((32, QT)) == 0, 1.0, 0.0).astype(BF)

    def queries(i):
        qt = jnp.concatenate([x_ref[i * per + p, 0:HEAD, :] for p in range(per)], axis=1)
        qs = qt.astype(F32) * scale
        hi = qs.astype(BF)
        lo = (qs - hi.astype(F32)).astype(BF)
        return jnp.concatenate([hi, one, lo, jnp.zeros((32, QT), BF)], axis=0)

    def score(buf, t, qaug, top):
        s = dot(kaug[t * KT : (t + 1) * KT, :], qaug)
        buf[t * KT : (t + 1) * KT, :] = s
        part = jnp.max(s.reshape(KT // 8, 8, QT), axis=0)
        return part if top is None else jnp.maximum(top, part)

    def out_copy(i, t):
        at = pl.ds(t * KT, 2 * KT)
        return pltpu.make_async_copy(ebuf.at[i, at], e_hbm.at[i, at], sems.at[i, t // 2])

    bufs = (even, odd)
    top = None
    qaug = queries(0)
    for t in range(tiles):
        top = score(bufs[0], t, qaug, top)
    for i in range(count):
        peak = jnp.max(top, axis=0, keepdims=True)
        top = None
        if i + 1 < count:
            qaug = queries(i + 1)
        acc = jnp.zeros((HEAD + 16, QT), F32)
        for t in range(tiles):
            rows = slice(t * KT, (t + 1) * KT)
            if i + 1 < count:
                top = score(bufs[(i + 1) % 2], t, qaug, top)
            e = jnp.exp2(bufs[i % 2][rows, :] - peak).astype(BF)
            ebuf[i, rows, :] = e
            acc = acc + dot(vaug[:, rows], e)
            if t % 2 == 1:
                out_copy(i, t - 1).start()
        inv = 1.0 / acc[HEAD : HEAD + 1, :]
        out = acc[0:HEAD, :] * inv
        at = slice(i * QT, (i + 1) * QT)
        o_ref[:, at] = out
        inv_ref[:, at] = jnp.broadcast_to(inv, (8, QT))
        rounded = out.astype(BF)
        for p in range(per):
            pay_ref[i * per + p, 0:HEAD, :] = rounded[:, p * LANES : (p + 1) * LANES]
    low = HEAD // 2
    lane = lane_iota((low, LANES))
    left = lane < LANES // 2
    outer_lanes = jnp.logical_or(lane < HALO, lane >= LANES - HALO)
    for j in range(blocks):
        after = pay_ref[min(j + 1, blocks - 1), 0:HEAD, :].astype(F32)
        before = pay_ref[max(j - 1, 0), 0:HEAD, :].astype(F32)
        first = jnp.where(left, after[0:low], before[0:low])
        second = jnp.where(left, after[low:HEAD], before[low:HEAD])
        second = pltpu.roll(second, LANES // 2, 1)
        pay_ref[j, HEAD : HEAD + low, :] = jnp.where(outer_lanes, first, second).astype(BF)
    for i in range(count):
        for t in range(0, tiles, 2):
            out_copy(i, t).wait()


def fwd(length, x):
    blocks = x.shape[0]
    frames = blocks * LANES
    steps = frames // QT
    return pl.pallas_call(
        fwd_kernel,
        out_shape=(
            pltpu.HBM((steps, frames, QT), BF),
            pltpu.HBM((HEAD, frames), F32),
            jax.ShapeDtypeStruct((8, frames), F32),
            jax.ShapeDtypeStruct((blocks, HEAD + HEAD // 2, LANES), BF),
        ),
        in_specs=[pl.BlockSpec(memory_space=pltpu.SMEM), pl.BlockSpec()],
        out_specs=(
            pl.BlockSpec(memory_space=pl.ANY),
            pl.BlockSpec(),
            pl.BlockSpec(),
            pl.BlockSpec(),
        ),
        scratch_shapes=[
            pltpu.VMEM((frames, 2 * LANES), BF),
            pltpu.VMEM((HEAD + 16, frames), BF),
            pltpu.VMEM((frames, QT), F32),
            pltpu.VMEM((frames, QT), F32),
            pltpu.VMEM((steps, frames, QT), BF),
            pltpu.SemaphoreType.DMA((steps, frames // KT // 2)),
        ],
        compiler_params=params(30),
        cost_estimate=cost(9e9, 1e7),
        name="attend",
    )(length, x)


def conv_kernel_body(
    info_ref, att_ref, res_hbm, cot_hbm, left_hbm, right_hbm, w_hbm, taps_hbm,
    out_hbm, pay_ref, keep_hbm, send_hbm,
    lhs, block_in, masked, cot, grad, taps_sum, bg_ref,
    res_ref, cot_ref, left_ref, right_ref, weight, taps_ref, proj, out_ref, sems,
):
    rows, width = res_ref.shape
    cols = width // LANES
    span = rows + 2 * HALO
    length = info_ref[0]
    first = info_ref[1]
    zbit = info_ref[3]
    pieces = cols // 2
    wide = 2 * LANES

    def chunk(n):
        at = pl.ds(pl.multiple_of(n * wide, wide), wide)
        return pltpu.make_async_copy(w_hbm.at[:, at], weight.at[:, at], sems.at[n])

    small = [
        pltpu.make_async_copy(src, dst, sems.at[pieces + n])
        for n, (src, dst) in enumerate(
            (
                (res_hbm, res_ref),
                (cot_hbm, cot_ref),
                (left_hbm, left_ref),
                (right_hbm, right_ref),
                (taps_hbm, taps_ref),
            )
        )
    ]
    chunk(0).start()
    for load in small:
        load.start()
    for n in range(1, pieces):
        chunk(n).start()
    main = jnp.concatenate([att_ref[h, 0:HEAD, :] for h in range(HEADS)], axis=0)
    packed = [att_ref[h, HEAD : HEAD + HEAD // 2, :].astype(F32) for h in range(HEADS)]
    halo = jnp.concatenate(
        [part for p in packed for part in (p, pltpu.roll(p, LANES // 2, 1))], axis=0
    ).astype(BF)
    halo = halo.T
    lhs[0:HALO, :] = halo[LANES - HALO : LANES, :]
    lhs[HALO : HALO + rows, :] = main.T
    lhs[HALO + rows : span, :] = halo[0:HALO, :]
    frame = first - HALO + row_iota((span, LANES))
    valid = jnp.logical_and(frame >= 0, frame < length)
    mid = rows + 32

    def project(n):
        at = pl.ds(pl.multiple_of(n * wide, wide), wide)
        proj[...] = dot(lhs[...], weight[:, at])

    def place(n):
        for m in range(2):
            c = 2 * n + m
            at = pl.ds(pl.multiple_of(c * LANES, LANES), LANES)
            res = jnp.concatenate(
                [left_ref[0:HALO, at], res_ref[:, at], right_ref[0:HALO, at]], axis=0
            ).astype(F32)
            block = res + proj[:, m * LANES : (m + 1) * LANES]
            block_in[c] = block
            masked[c] = jnp.where(valid, block, 0.0).astype(BF).astype(F32)
            cot[c] = jnp.concatenate(
                [left_ref[HALO : 2 * HALO, at], cot_ref[:, at], right_ref[HALO : 2 * HALO, at]],
                axis=0,
            ).astype(F32)[16 : 16 + mid, :]

    for load in small:
        load.wait()
    chunk(0).wait()
    project(0)
    place(0)

    def channels(c):
        at = pl.ds(pl.multiple_of(c * LANES, LANES), LANES)
        acc = jnp.zeros((mid, LANES), F32)
        for r in range(TAPS):
            acc = acc + taps_ref[r : r + 1, at] * masked[c, 1 + r : 1 + r + mid, :]
        gate = jax.nn.sigmoid(acc)
        cg = (cot[c] * (gate * (1.0 + acc * (1.0 - gate)))).astype(BF).astype(F32)
        grad[...] = cg
        out_ref[:, at] = (
            block_in[c, HALO : HALO + rows, :] + (acc * gate)[16 : 16 + rows, :]
        ).astype(BF)
        own = cg[16 : 16 + rows, :]
        back = jnp.zeros((rows, LANES), F32)
        for r in range(TAPS):
            back = back + taps_ref[r : r + 1, at] * grad[31 - r : 31 - r + rows, :]
            prod = own * masked[c, 17 + r : 17 + r + rows, :]
            prod = jnp.sum(prod.reshape(rows // 8, 8, LANES), axis=0)
            taps_sum[r // 2, pl.ds((r % 2) * cols + c, 1), :] = jnp.sum(prod, axis=0, keepdims=True)
        own_valid = valid[HALO : HALO + rows, :]
        bg_ref[:, at] = (cot[c, 16 : 16 + rows, :] + jnp.where(own_valid, back, 0.0)).astype(BF)

    @pl.loop(0, pieces)
    def _(n):
        @pl.when(n < pieces - 1)
        def _():
            chunk(n + 1).wait()

        after = lax.rem(n + 1, pieces)
        project(after)
        channels(2 * n)
        channels(2 * n + 1)
        place(after)

    taps_sum[HEADS - 1, pl.ds(cols, cols), :] = jnp.zeros((cols, LANES), F32)
    taps_sum[:, pl.ds(2 * cols, 8), :] = jnp.zeros((HEADS, 8, LANES), F32)
    half = width // 2
    mine = pl.ds(pl.multiple_of(zbit * half, LANES), half)
    other = pl.ds(pl.multiple_of((1 - zbit) * half, LANES), half)
    stores = [
        pltpu.make_async_copy(src, dst, sems.at[pieces + 5 + n])
        for n, (src, dst) in enumerate(
            (
                (bg_ref.at[:, other], send_hbm),
                (bg_ref.at[:, mine], keep_hbm),
                (out_ref, out_hbm),
            )
        )
    ]
    for store in stores:
        store.start()
    bg = bg_ref[...]
    for h in range(0, HEADS, 2):
        mixed = lax.dot_general(
            weight[h * HEAD : (h + 2) * HEAD, :], bg, (((1,), (1,)), ((), ())),
            preferred_element_type=F32,
        ).astype(BF)
        pay_ref[h, 0:HEAD, :] = mixed[0:HEAD]
        pay_ref[h + 1, 0:HEAD, :] = mixed[HEAD : 2 * HEAD]
    pay_ref[:, HEAD:LANES, :] = taps_sum[...].astype(BF)
    for store in stores:
        store.wait()


def conv(info, att, res, cot, left, right, w, taps):
    rows, width = res.shape
    cols = width // LANES
    span = rows + 2 * HALO
    vm = pl.BlockSpec()
    return pl.pallas_call(
        conv_kernel_body,
        out_shape=(
            pltpu.HBM((rows, width), BF),
            pltpu.HBM((HEADS, LANES, LANES), BF),
            pltpu.HBM((rows, width // 2), BF),
            pltpu.HBM((rows, width // 2), BF),
        ),
        in_specs=[pl.BlockSpec(memory_space=pltpu.SMEM)]
        + [vm]
        + [pl.BlockSpec(memory_space=pl.ANY)] * 6,
        out_specs=(
            pl.BlockSpec(memory_space=pl.ANY),
            vm,
            pl.BlockSpec(memory_space=pl.ANY),
            pl.BlockSpec(memory_space=pl.ANY),
        ),
        scratch_shapes=[
            pltpu.VMEM((span, width), BF),
            pltpu.VMEM((cols, span, LANES), F32),
            pltpu.VMEM((cols, span, LANES), F32),
            pltpu.VMEM((cols, rows + 32, LANES), F32),
            pltpu.VMEM((rows + 32, LANES), F32),
            pltpu.VMEM((HEADS, 32, LANES), F32),
            pltpu.VMEM((rows, width), BF),
            pltpu.VMEM((rows, width), BF),
            pltpu.VMEM((rows, width), BF),
            pltpu.VMEM((2 * HALO, width), BF),
            pltpu.VMEM((2 * HALO, width), BF),
            pltpu.VMEM((width, width), BF),
            pltpu.VMEM((TAPS, width), F32),
            pltpu.VMEM((span, 2 * LANES), F32),
            pltpu.VMEM((rows, width), BF),
            pltpu.SemaphoreType.DMA((cols // 2 + 8,)),
        ],
        compiler_params=params(20),
        cost_estimate=cost(9e9, 1e7),
        name="convolve",
    )(info, att, res, cot, left, right, w, taps)


def outer_kernel(info_ref, *refs):
    o_ref = refs[-1]
    core = info_ref[2]
    tall, wide = refs[0:4], refs[4:8]
    part = wide[0].shape[1] // 2
    at = pl.ds(pl.multiple_of(core * part, LANES), part)
    rhs = jnp.concatenate([ref[:, at] for ref in wide], axis=0)
    for h in range(0, HEADS, 4):
        lhs = jnp.concatenate(
            [
                jnp.concatenate([ref[g, 0:HEAD, :] for ref in tall], axis=1)
                for g in range(h, h + 4)
            ],
            axis=0,
        )
        full = dot(lhs, rhs).astype(BF)
        for g in range(4):
            for c in range(part // LANES):
                o_ref[h + g, c * HEAD : (c + 1) * HEAD, :] = full[
                    g * HEAD : (g + 1) * HEAD, c * LANES : (c + 1) * LANES
                ]


def outer(info, tall, wide):
    part = wide[0].shape[1] // 2
    return pl.pallas_call(
        outer_kernel,
        out_shape=pltpu.HBM((HEADS, part // LANES * HEAD + 32, LANES), BF),
        in_specs=[pl.BlockSpec(memory_space=pltpu.SMEM)] + [pl.BlockSpec()] * 8,
        compiler_params=params(20),
        cost_estimate=cost(1e9, 4e6),
        name="outer",
    )(info, *tall, *wide)


def tail_kernel(g_ref, w_ref, o_ref, taps, sems):
    taps[...] = jnp.sum(g_ref[:, HEAD:LANES, :].astype(F32), axis=0).astype(BF)
    base = o_ref.shape[1] - 32
    copies = [
        pltpu.make_async_copy(taps, o_ref.at[h, pl.ds(base, 32), :], sems.at[h])
        for h in range(HEADS)
    ]
    for copy in copies:
        copy.start()
    for copy in copies:
        copy.wait()


def tail(g, w):
    return pl.pallas_call(
        tail_kernel,
        out_shape=pltpu.HBM(w.shape, BF),
        in_specs=[pl.BlockSpec(), pl.BlockSpec(memory_space=pl.ANY)],
        out_specs=pl.BlockSpec(memory_space=pl.ANY),
        scratch_shapes=[pltpu.VMEM((32, LANES), BF), pltpu.SemaphoreType.DMA((HEADS,))],
        input_output_aliases={1: 0},
        compiler_params=params(8),
        cost_estimate=cost(1e6, 1e6),
        name="tail",
    )(g, w)


def bwd_kernel(x_ref, g_ref, e_ref, o_ref, inv_ref, pay_ref, vaug, kt, dk, dv):
    step = pl.program_id(0)
    blocks = x_ref.shape[0]
    scale = 1.0 / math.sqrt(HEAD)

    @pl.when(step == 0)
    def _():
        ones = jnp.where(row_iota((32, LANES)) < 3, 1.0, 0.0).astype(BF)
        for j in range(blocks):
            rows = pl.ds(j * LANES, LANES)
            turned = jnp.concatenate([x_ref[j, 2 * HEAD : 3 * HEAD, :], ones], axis=0).T
            vaug[rows, 0:LANES] = turned
            vaug[rows, LANES : 2 * LANES] = turned
            kt[:, rows] = x_ref[j, HEAD : 2 * HEAD, :]
        dk[...] = jnp.zeros_like(dk)
        dv[...] = jnp.zeros_like(dv)

    per = QT // LANES
    gt = jnp.concatenate([g_ref[step * per + p, 0:HEAD, :] for p in range(per)], axis=1).astype(F32)
    qt = jnp.concatenate([x_ref[step * per + p, 0:HEAD, :] for p in range(per)], axis=1)
    inv = inv_ref[0:1, :]
    centre = jnp.sum(gt * o_ref[...], axis=0, keepdims=True)
    ginv = gt * inv
    sg = ginv * scale
    hi = sg.astype(BF)
    lo = (sg - hi.astype(F32)).astype(BF)
    rest = centre * inv * (-scale)
    c0 = rest.astype(BF).astype(F32)
    c1 = (rest - c0).astype(BF).astype(F32)
    c2 = rest - c0 - c1
    at = row_iota((32, QT))
    crows = jnp.where(at == 0, c0, jnp.where(at == 1, c1, jnp.where(at == 2, c2, 0.0))).astype(BF)
    zeros = jnp.zeros((32, QT), BF)
    gaug = jnp.concatenate([hi, crows, lo, zeros], axis=0)
    gn = jnp.concatenate([ginv.astype(BF), zeros], axis=0).T
    qn = jnp.concatenate([qt, zeros], axis=0).T
    dq = jnp.zeros((HEAD, QT), F32)
    for t in range(kt.shape[1] // KT):
        rows = slice(t * KT, (t + 1) * KT)
        slope = dot(vaug[rows, :], gaug)
        e = e_ref[0, rows, :]
        ds = (e.astype(F32) * slope).astype(BF)
        dv[rows, :] += dot(e, gn)
        dk[rows, :] += dot(ds, qn)
        dq = dq + dot(kt[:, rows], ds)
    dq = dq.astype(BF)
    for p in range(per):
        pay_ref[step * per + p, 0:HEAD, :] = dq[:, p * LANES : (p + 1) * LANES]

    @pl.when(step == pl.num_programs(0) - 1)
    def _():
        for j in range(blocks):
            rows = pl.ds(j * LANES, LANES)
            pay_ref[j, HEAD : 2 * HEAD, :] = dk[rows, :].T[0:HEAD].astype(BF)
            pay_ref[j, 2 * HEAD : 3 * HEAD, :] = dv[rows, :].T[0:HEAD].astype(BF)


def bwd(x, g, e, o, inv):
    blocks = x.shape[0]
    frames = blocks * LANES
    steps = frames // QT
    return pl.pallas_call(
        bwd_kernel,
        grid=(steps,),
        out_shape=pltpu.HBM((blocks, 3 * HEAD, LANES), BF),
        in_specs=[
            pl.BlockSpec((blocks, 3 * HEAD, LANES), lambda i: (0, 0, 0)),
            pl.BlockSpec((blocks, LANES, LANES), lambda i: (0, 0, 0)),
            pl.BlockSpec((1, frames, QT), lambda i: (i, 0, 0)),
            pl.BlockSpec((HEAD, QT), lambda i: (0, i)),
            pl.BlockSpec((8, QT), lambda i: (0, i)),
        ],
        out_specs=pl.BlockSpec((blocks, 3 * HEAD, LANES), lambda i: (0, 0, 0)),
        scratch_shapes=[
            pltpu.VMEM((frames, 2 * LANES), BF),
            pltpu.VMEM((HEAD, frames), BF),
            pltpu.VMEM((frames, LANES), F32),
            pltpu.VMEM((frames, LANES), F32),
        ],
        compiler_params=params(30),
        cost_estimate=cost(2e10, 1e7),
        name="attend_back",
    )(x, g, e, o, inv)


def post_kernel(x_ref, q_ref, k_ref, v_ref):
    for part, ref in enumerate((q_ref, k_ref, v_ref)):
        rows = slice(part * HEAD, (part + 1) * HEAD)
        ref[...] = jnp.concatenate([x_ref[h, rows, :] for h in range(HEADS)], axis=0).T


def post(x):
    shape = jax.ShapeDtypeStruct((LANES, HEADS * HEAD), BF)
    return pl.pallas_call(
        post_kernel,
        out_shape=(shape,) * 3,
        compiler_params=params(12),
        cost_estimate=cost(1e6, 3e6),
        name="post",
    )(x)


GROUP = 8


def pack_kernel(info_ref, x_ref, *refs):
    keep_ref, send_ref, buf = refs
    cols = x_ref.shape[1] // HEAD
    below = cols * HEAD
    for r in range(HEAD // 16):
        for c in range(2 * cols):
            at = (c % cols) * HEAD + 16 * r
            tiles = [x_ref[2 * i + c // cols, at : at + 16, :].astype(F32) for i in range(HEADS // 2)]
            both = sum(tiles[1:], tiles[0])
            for e in range(2):
                n = (2 * r + e) * 2 * cols + c
                buf[8 * n : 8 * n + 8, :] = both[8 * e : 8 * e + 8, :]
    share = buf.shape[0] // GROUP
    for k in range(GROUP):
        j = jnp.bitwise_xor(info_ref[4], k)
        taps = [x_ref[2 * j + e, below : below + 32, :].astype(F32)[0:24] for e in range(2)]
        rest = jnp.zeros((LANES - share - 48, LANES), F32)
        out = send_ref if k % 2 else keep_ref
        out[k // 2] = jnp.concatenate(
            [buf[pl.ds(pl.multiple_of(share * j, 8), share), :]] + taps + [rest], axis=0
        ).astype(BF)


def pack(info, x):
    units = x.shape[1] // HEAD * HEAD * 2
    return pl.pallas_call(
        pack_kernel,
        out_shape=(pltpu.HBM((GROUP // 2, LANES, LANES), BF),) * 2,
        in_specs=[pl.BlockSpec(memory_space=pltpu.SMEM), pl.BlockSpec()],
        scratch_shapes=[pltpu.VMEM((units, LANES), F32)],
        compiler_params=params(12),
        cost_estimate=cost(1e6, 3e6),
        name="pack",
    )(info, x)


def merge_kernel(a_ref, b_ref, *outs):
    for k, out in enumerate(outs):
        out[...] = (a_ref[k].astype(F32) + b_ref[k].astype(F32)).astype(BF)


def merge(a, b):
    return pl.pallas_call(
        merge_kernel,
        out_shape=(pltpu.HBM(a.shape[1:], BF),) * a.shape[0],
        compiler_params=params(8),
        cost_estimate=cost(1e6, 1e6),
        name="merge",
    )(a, b)


def total_kernel(*refs):
    o_ref = refs[-1]
    total = sum([ref[...].astype(F32) for ref in refs[1:-1]], refs[0][...].astype(F32))
    total = total * (1.0 / o_ref.shape[0])
    o_ref[...] = jnp.broadcast_to(total.astype(BF)[None], o_ref.shape)


def total(xs, batch):
    return pl.pallas_call(
        total_kernel,
        out_shape=pltpu.HBM((batch,) + xs[0].shape, BF),
        compiler_params=params(12),
        cost_estimate=cost(1e6, 1e6),
        name="total",
    )(*xs)


def unpack_kernel(x_ref, w_ref, k_ref):
    width = w_ref.shape[1]
    cols = width // LANES
    share = HEAD // 8 * cols // 2 // GROUP
    for z in range(2):
        for j in range(GROUP):
            x = x_ref[4 * (j // 2) + 2 * z + j % 2].astype(F32)
            for i in range(share):
                n = j * share + i
                r, c = 8 * (n // (cols // 2)), width // 2 * z + LANES * (n % (cols // 2))
                w_ref[r : r + 8, c : c + LANES] = x[8 * i : 8 * i + 8, :]
    for j in range(GROUP):
        x = x_ref[4 * (j // 2) + j % 2].astype(F32) + x_ref[4 * (j // 2) + 2 + j % 2].astype(F32)
        for i in range(4):
            if 4 * j + i < TAPS:
                for c in range(cols):
                    at = 8 * share + cols * i + c
                    k_ref[4 * j + i : 4 * j + i + 1, c * LANES : (c + 1) * LANES] = x[at : at + 1, :]


def unpack(x, width):
    return pl.pallas_call(
        unpack_kernel,
        out_shape=(
            jax.ShapeDtypeStruct((HEAD, width), F32),
            jax.ShapeDtypeStruct((TAPS, width), F32),
        ),
        compiler_params=params(12),
        cost_estimate=cost(1e6, 1e6),
        name="unpack",
    )(x)


def in_hbm(x):
    return pltpu.with_memory_space_constraint(x, pltpu.HBM)


def exchange(x, axis, groups=None):
    return lax.all_to_all(
        x, axis, split_axis=0, concat_axis=0, tiled=True, axis_index_groups=groups
    )


def shards(query_proj, key_proj, value_proj, residual, lengths, out_weight, conv_kernel, cotangent):
    rows, width = query_proj.shape[1:]
    count = lax.axis_size("seq")
    me = lax.axis_index("seq")
    res, cot = residual[0], cotangent[0]
    up = [(i, i + 1) for i in range(count - 1)]
    down = [(i + 1, i) for i in range(count - 1)]
    cores = [(i, i ^ 1) for i in range(count)]
    batch = lax.axis_size("dp")
    depth = lax.axis_index("dp")
    levels = [(i, i ^ 2) for i in range(batch)]

    def hop(k):
        return [(i, i ^ (4 * (k // 2) + k % 2)) for i in range(batch)]

    query, key, value, res, cot, out_weight, conv_kernel = (
        in_hbm(x)
        for x in (query_proj[0], key_proj[0], value_proj[0], res, cot, out_weight, conv_kernel)
    )
    payload, edge_up, edge_down = pre(query, key, value, res, cot)
    heads = exchange(payload, "seq")
    left = lax.ppermute(edge_up, "seq", up)
    right = lax.ppermute(edge_down, "seq", down)
    heads, left, right = lax.optimization_barrier((heads, left, right))
    weights, mixed, inv, payload = fwd(lengths, heads)
    attended = exchange(payload, "seq")
    att_level = lax.ppermute(attended, "dp", levels)
    att_core = lax.ppermute(attended, "seq", cores)
    member = depth // 4 * 2 + depth % 2
    info = jnp.stack([lengths[0], me * rows, me % 2, depth // 2 % 2, member]).astype(jnp.int32)
    block_out, payload, keep, send = conv(
        info, attended, res, cot, in_hbm(left), in_hbm(right), out_weight, conv_kernel
    )
    att_level, payload = lax.optimization_barrier((att_level, payload))
    att_both = lax.ppermute(att_level, "seq", cores)
    grads = exchange(payload, "seq")
    level = lax.ppermute(send, "dp", levels)
    partner = lax.ppermute(keep, "seq", cores)
    both = lax.ppermute(level, "seq", cores)
    partial = outer(
        info, (attended, att_core, att_level, att_both), (keep, partner, level, both)
    )
    partial = exchange(tail(grads, partial), "seq")
    payload = bwd(heads, grads, in_hbm(weights), in_hbm(mixed), inv)
    payload, partial = lax.optimization_barrier((payload, partial))
    back = exchange(payload, "seq")
    packed = pack(info, partial)
    packed = merge(in_hbm(packed[0]), lax.ppermute(packed[1], "dp", hop(1)))
    packed = [in_hbm(packed[0])] + [
        lax.ppermute(packed[k], "dp", hop(2 * k)) for k in range(1, GROUP // 2)
    ]
    summed, back = lax.optimization_barrier((total(packed, batch), back))
    final = exchange(summed, "dp")
    query_grad, key_grad, value_grad = post(back)
    weight_grad, kernel_grad = unpack(final, width)
    return (
        block_out[None],
        query_grad[None],
        key_grad[None],
        value_grad[None],
        weight_grad,
        kernel_grad,
    )


def solution(mesh):
    split = P("dp", "seq", None)
    return jax.shard_map(
        shards,
        mesh=mesh,
        in_specs=(split, split, split, split, P("dp"), P(), P(), split),
        out_specs=(split, split, split, split, P("seq", None), P()),
        check_vma=False,
    )
```

```python
import math

import jax
import jax.numpy as jnp
from jax import lax
from jax.experimental import pallas as pl
from jax.experimental.pallas import tpu as pltpu
from jax.sharding import PartitionSpec as P

HEADS = 16
HEAD = 96
LANES = 128
TAPS = 31
HALF = 15
HALO = 32
NEAR = 16
QT = 512
KT = 256
BF = jnp.bfloat16
F32 = jnp.float32
MIB = 2**20


def params(mib):
    return pltpu.CompilerParams(vmem_limit_bytes=mib * MIB)


def cost(flops, moved):
    return pl.CostEstimate(flops=int(flops), bytes_accessed=int(moved), transcendentals=0)


def lane_iota(shape):
    return lax.broadcasted_iota(jnp.int32, shape, len(shape) - 1)


def row_iota(shape):
    return lax.broadcasted_iota(jnp.int32, shape, 0)


def dot(a, b):
    return jnp.dot(a, b, preferred_element_type=F32)


def pre_kernel(q_hbm, k_hbm, v_hbm, res_hbm, cot_hbm, o_ref, up_ref, down_ref, buf, sems):
    rows = q_hbm.shape[0]
    loads = [
        pltpu.make_async_copy(ref, buf.at[i], sems.at[i])
        for i, ref in enumerate((q_hbm, k_hbm, v_hbm))
    ]
    edges = [
        pltpu.make_async_copy(ref.at[pl.ds(lo, size)], out.at[pl.ds(at, size)], sems.at[n])
        for n, ref, lo, size, out, at in (
            (3, res_hbm, rows - HALO, HALO, up_ref, 0),
            (4, cot_hbm, rows - NEAR, NEAR, up_ref, HALO),
            (5, res_hbm, 0, HALO, down_ref, 0),
            (6, cot_hbm, 0, NEAR, down_ref, HALO),
        )
    ]
    for copy in loads + edges:
        copy.start()
    for part, copy in enumerate(loads):
        copy.wait()
        turned = buf[part].T
        for h in range(HEADS):
            o_ref[h, part * HEAD : (part + 1) * HEAD, :] = turned[h * HEAD : (h + 1) * HEAD, :]
    for copy in edges:
        copy.wait()


def pre(q, k, v, res, cot):
    edge = jax.ShapeDtypeStruct((HALO + NEAR, q.shape[1]), BF)
    return pl.pallas_call(
        pre_kernel,
        out_shape=(jax.ShapeDtypeStruct((HEADS, 3 * HEAD, LANES), BF), edge, edge),
        in_specs=[pl.BlockSpec(memory_space=pltpu.HBM)] * 5,
        scratch_shapes=[pltpu.VMEM((3,) + q.shape, BF), pltpu.SemaphoreType.DMA((7,))],
        compiler_params=params(8),
        cost_estimate=cost(1e6, 3e6),
        name="pre",
    )(q, k, v, res, cot)


def fwd_kernel(len_ref, x_ref, e_hbm, o_ref, inv_ref, pay_ref, kaug, vaug, even, odd, ebuf, sems):
    blocks = x_ref.shape[0]
    frames = blocks * LANES
    scale = math.log2(math.e) / math.sqrt(HEAD)
    length = len_ref[0]
    for j in range(blocks):
        rows = slice(j * LANES, (j + 1) * LANES)
        bias = jnp.where(j * LANES + lane_iota((32, LANES)) < length, 0.0, -1e30)
        bias = jnp.where(row_iota((32, LANES)) == 0, bias, 0.0)
        turned = jnp.concatenate([x_ref[j, HEAD : 2 * HEAD, :], bias.astype(BF)], axis=0).T
        kaug[rows, 0:LANES] = turned
        kaug[rows, LANES : 2 * LANES] = turned
        vaug[0:HEAD, rows] = x_ref[j, 2 * HEAD : 3 * HEAD, :]
        vaug[HEAD : HEAD + 16, rows] = jnp.where(row_iota((16, LANES)) == 0, 1.0, 0.0).astype(BF)
    per = QT // LANES
    count = frames // QT
    tiles = frames // KT
    one = jnp.where(row_iota((32, QT)) == 0, 1.0, 0.0).astype(BF)

    def queries(i):
        qt = jnp.concatenate([x_ref[i * per + p, 0:HEAD, :] for p in range(per)], axis=1)
        qs = qt.astype(F32) * scale
        hi = qs.astype(BF)
        lo = (qs - hi.astype(F32)).astype(BF)
        return jnp.concatenate([hi, one, lo, jnp.zeros((32, QT), BF)], axis=0)

    def score(buf, t, qaug, top):
        s = dot(kaug[t * KT : (t + 1) * KT, :], qaug)
        buf[t * KT : (t + 1) * KT, :] = s
        part = jnp.max(s.reshape(KT // 8, 8, QT), axis=0)
        return part if top is None else jnp.maximum(top, part)

    def out_copy(i, t):
        at = pl.ds(t * KT, 2 * KT)
        return pltpu.make_async_copy(ebuf.at[i, at], e_hbm.at[i, at], sems.at[i, t // 2])

    bufs = (even, odd)
    top = None
    qaug = queries(0)
    for t in range(tiles):
        top = score(bufs[0], t, qaug, top)
    for i in range(count):
        peak = jnp.max(top, axis=0, keepdims=True)
        top = None
        if i + 1 < count:
            qaug = queries(i + 1)
        acc = jnp.zeros((HEAD + 16, QT), F32)
        for t in range(tiles):
            rows = slice(t * KT, (t + 1) * KT)
            if i + 1 < count:
                top = score(bufs[(i + 1) % 2], t, qaug, top)
            e = jnp.exp2(bufs[i % 2][rows, :] - peak).astype(BF)
            ebuf[i, rows, :] = e
            acc = acc + dot(vaug[:, rows], e)
            if t % 2 == 1:
                out_copy(i, t - 1).start()
        inv = 1.0 / acc[HEAD : HEAD + 1, :]
        out = acc[0:HEAD, :] * inv
        at = slice(i * QT, (i + 1) * QT)
        o_ref[:, at] = out
        inv_ref[:, at] = jnp.broadcast_to(inv, (8, QT))
        rounded = out.astype(BF)
        for p in range(per):
            pay_ref[i * per + p, 0:HEAD, :] = rounded[:, p * LANES : (p + 1) * LANES]
    low = HEAD // 2
    lane = lane_iota((low, LANES))
    left = lane < LANES // 2
    outer_lanes = jnp.logical_or(lane < HALO, lane >= LANES - HALO)
    for j in range(blocks):
        after = pay_ref[min(j + 1, blocks - 1), 0:HEAD, :].astype(F32)
        before = pay_ref[max(j - 1, 0), 0:HEAD, :].astype(F32)
        first = jnp.where(left, after[0:low], before[0:low])
        second = jnp.where(left, after[low:HEAD], before[low:HEAD])
        second = pltpu.roll(second, LANES // 2, 1)
        pay_ref[j, HEAD : HEAD + low, :] = jnp.where(outer_lanes, first, second).astype(BF)
    for i in range(count):
        for t in range(0, tiles, 2):
            out_copy(i, t).wait()


def fwd(length, x):
    blocks = x.shape[0]
    frames = blocks * LANES
    steps = frames // QT
    return pl.pallas_call(
        fwd_kernel,
        out_shape=(
            pltpu.HBM((steps, frames, QT), BF),
            pltpu.HBM((HEAD, frames), F32),
            jax.ShapeDtypeStruct((8, frames), F32),
            jax.ShapeDtypeStruct((blocks, HEAD + HEAD // 2, LANES), BF),
        ),
        in_specs=[pl.BlockSpec(memory_space=pltpu.SMEM), pl.BlockSpec()],
        out_specs=(
            pl.BlockSpec(memory_space=pl.ANY),
            pl.BlockSpec(),
            pl.BlockSpec(),
            pl.BlockSpec(),
        ),
        scratch_shapes=[
            pltpu.VMEM((frames, 2 * LANES), BF),
            pltpu.VMEM((HEAD + 16, frames), BF),
            pltpu.VMEM((frames, QT), F32),
            pltpu.VMEM((frames, QT), F32),
            pltpu.VMEM((steps, frames, QT), BF),
            pltpu.SemaphoreType.DMA((steps, frames // KT // 2)),
        ],
        compiler_params=params(30),
        cost_estimate=cost(9e9, 1e7),
        name="attend",
    )(length, x)


def conv_kernel_body(
    info_ref, att_ref, res_hbm, cot_hbm, left_hbm, right_hbm, w_hbm, taps_hbm,
    out_hbm, pay_ref, keep_hbm, send_hbm,
    lhs, block_in, masked, cot, grad, taps_sum, bg_ref,
    res_ref, cot_ref, left_ref, right_ref, weight, taps_ref, proj, out_ref, sems,
):
    rows, width = res_ref.shape
    cols = width // LANES
    span = rows + 2 * HALO
    length = info_ref[0]
    first = info_ref[1]
    zbit = info_ref[3]
    pieces = cols // 2
    wide = 2 * LANES

    def chunk(n):
        at = pl.ds(pl.multiple_of(n * wide, wide), wide)
        return pltpu.make_async_copy(w_hbm.at[:, at], weight.at[:, at], sems.at[n])

    small = [
        pltpu.make_async_copy(src, dst, sems.at[pieces + n])
        for n, (src, dst) in enumerate(
            (
                (res_hbm, res_ref),
                (cot_hbm, cot_ref),
                (left_hbm, left_ref),
                (right_hbm, right_ref),
                (taps_hbm, taps_ref),
            )
        )
    ]
    chunk(0).start()
    for load in small:
        load.start()
    for n in range(1, pieces):
        chunk(n).start()
    main = jnp.concatenate([att_ref[h, 0:HEAD, :] for h in range(HEADS)], axis=0)
    packed = [att_ref[h, HEAD : HEAD + HEAD // 2, :].astype(F32) for h in range(HEADS)]
    halo = jnp.concatenate(
        [part for p in packed for part in (p, pltpu.roll(p, LANES // 2, 1))], axis=0
    ).astype(BF)
    halo = halo.T
    lhs[0:HALO, :] = halo[LANES - HALO : LANES, :]
    lhs[HALO : HALO + rows, :] = main.T
    lhs[HALO + rows : span, :] = halo[0:HALO, :]
    frame = first - HALO + row_iota((span, LANES))
    valid = jnp.logical_and(frame >= 0, frame < length)
    mid = rows + 32

    def project(n):
        at = pl.ds(pl.multiple_of(n * wide, wide), wide)
        proj[...] = dot(lhs[...], weight[:, at])

    def place(n):
        for m in range(2):
            c = 2 * n + m
            at = pl.ds(pl.multiple_of(c * LANES, LANES), LANES)
            res = jnp.concatenate(
                [left_ref[0:HALO, at], res_ref[:, at], right_ref[0:HALO, at]], axis=0
            ).astype(F32)
            block = res + proj[:, m * LANES : (m + 1) * LANES]
            block_in[c] = block
            masked[c] = jnp.where(valid, block, 0.0).astype(BF).astype(F32)
            cot[c] = jnp.concatenate(
                [
                    left_ref[HALO : HALO + NEAR, at],
                    cot_ref[:, at],
                    right_ref[HALO : HALO + NEAR, at],
                ],
                axis=0,
            ).astype(F32)

    for load in small:
        load.wait()
    chunk(0).wait()
    project(0)
    place(0)

    def channels(c):
        at = pl.ds(pl.multiple_of(c * LANES, LANES), LANES)
        acc = jnp.zeros((mid, LANES), F32)
        for r in range(TAPS):
            acc = acc + taps_ref[r : r + 1, at] * masked[c, 1 + r : 1 + r + mid, :]
        gate = jax.nn.sigmoid(acc)
        cg = (cot[c] * (gate * (1.0 + acc * (1.0 - gate)))).astype(BF).astype(F32)
        grad[...] = cg
        out_ref[:, at] = (
            block_in[c, HALO : HALO + rows, :] + (acc * gate)[16 : 16 + rows, :]
        ).astype(BF)
        own = cg[16 : 16 + rows, :]
        back = jnp.zeros((rows, LANES), F32)
        for r in range(TAPS):
            back = back + taps_ref[r : r + 1, at] * grad[31 - r : 31 - r + rows, :]
            prod = own * masked[c, 17 + r : 17 + r + rows, :]
            prod = jnp.sum(prod.reshape(rows // 8, 8, LANES), axis=0)
            taps_sum[r // 2, pl.ds((r % 2) * cols + c, 1), :] = jnp.sum(prod, axis=0, keepdims=True)
        own_valid = valid[HALO : HALO + rows, :]
        bg_ref[:, at] = (cot[c, 16 : 16 + rows, :] + jnp.where(own_valid, back, 0.0)).astype(BF)

    @pl.loop(0, pieces)
    def _(n):
        @pl.when(n < pieces - 1)
        def _():
            chunk(n + 1).wait()

        after = lax.rem(n + 1, pieces)
        project(after)
        channels(2 * n)
        channels(2 * n + 1)
        place(after)

    taps_sum[HEADS - 1, pl.ds(cols, cols), :] = jnp.zeros((cols, LANES), F32)
    taps_sum[:, pl.ds(2 * cols, 8), :] = jnp.zeros((HEADS, 8, LANES), F32)
    half = width // 2
    mine = pl.ds(pl.multiple_of(zbit * half, LANES), half)
    other = pl.ds(pl.multiple_of((1 - zbit) * half, LANES), half)
    stores = [
        pltpu.make_async_copy(src, dst, sems.at[pieces + 5 + n])
        for n, (src, dst) in enumerate(
            (
                (bg_ref.at[:, other], send_hbm),
                (bg_ref.at[:, mine], keep_hbm),
                (out_ref, out_hbm),
            )
        )
    ]
    for store in stores:
        store.start()
    bg = bg_ref[...]
    for h in range(0, HEADS, 2):
        mixed = lax.dot_general(
            weight[h * HEAD : (h + 2) * HEAD, :], bg, (((1,), (1,)), ((), ())),
            preferred_element_type=F32,
        ).astype(BF)
        pay_ref[h, 0:HEAD, :] = mixed[0:HEAD]
        pay_ref[h + 1, 0:HEAD, :] = mixed[HEAD : 2 * HEAD]
    pay_ref[:, HEAD:LANES, :] = taps_sum[...].astype(BF)
    for store in stores:
        store.wait()


def conv(info, att, res, cot, left, right, w, taps):
    rows, width = res.shape
    cols = width // LANES
    span = rows + 2 * HALO
    vm = pl.BlockSpec()
    return pl.pallas_call(
        conv_kernel_body,
        out_shape=(
            pltpu.HBM((rows, width), BF),
            pltpu.HBM((HEADS, LANES, LANES), BF),
            pltpu.HBM((rows, width // 2), BF),
            pltpu.HBM((rows, width // 2), BF),
        ),
        in_specs=[pl.BlockSpec(memory_space=pltpu.SMEM)]
        + [vm]
        + [pl.BlockSpec(memory_space=pl.ANY)] * 6,
        out_specs=(
            pl.BlockSpec(memory_space=pl.ANY),
            vm,
            pl.BlockSpec(memory_space=pl.ANY),
            pl.BlockSpec(memory_space=pl.ANY),
        ),
        scratch_shapes=[
            pltpu.VMEM((span, width), BF),
            pltpu.VMEM((cols, span, LANES), F32),
            pltpu.VMEM((cols, span, LANES), F32),
            pltpu.VMEM((cols, rows + 32, LANES), F32),
            pltpu.VMEM((rows + 32, LANES), F32),
            pltpu.VMEM((HEADS, 32, LANES), F32),
            pltpu.VMEM((rows, width), BF),
            pltpu.VMEM((rows, width), BF),
            pltpu.VMEM((rows, width), BF),
            pltpu.VMEM((HALO + NEAR, width), BF),
            pltpu.VMEM((HALO + NEAR, width), BF),
            pltpu.VMEM((width, width), BF),
            pltpu.VMEM((TAPS, width), F32),
            pltpu.VMEM((span, 2 * LANES), F32),
            pltpu.VMEM((rows, width), BF),
            pltpu.SemaphoreType.DMA((cols // 2 + 8,)),
        ],
        compiler_params=params(20),
        cost_estimate=cost(9e9, 1e7),
        name="convolve",
    )(info, att, res, cot, left, right, w, taps)


def outer_kernel(info_ref, *refs):
    o_ref = refs[-1]
    core = info_ref[2]
    tall, wide = refs[0:4], refs[4:8]
    part = wide[0].shape[1] // 2
    at = pl.ds(pl.multiple_of(core * part, LANES), part)
    rhs = jnp.concatenate([ref[:, at] for ref in wide], axis=0)
    for h in range(0, HEADS, 4):
        lhs = jnp.concatenate(
            [
                jnp.concatenate([ref[g, 0:HEAD, :] for ref in tall], axis=1)
                for g in range(h, h + 4)
            ],
            axis=0,
        )
        full = dot(lhs, rhs).astype(BF)
        for g in range(4):
            for c in range(part // LANES):
                o_ref[h + g, c * HEAD : (c + 1) * HEAD, :] = full[
                    g * HEAD : (g + 1) * HEAD, c * LANES : (c + 1) * LANES
                ]


def outer(info, tall, wide):
    part = wide[0].shape[1] // 2
    return pl.pallas_call(
        outer_kernel,
        out_shape=pltpu.HBM((HEADS, part // LANES * HEAD + 32, LANES), BF),
        in_specs=[pl.BlockSpec(memory_space=pltpu.SMEM)] + [pl.BlockSpec()] * 8,
        compiler_params=params(20),
        cost_estimate=cost(1e9, 4e6),
        name="outer",
    )(info, *tall, *wide)


def tail_kernel(g_ref, w_ref, o_ref, taps, sems):
    taps[...] = jnp.sum(g_ref[:, HEAD:LANES, :].astype(F32), axis=0).astype(BF)
    base = o_ref.shape[1] - 32
    copies = [
        pltpu.make_async_copy(taps, o_ref.at[h, pl.ds(base, 32), :], sems.at[h])
        for h in range(HEADS)
    ]
    for copy in copies:
        copy.start()
    for copy in copies:
        copy.wait()


def tail(g, w):
    return pl.pallas_call(
        tail_kernel,
        out_shape=pltpu.HBM(w.shape, BF),
        in_specs=[pl.BlockSpec(), pl.BlockSpec(memory_space=pl.ANY)],
        out_specs=pl.BlockSpec(memory_space=pl.ANY),
        scratch_shapes=[pltpu.VMEM((32, LANES), BF), pltpu.SemaphoreType.DMA((HEADS,))],
        input_output_aliases={1: 0},
        compiler_params=params(8),
        cost_estimate=cost(1e6, 1e6),
        name="tail",
    )(g, w)


def bwd_kernel(x_ref, g_ref, e_ref, o_ref, inv_ref, pay_ref, vaug, kt, dk, dv):
    step = pl.program_id(0)
    blocks = x_ref.shape[0]
    scale = 1.0 / math.sqrt(HEAD)

    @pl.when(step == 0)
    def _():
        ones = jnp.where(row_iota((32, LANES)) < 3, 1.0, 0.0).astype(BF)
        for j in range(blocks):
            rows = pl.ds(j * LANES, LANES)
            turned = jnp.concatenate([x_ref[j, 2 * HEAD : 3 * HEAD, :], ones], axis=0).T
            vaug[rows, 0:LANES] = turned
            vaug[rows, LANES : 2 * LANES] = turned
            kt[:, rows] = x_ref[j, HEAD : 2 * HEAD, :]
        dk[...] = jnp.zeros_like(dk)
        dv[...] = jnp.zeros_like(dv)

    per = QT // LANES
    gt = jnp.concatenate([g_ref[step * per + p, 0:HEAD, :] for p in range(per)], axis=1).astype(F32)
    qt = jnp.concatenate([x_ref[step * per + p, 0:HEAD, :] for p in range(per)], axis=1)
    inv = inv_ref[0:1, :]
    centre = jnp.sum(gt * o_ref[...], axis=0, keepdims=True)
    ginv = gt * inv
    sg = ginv * scale
    hi = sg.astype(BF)
    lo = (sg - hi.astype(F32)).astype(BF)
    rest = centre * inv * (-scale)
    c0 = rest.astype(BF).astype(F32)
    c1 = (rest - c0).astype(BF).astype(F32)
    c2 = rest - c0 - c1
    at = row_iota((32, QT))
    crows = jnp.where(at == 0, c0, jnp.where(at == 1, c1, jnp.where(at == 2, c2, 0.0))).astype(BF)
    zeros = jnp.zeros((32, QT), BF)
    gaug = jnp.concatenate([hi, crows, lo, zeros], axis=0)
    gn = jnp.concatenate([ginv.astype(BF), zeros], axis=0).T
    qn = jnp.concatenate([qt, zeros], axis=0).T
    dq = jnp.zeros((HEAD, QT), F32)
    for t in range(kt.shape[1] // KT):
        rows = slice(t * KT, (t + 1) * KT)
        slope = dot(vaug[rows, :], gaug)
        e = e_ref[0, rows, :]
        ds = (e.astype(F32) * slope).astype(BF)
        dv[rows, :] += dot(e, gn)
        dk[rows, :] += dot(ds, qn)
        dq = dq + dot(kt[:, rows], ds)
    dq = dq.astype(BF)
    for p in range(per):
        pay_ref[step * per + p, 0:HEAD, :] = dq[:, p * LANES : (p + 1) * LANES]

    @pl.when(step == pl.num_programs(0) - 1)
    def _():
        for j in range(blocks):
            rows = pl.ds(j * LANES, LANES)
            pay_ref[j, HEAD : 2 * HEAD, :] = dk[rows, :].T[0:HEAD].astype(BF)
            pay_ref[j, 2 * HEAD : 3 * HEAD, :] = dv[rows, :].T[0:HEAD].astype(BF)


def bwd(x, g, e, o, inv):
    blocks = x.shape[0]
    frames = blocks * LANES
    steps = frames // QT
    return pl.pallas_call(
        bwd_kernel,
        grid=(steps,),
        out_shape=pltpu.HBM((blocks, 3 * HEAD, LANES), BF),
        in_specs=[
            pl.BlockSpec((blocks, 3 * HEAD, LANES), lambda i: (0, 0, 0)),
            pl.BlockSpec((blocks, LANES, LANES), lambda i: (0, 0, 0)),
            pl.BlockSpec((1, frames, QT), lambda i: (i, 0, 0)),
            pl.BlockSpec((HEAD, QT), lambda i: (0, i)),
            pl.BlockSpec((8, QT), lambda i: (0, i)),
        ],
        out_specs=pl.BlockSpec((blocks, 3 * HEAD, LANES), lambda i: (0, 0, 0)),
        scratch_shapes=[
            pltpu.VMEM((frames, 2 * LANES), BF),
            pltpu.VMEM((HEAD, frames), BF),
            pltpu.VMEM((frames, LANES), F32),
            pltpu.VMEM((frames, LANES), F32),
        ],
        compiler_params=params(30),
        cost_estimate=cost(2e10, 1e7),
        name="attend_back",
    )(x, g, e, o, inv)


def post_kernel(x_ref, q_ref, k_ref, v_ref):
    for part, ref in enumerate((q_ref, k_ref, v_ref)):
        rows = slice(part * HEAD, (part + 1) * HEAD)
        ref[...] = jnp.concatenate([x_ref[h, rows, :] for h in range(HEADS)], axis=0).T


def post(x):
    shape = jax.ShapeDtypeStruct((LANES, HEADS * HEAD), BF)
    return pl.pallas_call(
        post_kernel,
        out_shape=(shape,) * 3,
        compiler_params=params(12),
        cost_estimate=cost(1e6, 3e6),
        name="post",
    )(x)


GROUP = 8


def pack_kernel(info_ref, x_ref, *refs):
    outs, buf = refs[:-1], refs[-1]
    cols = x_ref.shape[1] // HEAD
    below = cols * HEAD
    for r in range(HEAD // 16):
        for c in range(2 * cols):
            at = (c % cols) * HEAD + 16 * r
            tiles = [x_ref[2 * i + c // cols, at : at + 16, :].astype(F32) for i in range(HEADS // 2)]
            both = sum(tiles[1:], tiles[0])
            for e in range(2):
                n = (2 * r + e) * 2 * cols + c
                buf[8 * n : 8 * n + 8, :] = both[8 * e : 8 * e + 8, :]
    share = buf.shape[0] // GROUP
    for k in range(GROUP):
        j = jnp.bitwise_xor(info_ref[4], k)
        taps = [x_ref[2 * j + e, below : below + 32, :].astype(F32)[0:24] for e in range(2)]
        rest = jnp.zeros((LANES - share - 48, LANES), F32)
        outs[k // 2][k % 2] = jnp.concatenate(
            [buf[pl.ds(pl.multiple_of(share * j, 8), share), :]] + taps + [rest], axis=0
        ).astype(BF)


def pack(info, x):
    units = x.shape[1] // HEAD * HEAD * 2
    return pl.pallas_call(
        pack_kernel,
        out_shape=(pltpu.HBM((2, LANES, LANES), BF),) * (GROUP // 2),
        in_specs=[pl.BlockSpec(memory_space=pltpu.SMEM), pl.BlockSpec()],
        scratch_shapes=[pltpu.VMEM((units, LANES), F32)],
        compiler_params=params(12),
        cost_estimate=cost(1e6, 3e6),
        name="pack",
    )(info, x)


def merge_kernel(*refs):
    keep_ref, send_ref = refs[-2:]
    both = sum([ref[...].astype(F32) for ref in refs[1:-2]], refs[0][...].astype(F32))
    keep_ref[...] = both[0].astype(BF)
    send_ref[...] = both[1].astype(BF)


def merge(xs):
    return pl.pallas_call(
        merge_kernel,
        out_shape=(pltpu.HBM(xs[0].shape[1:], BF),) * 2,
        compiler_params=params(8),
        cost_estimate=cost(1e6, 1e6),
        name="merge",
    )(*xs)


def total_kernel(*refs):
    o_ref = refs[-1]
    total = sum([ref[...].astype(F32) for ref in refs[1:-1]], refs[0][...].astype(F32))
    total = total * (1.0 / o_ref.shape[0])
    o_ref[...] = jnp.broadcast_to(total.astype(BF)[None], o_ref.shape)


def total(xs, batch):
    return pl.pallas_call(
        total_kernel,
        out_shape=pltpu.HBM((batch,) + xs[0].shape, BF),
        compiler_params=params(12),
        cost_estimate=cost(1e6, 1e6),
        name="total",
    )(*xs)


def unpack_kernel(x_ref, w_ref, k_ref):
    width = w_ref.shape[1]
    cols = width // LANES
    share = HEAD // 8 * cols // 2 // GROUP
    for z in range(2):
        for j in range(GROUP):
            x = x_ref[4 * (j // 2) + 2 * z + j % 2].astype(F32)
            for i in range(share):
                n = j * share + i
                r, c = 8 * (n // (cols // 2)), width // 2 * z + LANES * (n % (cols // 2))
                w_ref[r : r + 8, c : c + LANES] = x[8 * i : 8 * i + 8, :]
    for j in range(GROUP):
        x = x_ref[4 * (j // 2) + j % 2].astype(F32) + x_ref[4 * (j // 2) + 2 + j % 2].astype(F32)
        for i in range(4):
            if 4 * j + i < TAPS:
                for c in range(cols):
                    at = 8 * share + cols * i + c
                    k_ref[4 * j + i : 4 * j + i + 1, c * LANES : (c + 1) * LANES] = x[at : at + 1, :]


def unpack(x, width):
    return pl.pallas_call(
        unpack_kernel,
        out_shape=(
            jax.ShapeDtypeStruct((HEAD, width), F32),
            jax.ShapeDtypeStruct((TAPS, width), F32),
        ),
        compiler_params=params(12),
        cost_estimate=cost(1e6, 1e6),
        name="unpack",
    )(x)


def in_hbm(x):
    return pltpu.with_memory_space_constraint(x, pltpu.HBM)


def exchange(x, axis, groups=None):
    return lax.all_to_all(
        x, axis, split_axis=0, concat_axis=0, tiled=True, axis_index_groups=groups
    )


def shards(query_proj, key_proj, value_proj, residual, lengths, out_weight, conv_kernel, cotangent):
    rows, width = query_proj.shape[1:]
    count = lax.axis_size("seq")
    me = lax.axis_index("seq")
    res, cot = residual[0], cotangent[0]
    up = [(i, i + 1) for i in range(count - 1)]
    down = [(i + 1, i) for i in range(count - 1)]
    cores = [(i, i ^ 1) for i in range(count)]
    batch = lax.axis_size("dp")
    depth = lax.axis_index("dp")
    levels = [(i, i ^ 2) for i in range(batch)]

    def hop(k):
        return [(i, i ^ (4 * (k // 2) + k % 2)) for i in range(batch)]

    query, key, value, res, cot, out_weight, conv_kernel = (
        in_hbm(x)
        for x in (query_proj[0], key_proj[0], value_proj[0], res, cot, out_weight, conv_kernel)
    )
    payload, edge_up, edge_down = pre(query, key, value, res, cot)
    heads = exchange(payload, "seq")
    left = lax.ppermute(edge_up, "seq", up)
    right = lax.ppermute(edge_down, "seq", down)
    heads, left, right = lax.optimization_barrier((heads, left, right))
    weights, mixed, inv, payload = fwd(lengths, heads)
    attended = exchange(payload, "seq")
    att_level = lax.ppermute(attended, "dp", levels)
    att_core = lax.ppermute(attended, "seq", cores)
    member = depth // 4 * 2 + depth % 2
    info = jnp.stack([lengths[0], me * rows, me % 2, depth // 2 % 2, member]).astype(jnp.int32)
    block_out, payload, keep, send = conv(
        info, attended, res, cot, in_hbm(left), in_hbm(right), out_weight, conv_kernel
    )
    att_level, payload = lax.optimization_barrier((att_level, payload))
    att_both = lax.ppermute(att_level, "seq", cores)
    grads = exchange(payload, "seq")
    level = lax.ppermute(send, "dp", levels)
    partner = lax.ppermute(keep, "seq", cores)
    both = lax.ppermute(level, "seq", cores)
    partial = outer(
        info, (attended, att_core, att_level, att_both), (in_hbm(keep), partner, level, both)
    )
    partial = exchange(tail(grads, partial), "seq")
    payload = bwd(heads, grads, in_hbm(weights), in_hbm(mixed), inv)
    payload, partial = lax.optimization_barrier((payload, partial))
    back = exchange(payload, "seq")
    packed = pack(info, partial)
    level_parts = [in_hbm(packed[0])] + [
        lax.ppermute(packed[k], "dp", hop(2 * k)) for k in range(1, GROUP // 2)
    ]
    keep, send = merge(level_parts)
    packed = [in_hbm(keep), lax.ppermute(send, "dp", hop(1))]
    summed, back = lax.optimization_barrier((total(packed, batch), back))
    final = exchange(summed, "dp")
    query_grad, key_grad, value_grad = post(back)
    weight_grad, kernel_grad = unpack(final, width)
    return (
        block_out[None],
        query_grad[None],
        key_grad[None],
        value_grad[None],
        weight_grad,
        kernel_grad,
    )


def solution(mesh):
    split = P("dp", "seq", None)
    return jax.shard_map(
        shards,
        mesh=mesh,
        in_specs=(split, split, split, split, P("dp"), P(), P(), split),
        out_specs=(split, split, split, split, P("seq", None), P()),
        check_vma=False,
    )
```

```python
import math

import jax
import jax.numpy as jnp
from jax import lax
from jax.experimental import pallas as pl
from jax.experimental.pallas import tpu as pltpu
from jax.sharding import PartitionSpec as P

HEADS = 16
HEAD = 96
LANES = 128
TAPS = 31
HALF = 15
HALO = 32
NEAR = 16
QT = 512
KT = 256
BF = jnp.bfloat16
F32 = jnp.float32
MIB = 2**20


def params(mib):
    return pltpu.CompilerParams(vmem_limit_bytes=mib * MIB)


def cost(flops, moved):
    return pl.CostEstimate(flops=int(flops), bytes_accessed=int(moved), transcendentals=0)


def lane_iota(shape):
    return lax.broadcasted_iota(jnp.int32, shape, len(shape) - 1)


def row_iota(shape):
    return lax.broadcasted_iota(jnp.int32, shape, 0)


def dot(a, b):
    return jnp.dot(a, b, preferred_element_type=F32)


def pre_kernel(q_hbm, k_hbm, v_hbm, res_hbm, cot_hbm, o_ref, up_ref, down_ref, buf, sems):
    rows = q_hbm.shape[0]
    loads = [
        pltpu.make_async_copy(ref, buf.at[i], sems.at[i])
        for i, ref in enumerate((q_hbm, k_hbm, v_hbm))
    ]
    edges = [
        pltpu.make_async_copy(ref.at[pl.ds(lo, size)], out.at[pl.ds(at, size)], sems.at[n])
        for n, ref, lo, size, out, at in (
            (3, res_hbm, rows - HALO, HALO, up_ref, 0),
            (4, cot_hbm, rows - NEAR, NEAR, up_ref, HALO),
            (5, res_hbm, 0, HALO, down_ref, 0),
            (6, cot_hbm, 0, NEAR, down_ref, HALO),
        )
    ]
    for copy in loads + edges:
        copy.start()
    for part, copy in enumerate(loads):
        copy.wait()
        turned = buf[part].T
        for h in range(HEADS):
            o_ref[h, part * HEAD : (part + 1) * HEAD, :] = turned[h * HEAD : (h + 1) * HEAD, :]
    for copy in edges:
        copy.wait()


def pre(q, k, v, res, cot):
    edge = jax.ShapeDtypeStruct((HALO + NEAR, q.shape[1]), BF)
    return pl.pallas_call(
        pre_kernel,
        out_shape=(jax.ShapeDtypeStruct((HEADS, 3 * HEAD, LANES), BF), edge, edge),
        in_specs=[pl.BlockSpec(memory_space=pltpu.HBM)] * 5,
        scratch_shapes=[pltpu.VMEM((3,) + q.shape, BF), pltpu.SemaphoreType.DMA((7,))],
        compiler_params=params(8),
        cost_estimate=cost(1e6, 3e6),
        name="pre",
    )(q, k, v, res, cot)


def fwd_kernel(len_ref, x_ref, e_hbm, o_ref, inv_ref, pay_ref, kaug, vaug, even, odd, ebuf, sems):
    blocks = x_ref.shape[0]
    frames = blocks * LANES
    scale = math.log2(math.e) / math.sqrt(HEAD)
    length = len_ref[0]
    for j in range(blocks):
        rows = slice(j * LANES, (j + 1) * LANES)
        bias = jnp.where(j * LANES + lane_iota((32, LANES)) < length, 0.0, -1e30)
        bias = jnp.where(row_iota((32, LANES)) == 0, bias, 0.0)
        turned = jnp.concatenate([x_ref[j, HEAD : 2 * HEAD, :], bias.astype(BF)], axis=0).T
        kaug[rows, 0:LANES] = turned
        kaug[rows, LANES : 2 * LANES] = turned
        vaug[0:HEAD, rows] = x_ref[j, 2 * HEAD : 3 * HEAD, :]
        vaug[HEAD : HEAD + 16, rows] = jnp.where(row_iota((16, LANES)) == 0, 1.0, 0.0).astype(BF)
    per = QT // LANES
    count = frames // QT
    tiles = frames // KT
    one = jnp.where(row_iota((32, QT)) == 0, 1.0, 0.0).astype(BF)

    def queries(i):
        qt = jnp.concatenate([x_ref[i * per + p, 0:HEAD, :] for p in range(per)], axis=1)
        qs = qt.astype(F32) * scale
        hi = qs.astype(BF)
        lo = (qs - hi.astype(F32)).astype(BF)
        return jnp.concatenate([hi, one, lo, jnp.zeros((32, QT), BF)], axis=0)

    def score(buf, t, qaug, top):
        s = dot(kaug[t * KT : (t + 1) * KT, :], qaug)
        buf[t * KT : (t + 1) * KT, :] = s
        part = jnp.max(s.reshape(KT // 8, 8, QT), axis=0)
        return part if top is None else jnp.maximum(top, part)

    def out_copy(i, t):
        at = pl.ds(t * KT, 2 * KT)
        return pltpu.make_async_copy(ebuf.at[i, at], e_hbm.at[i, at], sems.at[i, t // 2])

    bufs = (even, odd)
    top = None
    qaug = queries(0)
    for t in range(tiles):
        top = score(bufs[0], t, qaug, top)
    for i in range(count):
        peak = jnp.max(top, axis=0, keepdims=True)
        top = None
        if i + 1 < count:
            qaug = queries(i + 1)
        acc = jnp.zeros((HEAD + 16, QT), F32)
        for t in range(tiles):
            rows = slice(t * KT, (t + 1) * KT)
            if i + 1 < count:
                top = score(bufs[(i + 1) % 2], t, qaug, top)
            e = jnp.exp2(bufs[i % 2][rows, :] - peak).astype(BF)
            ebuf[i, rows, :] = e
            acc = acc + dot(vaug[:, rows], e)
            if t % 2 == 1:
                out_copy(i, t - 1).start()
        inv = 1.0 / acc[HEAD : HEAD + 1, :]
        out = acc[0:HEAD, :] * inv
        at = slice(i * QT, (i + 1) * QT)
        o_ref[:, at] = out
        inv_ref[:, at] = jnp.broadcast_to(inv, (8, QT))
        rounded = out.astype(BF)
        for p in range(per):
            pay_ref[i * per + p, 0:HEAD, :] = rounded[:, p * LANES : (p + 1) * LANES]
    low = HEAD // 2
    lane = lane_iota((low, LANES))
    left = lane < LANES // 2
    outer_lanes = jnp.logical_or(lane < HALO, lane >= LANES - HALO)
    for j in range(blocks):
        after = pay_ref[min(j + 1, blocks - 1), 0:HEAD, :].astype(F32)
        before = pay_ref[max(j - 1, 0), 0:HEAD, :].astype(F32)
        first = jnp.where(left, after[0:low], before[0:low])
        second = jnp.where(left, after[low:HEAD], before[low:HEAD])
        second = pltpu.roll(second, LANES // 2, 1)
        pay_ref[j, HEAD : HEAD + low, :] = jnp.where(outer_lanes, first, second).astype(BF)
    for i in range(count):
        for t in range(0, tiles, 2):
            out_copy(i, t).wait()


def fwd(length, x):
    blocks = x.shape[0]
    frames = blocks * LANES
    steps = frames // QT
    return pl.pallas_call(
        fwd_kernel,
        out_shape=(
            pltpu.HBM((steps, frames, QT), BF),
            pltpu.HBM((HEAD, frames), F32),
            jax.ShapeDtypeStruct((8, frames), F32),
            jax.ShapeDtypeStruct((blocks, HEAD + HEAD // 2, LANES), BF),
        ),
        in_specs=[pl.BlockSpec(memory_space=pltpu.SMEM), pl.BlockSpec()],
        out_specs=(
            pl.BlockSpec(memory_space=pl.ANY),
            pl.BlockSpec(),
            pl.BlockSpec(),
            pl.BlockSpec(),
        ),
        scratch_shapes=[
            pltpu.VMEM((frames, 2 * LANES), BF),
            pltpu.VMEM((HEAD + 16, frames), BF),
            pltpu.VMEM((frames, QT), F32),
            pltpu.VMEM((frames, QT), F32),
            pltpu.VMEM((steps, frames, QT), BF),
            pltpu.SemaphoreType.DMA((steps, frames // KT // 2)),
        ],
        compiler_params=params(30),
        cost_estimate=cost(9e9, 1e7),
        name="attend",
    )(length, x)


def conv_kernel_body(
    info_ref, att_ref, res_hbm, cot_hbm, left_hbm, right_hbm, w_hbm, taps_hbm,
    out_hbm, pay_hbm, keep_hbm, send_hbm,
    lhs, block_in, masked, cot, grad, taps_sum, bg_ref,
    res_ref, cot_ref, left_ref, right_ref, weight, taps_ref, proj, out_ref, pay_ref, sems,
):
    rows, width = res_ref.shape
    cols = width // LANES
    span = rows + 2 * HALO
    length = info_ref[0]
    first = info_ref[1]
    zbit = info_ref[3]
    pieces = cols // 2
    wide = 2 * LANES

    def chunk(n):
        at = pl.ds(pl.multiple_of(n * wide, wide), wide)
        return pltpu.make_async_copy(w_hbm.at[:, at], weight.at[:, at], sems.at[n])

    small = [
        pltpu.make_async_copy(src, dst, sems.at[pieces + n])
        for n, (src, dst) in enumerate(
            (
                (res_hbm, res_ref),
                (cot_hbm, cot_ref),
                (left_hbm, left_ref),
                (right_hbm, right_ref),
                (taps_hbm, taps_ref),
            )
        )
    ]
    chunk(0).start()
    for load in small:
        load.start()
    for n in range(1, pieces):
        chunk(n).start()
    main = jnp.concatenate([att_ref[h, 0:HEAD, :] for h in range(HEADS)], axis=0)
    packed = [att_ref[h, HEAD : HEAD + HEAD // 2, :].astype(F32) for h in range(HEADS)]
    halo = jnp.concatenate(
        [part for p in packed for part in (p, pltpu.roll(p, LANES // 2, 1))], axis=0
    ).astype(BF)
    halo = halo.T
    lhs[0:HALO, :] = halo[LANES - HALO : LANES, :]
    lhs[HALO : HALO + rows, :] = main.T
    lhs[HALO + rows : span, :] = halo[0:HALO, :]
    frame = first - HALO + row_iota((span, LANES))
    valid = jnp.logical_and(frame >= 0, frame < length)
    mid = rows + 32

    def project(n):
        at = pl.ds(pl.multiple_of(n * wide, wide), wide)
        proj[...] = dot(lhs[...], weight[:, at])

    def place(n):
        for m in range(2):
            c = 2 * n + m
            at = pl.ds(pl.multiple_of(c * LANES, LANES), LANES)
            res = jnp.concatenate(
                [left_ref[0:HALO, at], res_ref[:, at], right_ref[0:HALO, at]], axis=0
            ).astype(F32)
            block = res + proj[:, m * LANES : (m + 1) * LANES]
            block_in[c] = block
            masked[c] = jnp.where(valid, block, 0.0).astype(BF).astype(F32)
            cot[c] = jnp.concatenate(
                [
                    left_ref[HALO : HALO + NEAR, at],
                    cot_ref[:, at],
                    right_ref[HALO : HALO + NEAR, at],
                ],
                axis=0,
            ).astype(F32)

    for load in small:
        load.wait()
    chunk(0).wait()
    project(0)
    place(0)

    def channels(c):
        at = pl.ds(pl.multiple_of(c * LANES, LANES), LANES)
        acc = jnp.zeros((mid, LANES), F32)
        for r in range(TAPS):
            acc = acc + taps_ref[r : r + 1, at] * masked[c, 1 + r : 1 + r + mid, :]
        gate = jax.nn.sigmoid(acc)
        cg = (cot[c] * (gate * (1.0 + acc * (1.0 - gate)))).astype(BF).astype(F32)
        grad[...] = cg
        out_ref[:, at] = (
            block_in[c, HALO : HALO + rows, :] + (acc * gate)[16 : 16 + rows, :]
        ).astype(BF)
        own = cg[16 : 16 + rows, :]
        back = jnp.zeros((rows, LANES), F32)
        for r in range(TAPS):
            back = back + taps_ref[r : r + 1, at] * grad[31 - r : 31 - r + rows, :]
            prod = own * masked[c, 17 + r : 17 + r + rows, :]
            prod = jnp.sum(prod.reshape(rows // 8, 8, LANES), axis=0)
            taps_sum[r // 2, pl.ds((r % 2) * cols + c, 1), :] = jnp.sum(prod, axis=0, keepdims=True)
        own_valid = valid[HALO : HALO + rows, :]
        bg_ref[:, at] = (cot[c, 16 : 16 + rows, :] + jnp.where(own_valid, back, 0.0)).astype(BF)

    @pl.loop(0, pieces)
    def _(n):
        @pl.when(n < pieces - 1)
        def _():
            chunk(n + 1).wait()

        after = lax.rem(n + 1, pieces)
        project(after)
        channels(2 * n)
        channels(2 * n + 1)
        place(after)

    taps_sum[HEADS - 1, pl.ds(cols, cols), :] = jnp.zeros((cols, LANES), F32)
    taps_sum[:, pl.ds(2 * cols, 8), :] = jnp.zeros((HEADS, 8, LANES), F32)
    half = width // 2
    mine = pl.ds(pl.multiple_of(zbit * half, LANES), half)
    other = pl.ds(pl.multiple_of((1 - zbit) * half, LANES), half)
    stores = [
        pltpu.make_async_copy(src, dst, sems.at[pieces + 5 + n])
        for n, (src, dst) in enumerate(
            (
                (bg_ref.at[:, other], send_hbm),
                (bg_ref.at[:, mine], keep_hbm),
                (out_ref, out_hbm),
            )
        )
    ]
    for store in stores:
        store.start()
    pay_ref[:, HEAD:LANES, :] = taps_sum[...].astype(BF)
    bg = bg_ref[...]
    for h in range(0, HEADS, 2):
        mixed = lax.dot_general(
            weight[h * HEAD : (h + 2) * HEAD, :], bg, (((1,), (1,)), ((), ())),
            preferred_element_type=F32,
        ).astype(BF)
        pay_ref[h, 0:HEAD, :] = mixed[0:HEAD]
        pay_ref[h + 1, 0:HEAD, :] = mixed[HEAD : 2 * HEAD]
        if h % 4 == 2:
            at = pl.ds(h - 2, 4)
            store = pltpu.make_async_copy(
                pay_ref.at[at], pay_hbm.at[at], sems.at[pieces + 8 + h // 4]
            )
            store.start()
            stores.append(store)
    for store in stores:
        store.wait()


def conv(info, att, res, cot, left, right, w, taps):
    rows, width = res.shape
    cols = width // LANES
    span = rows + 2 * HALO
    vm = pl.BlockSpec()
    return pl.pallas_call(
        conv_kernel_body,
        out_shape=(
            pltpu.HBM((rows, width), BF),
            pltpu.HBM((HEADS, LANES, LANES), BF),
            pltpu.HBM((rows, width // 2), BF),
            pltpu.HBM((rows, width // 2), BF),
        ),
        in_specs=[pl.BlockSpec(memory_space=pltpu.SMEM)]
        + [vm]
        + [pl.BlockSpec(memory_space=pl.ANY)] * 6,
        out_specs=(
            pl.BlockSpec(memory_space=pl.ANY),
        )
        * 4,
        scratch_shapes=[
            pltpu.VMEM((span, width), BF),
            pltpu.VMEM((cols, span, LANES), F32),
            pltpu.VMEM((cols, span, LANES), F32),
            pltpu.VMEM((cols, rows + 32, LANES), F32),
            pltpu.VMEM((rows + 32, LANES), F32),
            pltpu.VMEM((HEADS, 32, LANES), F32),
            pltpu.VMEM((rows, width), BF),
            pltpu.VMEM((rows, width), BF),
            pltpu.VMEM((rows, width), BF),
            pltpu.VMEM((HALO + NEAR, width), BF),
            pltpu.VMEM((HALO + NEAR, width), BF),
            pltpu.VMEM((width, width), BF),
            pltpu.VMEM((TAPS, width), F32),
            pltpu.VMEM((span, 2 * LANES), F32),
            pltpu.VMEM((rows, width), BF),
            pltpu.VMEM((HEADS, LANES, LANES), BF),
            pltpu.SemaphoreType.DMA((cols // 2 + 12,)),
        ],
        compiler_params=params(20),
        cost_estimate=cost(9e9, 1e7),
        name="convolve",
    )(info, att, res, cot, left, right, w, taps)


def outer_kernel(info_ref, *refs):
    o_ref = refs[-1]
    core = info_ref[2]
    tall, wide = refs[0:4], refs[4:8]
    part = wide[0].shape[1] // 2
    at = pl.ds(pl.multiple_of(core * part, LANES), part)
    rhs = jnp.concatenate([ref[:, at] for ref in wide], axis=0)
    for h in range(0, HEADS, 4):
        lhs = jnp.concatenate(
            [
                jnp.concatenate([ref[g, 0:HEAD, :] for ref in tall], axis=1)
                for g in range(h, h + 4)
            ],
            axis=0,
        )
        full = dot(lhs, rhs).astype(BF)
        for g in range(4):
            for c in range(part // LANES):
                o_ref[h + g, c * HEAD : (c + 1) * HEAD, :] = full[
                    g * HEAD : (g + 1) * HEAD, c * LANES : (c + 1) * LANES
                ]


def outer(info, tall, wide):
    part = wide[0].shape[1] // 2
    return pl.pallas_call(
        outer_kernel,
        out_shape=pltpu.HBM((HEADS, part // LANES * HEAD + 32, LANES), BF),
        in_specs=[pl.BlockSpec(memory_space=pltpu.SMEM)] + [pl.BlockSpec()] * 8,
        compiler_params=params(20),
        cost_estimate=cost(1e9, 4e6),
        name="outer",
    )(info, *tall, *wide)


def tail_kernel(g_ref, w_ref, o_ref, taps, sems):
    taps[...] = jnp.sum(g_ref[:, HEAD:LANES, :].astype(F32), axis=0).astype(BF)
    base = o_ref.shape[1] - 32
    copies = [
        pltpu.make_async_copy(taps, o_ref.at[h, pl.ds(base, 32), :], sems.at[h])
        for h in range(HEADS)
    ]
    for copy in copies:
        copy.start()
    for copy in copies:
        copy.wait()


def tail(g, w):
    return pl.pallas_call(
        tail_kernel,
        out_shape=pltpu.HBM(w.shape, BF),
        in_specs=[pl.BlockSpec(), pl.BlockSpec(memory_space=pl.ANY)],
        out_specs=pl.BlockSpec(memory_space=pl.ANY),
        scratch_shapes=[pltpu.VMEM((32, LANES), BF), pltpu.SemaphoreType.DMA((HEADS,))],
        input_output_aliases={1: 0},
        compiler_params=params(8),
        cost_estimate=cost(1e6, 1e6),
        name="tail",
    )(g, w)


def bwd_kernel(x_ref, g_ref, e_ref, o_ref, inv_ref, pay_ref, vaug, kt, dk, dv):
    step = pl.program_id(0)
    blocks = x_ref.shape[0]
    scale = 1.0 / math.sqrt(HEAD)

    @pl.when(step == 0)
    def _():
        ones = jnp.where(row_iota((32, LANES)) < 3, 1.0, 0.0).astype(BF)
        for j in range(blocks):
            rows = pl.ds(j * LANES, LANES)
            turned = jnp.concatenate([x_ref[j, 2 * HEAD : 3 * HEAD, :], ones], axis=0).T
            vaug[rows, 0:LANES] = turned
            vaug[rows, LANES : 2 * LANES] = turned
            kt[:, rows] = x_ref[j, HEAD : 2 * HEAD, :]
        dk[...] = jnp.zeros_like(dk)
        dv[...] = jnp.zeros_like(dv)

    per = QT // LANES
    gt = jnp.concatenate([g_ref[step * per + p, 0:HEAD, :] for p in range(per)], axis=1).astype(F32)
    qt = jnp.concatenate([x_ref[step * per + p, 0:HEAD, :] for p in range(per)], axis=1)
    inv = inv_ref[0:1, :]
    centre = jnp.sum(gt * o_ref[...], axis=0, keepdims=True)
    ginv = gt * inv
    sg = ginv * scale
    hi = sg.astype(BF)
    lo = (sg - hi.astype(F32)).astype(BF)
    rest = centre * inv * (-scale)
    c0 = rest.astype(BF).astype(F32)
    c1 = (rest - c0).astype(BF).astype(F32)
    c2 = rest - c0 - c1
    at = row_iota((32, QT))
    crows = jnp.where(at == 0, c0, jnp.where(at == 1, c1, jnp.where(at == 2, c2, 0.0))).astype(BF)
    zeros = jnp.zeros((32, QT), BF)
    gaug = jnp.concatenate([hi, crows, lo, zeros], axis=0)
    gn = jnp.concatenate([ginv.astype(BF), zeros], axis=0).T
    qn = jnp.concatenate([qt, zeros], axis=0).T
    dq = jnp.zeros((HEAD, QT), F32)
    for t in range(kt.shape[1] // KT):
        rows = slice(t * KT, (t + 1) * KT)
        slope = dot(vaug[rows, :], gaug)
        e = e_ref[0, rows, :]
        ds = (e.astype(F32) * slope).astype(BF)
        dv[rows, :] += dot(e, gn)
        dk[rows, :] += dot(ds, qn)
        dq = dq + dot(kt[:, rows], ds)
    dq = dq.astype(BF)
    for p in range(per):
        pay_ref[step * per + p, 0:HEAD, :] = dq[:, p * LANES : (p + 1) * LANES]

    @pl.when(step == pl.num_programs(0) - 1)
    def _():
        for j in range(blocks):
            rows = pl.ds(j * LANES, LANES)
            pay_ref[j, HEAD : 2 * HEAD, :] = dk[rows, :].T[0:HEAD].astype(BF)
            pay_ref[j, 2 * HEAD : 3 * HEAD, :] = dv[rows, :].T[0:HEAD].astype(BF)


def bwd(x, g, e, o, inv):
    blocks = x.shape[0]
    frames = blocks * LANES
    steps = frames // QT
    return pl.pallas_call(
        bwd_kernel,
        grid=(steps,),
        out_shape=pltpu.HBM((blocks, 3 * HEAD, LANES), BF),
        in_specs=[
            pl.BlockSpec((blocks, 3 * HEAD, LANES), lambda i: (0, 0, 0)),
            pl.BlockSpec((blocks, LANES, LANES), lambda i: (0, 0, 0)),
            pl.BlockSpec((1, frames, QT), lambda i: (i, 0, 0)),
            pl.BlockSpec((HEAD, QT), lambda i: (0, i)),
            pl.BlockSpec((8, QT), lambda i: (0, i)),
        ],
        out_specs=pl.BlockSpec((blocks, 3 * HEAD, LANES), lambda i: (0, 0, 0)),
        scratch_shapes=[
            pltpu.VMEM((frames, 2 * LANES), BF),
            pltpu.VMEM((HEAD, frames), BF),
            pltpu.VMEM((frames, LANES), F32),
            pltpu.VMEM((frames, LANES), F32),
        ],
        compiler_params=params(30),
        cost_estimate=cost(2e10, 1e7),
        name="attend_back",
    )(x, g, e, o, inv)


def post_kernel(x_ref, q_ref, k_ref, v_ref):
    for part, ref in enumerate((q_ref, k_ref, v_ref)):
        rows = slice(part * HEAD, (part + 1) * HEAD)
        ref[...] = jnp.concatenate([x_ref[h, rows, :] for h in range(HEADS)], axis=0).T


def post(x):
    shape = jax.ShapeDtypeStruct((LANES, HEADS * HEAD), BF)
    return pl.pallas_call(
        post_kernel,
        out_shape=(shape,) * 3,
        compiler_params=params(12),
        cost_estimate=cost(1e6, 3e6),
        name="post",
    )(x)


GROUP = 8
PIECE = 120


def pack_kernel(info_ref, x_ref, *refs):
    outs, buf = refs[:-1], refs[-1]
    cols = x_ref.shape[1] // HEAD
    below = cols * HEAD
    for r in range(HEAD // 16):
        for c in range(2 * cols):
            at = (c % cols) * HEAD + 16 * r
            tiles = [x_ref[2 * i + c // cols, at : at + 16, :].astype(F32) for i in range(HEADS // 2)]
            both = sum(tiles[1:], tiles[0])
            for e in range(2):
                n = (2 * r + e) * 2 * cols + c
                buf[8 * n : 8 * n + 8, :] = both[8 * e : 8 * e + 8, :]
    share = buf.shape[0] // GROUP
    for k in range(GROUP):
        j = jnp.bitwise_xor(info_ref[4], k)
        taps = [x_ref[2 * j + e, below : below + 32, :].astype(F32)[0:24] for e in range(2)]
        outs[k // 2][k % 2] = jnp.concatenate(
            [buf[pl.ds(pl.multiple_of(share * j, 8), share), :]] + taps, axis=0
        ).astype(BF)


def pack(info, x):
    units = x.shape[1] // HEAD * HEAD * 2
    return pl.pallas_call(
        pack_kernel,
        out_shape=(pltpu.HBM((2, PIECE, LANES), BF),) * (GROUP // 2),
        in_specs=[pl.BlockSpec(memory_space=pltpu.SMEM), pl.BlockSpec()],
        scratch_shapes=[pltpu.VMEM((units, LANES), F32)],
        compiler_params=params(12),
        cost_estimate=cost(1e6, 3e6),
        name="pack",
    )(info, x)


def merge_kernel(*refs):
    keep_ref, send_ref = refs[-2:]
    both = sum([ref[...].astype(F32) for ref in refs[1:-2]], refs[0][...].astype(F32))
    keep_ref[...] = both[0].astype(BF)
    send_ref[...] = both[1].astype(BF)


def merge(xs):
    return pl.pallas_call(
        merge_kernel,
        out_shape=(pltpu.HBM(xs[0].shape[1:], BF),) * 2,
        compiler_params=params(8),
        cost_estimate=cost(1e6, 1e6),
        name="merge",
    )(*xs)


def total_kernel(*refs):
    o_ref = refs[-1]
    total = sum([ref[...].astype(F32) for ref in refs[1:-1]], refs[0][...].astype(F32))
    total = total * (1.0 / o_ref.shape[0])
    o_ref[...] = jnp.broadcast_to(total.astype(BF)[None], o_ref.shape)


def total(xs, batch):
    return pl.pallas_call(
        total_kernel,
        out_shape=pltpu.HBM((batch,) + xs[0].shape, BF),
        compiler_params=params(12),
        cost_estimate=cost(1e6, 1e6),
        name="total",
    )(*xs)


def unpack_kernel(x_ref, w_ref, k_ref):
    width = w_ref.shape[1]
    cols = width // LANES
    share = HEAD // 8 * cols // 2 // GROUP
    for z in range(2):
        for j in range(GROUP):
            x = x_ref[4 * (j // 2) + 2 * z + j % 2].astype(F32)
            for i in range(share):
                n = j * share + i
                r, c = 8 * (n // (cols // 2)), width // 2 * z + LANES * (n % (cols // 2))
                w_ref[r : r + 8, c : c + LANES] = x[8 * i : 8 * i + 8, :]
    for j in range(GROUP):
        x = x_ref[4 * (j // 2) + j % 2].astype(F32) + x_ref[4 * (j // 2) + 2 + j % 2].astype(F32)
        for i in range(4):
            if 4 * j + i < TAPS:
                for c in range(cols):
                    at = 8 * share + cols * i + c
                    k_ref[4 * j + i : 4 * j + i + 1, c * LANES : (c + 1) * LANES] = x[at : at + 1, :]


def unpack(x, width):
    return pl.pallas_call(
        unpack_kernel,
        out_shape=(
            jax.ShapeDtypeStruct((HEAD, width), F32),
            jax.ShapeDtypeStruct((TAPS, width), F32),
        ),
        compiler_params=params(12),
        cost_estimate=cost(1e6, 1e6),
        name="unpack",
    )(x)


def in_hbm(x):
    return pltpu.with_memory_space_constraint(x, pltpu.HBM)


def exchange(x, axis, groups=None):
    return lax.all_to_all(
        x, axis, split_axis=0, concat_axis=0, tiled=True, axis_index_groups=groups
    )


def shards(query_proj, key_proj, value_proj, residual, lengths, out_weight, conv_kernel, cotangent):
    rows, width = query_proj.shape[1:]
    count = lax.axis_size("seq")
    me = lax.axis_index("seq")
    res, cot = residual[0], cotangent[0]
    up = [(i, i + 1) for i in range(count - 1)]
    down = [(i + 1, i) for i in range(count - 1)]
    cores = [(i, i ^ 1) for i in range(count)]
    batch = lax.axis_size("dp")
    depth = lax.axis_index("dp")
    levels = [(i, i ^ 2) for i in range(batch)]

    def hop(k):
        return [(i, i ^ (4 * (k // 2) + k % 2)) for i in range(batch)]

    query, key, value, res, cot, out_weight, conv_kernel = (
        in_hbm(x)
        for x in (query_proj[0], key_proj[0], value_proj[0], res, cot, out_weight, conv_kernel)
    )
    payload, edge_up, edge_down = pre(query, key, value, res, cot)
    heads = exchange(payload, "seq")
    left = lax.ppermute(edge_up, "seq", up)
    right = lax.ppermute(edge_down, "seq", down)
    heads, left, right = lax.optimization_barrier((heads, left, right))
    weights, mixed, inv, payload = fwd(lengths, heads)
    attended = exchange(payload, "seq")
    att_level = lax.ppermute(attended, "dp", levels)
    att_core = lax.ppermute(attended, "seq", cores)
    member = depth // 4 * 2 + depth % 2
    info = jnp.stack([lengths[0], me * rows, me % 2, depth // 2 % 2, member]).astype(jnp.int32)
    block_out, payload, keep, send = conv(
        info, attended, res, cot, in_hbm(left), in_hbm(right), out_weight, conv_kernel
    )
    att_level, send = lax.optimization_barrier((att_level, send))
    att_both = lax.ppermute(att_level, "seq", cores)
    grads = exchange(payload, "seq")
    level = lax.ppermute(send, "dp", levels)
    partner = lax.ppermute(keep, "seq", cores)
    both = lax.ppermute(level, "seq", cores)
    partial = outer(
        info, (attended, att_core, att_level, att_both), (in_hbm(keep), partner, level, both)
    )
    partial = exchange(tail(grads, partial), "seq")
    payload = bwd(heads, grads, in_hbm(weights), in_hbm(mixed), inv)
    payload, partial = lax.optimization_barrier((payload, partial))
    back = exchange(payload, "seq")
    packed = pack(info, partial)
    level_parts = [in_hbm(packed[0])] + [
        lax.ppermute(packed[k], "dp", hop(2 * k)) for k in range(1, GROUP // 2)
    ]
    keep, send = merge(level_parts)
    packed = [in_hbm(keep), lax.ppermute(send, "dp", hop(1))]
    summed, back = lax.optimization_barrier((total(packed, batch), back))
    final = exchange(summed, "dp")
    query_grad, key_grad, value_grad = post(back)
    weight_grad, kernel_grad = unpack(final, width)
    return (
        block_out[None],
        query_grad[None],
        key_grad[None],
        value_grad[None],
        weight_grad,
        kernel_grad,
    )


def solution(mesh):
    split = P("dp", "seq", None)
    return jax.shard_map(
        shards,
        mesh=mesh,
        in_specs=(split, split, split, split, P("dp"), P(), P(), split),
        out_specs=(split, split, split, split, P("seq", None), P()),
        check_vma=False,
    )
```

```python
import math

import jax
import jax.numpy as jnp
from jax import lax
from jax.experimental import pallas as pl
from jax.experimental.pallas import tpu as pltpu
from jax.sharding import PartitionSpec as P

HEADS = 16
HEAD = 96
LANES = 128
TAPS = 31
HALF = 15
HALO = 32
NEAR = 16
QT = 512
KT = 256
BF = jnp.bfloat16
F32 = jnp.float32
MIB = 2**20


def params(mib):
    return pltpu.CompilerParams(vmem_limit_bytes=mib * MIB)


def cost(flops, moved):
    return pl.CostEstimate(flops=int(flops), bytes_accessed=int(moved), transcendentals=0)


def lane_iota(shape):
    return lax.broadcasted_iota(jnp.int32, shape, len(shape) - 1)


def row_iota(shape):
    return lax.broadcasted_iota(jnp.int32, shape, 0)


def dot(a, b):
    return jnp.dot(a, b, preferred_element_type=F32)


def pre_kernel(q_hbm, k_hbm, v_hbm, res_hbm, cot_hbm, o_ref, up_ref, down_ref, buf, sems):
    rows = q_hbm.shape[0]
    loads = [
        pltpu.make_async_copy(ref, buf.at[i], sems.at[i])
        for i, ref in enumerate((q_hbm, k_hbm, v_hbm))
    ]
    edges = [
        pltpu.make_async_copy(ref.at[pl.ds(lo, size)], out.at[pl.ds(at, size)], sems.at[n])
        for n, ref, lo, size, out, at in (
            (3, res_hbm, rows - HALO, HALO, up_ref, 0),
            (4, cot_hbm, rows - NEAR, NEAR, up_ref, HALO),
            (5, res_hbm, 0, HALO, down_ref, 0),
            (6, cot_hbm, 0, NEAR, down_ref, HALO),
        )
    ]
    for copy in loads + edges:
        copy.start()
    for part, copy in enumerate(loads):
        copy.wait()
        turned = buf[part].T
        for h in range(HEADS):
            o_ref[h, part * HEAD : (part + 1) * HEAD, :] = turned[h * HEAD : (h + 1) * HEAD, :]
    for copy in edges:
        copy.wait()


def pre(q, k, v, res, cot):
    edge = jax.ShapeDtypeStruct((HALO + NEAR, q.shape[1]), BF)
    return pl.pallas_call(
        pre_kernel,
        out_shape=(jax.ShapeDtypeStruct((HEADS, 3 * HEAD, LANES), BF), edge, edge),
        in_specs=[pl.BlockSpec(memory_space=pltpu.HBM)] * 5,
        scratch_shapes=[pltpu.VMEM((3,) + q.shape, BF), pltpu.SemaphoreType.DMA((7,))],
        compiler_params=params(8),
        cost_estimate=cost(1e6, 3e6),
        name="pre",
    )(q, k, v, res, cot)


def fwd_kernel(len_ref, x_ref, e_hbm, o_ref, inv_ref, pay_ref, kaug, vaug, even, odd, ebuf, sems):
    blocks = x_ref.shape[0]
    frames = blocks * LANES
    scale = math.log2(math.e) / math.sqrt(HEAD)
    length = len_ref[0]
    for j in range(blocks):
        rows = slice(j * LANES, (j + 1) * LANES)
        bias = jnp.where(j * LANES + lane_iota((32, LANES)) < length, 0.0, -1e30)
        bias = jnp.where(row_iota((32, LANES)) == 0, bias, 0.0)
        turned = jnp.concatenate([x_ref[j, HEAD : 2 * HEAD, :], bias.astype(BF)], axis=0).T
        kaug[rows, 0:LANES] = turned
        kaug[rows, LANES : 2 * LANES] = turned
        vaug[0:HEAD, rows] = x_ref[j, 2 * HEAD : 3 * HEAD, :]
        vaug[HEAD : HEAD + 16, rows] = jnp.where(row_iota((16, LANES)) == 0, 1.0, 0.0).astype(BF)
    per = QT // LANES
    count = frames // QT
    tiles = frames // KT
    one = jnp.where(row_iota((32, QT)) == 0, 1.0, 0.0).astype(BF)

    def queries(i):
        qt = jnp.concatenate([x_ref[i * per + p, 0:HEAD, :] for p in range(per)], axis=1)
        qs = qt.astype(F32) * scale
        hi = qs.astype(BF)
        lo = (qs - hi.astype(F32)).astype(BF)
        return jnp.concatenate([hi, one, lo, jnp.zeros((32, QT), BF)], axis=0)

    def score(buf, t, qaug, top):
        s = dot(kaug[t * KT : (t + 1) * KT, :], qaug)
        buf[t * KT : (t + 1) * KT, :] = s
        part = jnp.max(s.reshape(KT // 8, 8, QT), axis=0)
        return part if top is None else jnp.maximum(top, part)

    def out_copy(i, t):
        at = pl.ds(t * KT, 2 * KT)
        return pltpu.make_async_copy(ebuf.at[i, at], e_hbm.at[i, at], sems.at[i, t // 2])

    bufs = (even, odd)
    top = None
    qaug = queries(0)
    for t in range(tiles):
        top = score(bufs[0], t, qaug, top)
    for i in range(count):
        peak = jnp.max(top, axis=0, keepdims=True)
        top = None
        if i + 1 < count:
            qaug = queries(i + 1)
        acc = jnp.zeros((HEAD + 16, QT), F32)
        for t in range(tiles):
            rows = slice(t * KT, (t + 1) * KT)
            if i + 1 < count:
                top = score(bufs[(i + 1) % 2], t, qaug, top)
            e = jnp.exp2(bufs[i % 2][rows, :] - peak).astype(BF)
            ebuf[i, rows, :] = e
            acc = acc + dot(vaug[:, rows], e)
            if t % 2 == 1:
                out_copy(i, t - 1).start()
        inv = 1.0 / acc[HEAD : HEAD + 1, :]
        out = acc[0:HEAD, :] * inv
        at = slice(i * QT, (i + 1) * QT)
        o_ref[:, at] = out
        inv_ref[:, at] = jnp.broadcast_to(inv, (8, QT))
        rounded = out.astype(BF)
        for p in range(per):
            pay_ref[i * per + p, 0:HEAD, :] = rounded[:, p * LANES : (p + 1) * LANES]
    low = HEAD // 2
    lane = lane_iota((low, LANES))
    left = lane < LANES // 2
    outer_lanes = jnp.logical_or(lane < HALO, lane >= LANES - HALO)
    for j in range(blocks):
        after = pay_ref[min(j + 1, blocks - 1), 0:HEAD, :].astype(F32)
        before = pay_ref[max(j - 1, 0), 0:HEAD, :].astype(F32)
        first = jnp.where(left, after[0:low], before[0:low])
        second = jnp.where(left, after[low:HEAD], before[low:HEAD])
        second = pltpu.roll(second, LANES // 2, 1)
        pay_ref[j, HEAD : HEAD + low, :] = jnp.where(outer_lanes, first, second).astype(BF)
    for i in range(count):
        for t in range(0, tiles, 2):
            out_copy(i, t).wait()


def fwd(length, x):
    blocks = x.shape[0]
    frames = blocks * LANES
    steps = frames // QT
    return pl.pallas_call(
        fwd_kernel,
        out_shape=(
            pltpu.HBM((steps, frames, QT), BF),
            pltpu.HBM((HEAD, frames), F32),
            jax.ShapeDtypeStruct((8, frames), F32),
            jax.ShapeDtypeStruct((blocks, HEAD + HEAD // 2, LANES), BF),
        ),
        in_specs=[pl.BlockSpec(memory_space=pltpu.SMEM), pl.BlockSpec()],
        out_specs=(
            pl.BlockSpec(memory_space=pl.ANY),
            pl.BlockSpec(),
            pl.BlockSpec(),
            pl.BlockSpec(),
        ),
        scratch_shapes=[
            pltpu.VMEM((frames, 2 * LANES), BF),
            pltpu.VMEM((HEAD + 16, frames), BF),
            pltpu.VMEM((frames, QT), F32),
            pltpu.VMEM((frames, QT), F32),
            pltpu.VMEM((steps, frames, QT), BF),
            pltpu.SemaphoreType.DMA((steps, frames // KT // 2)),
        ],
        compiler_params=params(30),
        cost_estimate=cost(9e9, 1e7),
        name="attend",
    )(length, x)


def conv_kernel_body(
    info_ref, att_ref, res_hbm, cot_hbm, left_hbm, right_hbm, w_hbm, taps_hbm,
    out_hbm, pay_hbm, keep_hbm, send_hbm,
    lhs, block_in, masked, cot, grad, taps_sum, bg_ref,
    res_ref, cot_ref, left_ref, right_ref, weight, taps_ref, proj, out_ref, pay_ref, sems,
):
    rows, width = res_ref.shape
    cols = width // LANES
    span = rows + 2 * HALO
    length = info_ref[0]
    first = info_ref[1]
    zbit = info_ref[3]
    pieces = cols // 2
    wide = 2 * LANES

    def chunk(n):
        at = pl.ds(pl.multiple_of(n * wide, wide), wide)
        return pltpu.make_async_copy(w_hbm.at[:, at], weight.at[:, at], sems.at[n])

    small = [
        pltpu.make_async_copy(src, dst, sems.at[pieces + n])
        for n, (src, dst) in enumerate(
            (
                (res_hbm, res_ref),
                (cot_hbm, cot_ref),
                (left_hbm, left_ref),
                (right_hbm, right_ref),
                (taps_hbm, taps_ref),
            )
        )
    ]
    chunk(0).start()
    for load in small:
        load.start()
    for n in range(1, pieces):
        chunk(n).start()
    main = jnp.concatenate([att_ref[h, 0:HEAD, :] for h in range(HEADS)], axis=0)
    packed = [att_ref[h, HEAD : HEAD + HEAD // 2, :].astype(F32) for h in range(HEADS)]
    halo = jnp.concatenate(
        [part for p in packed for part in (p, pltpu.roll(p, LANES // 2, 1))], axis=0
    ).astype(BF)
    halo = halo.T
    lhs[0:HALO, :] = halo[LANES - HALO : LANES, :]
    lhs[HALO : HALO + rows, :] = main.T
    lhs[HALO + rows : span, :] = halo[0:HALO, :]
    frame = first - HALO + row_iota((span, LANES))
    valid = jnp.logical_and(frame >= 0, frame < length)
    mid = rows + 32

    def project(n):
        at = pl.ds(pl.multiple_of(n * wide, wide), wide)
        proj[...] = dot(lhs[...], weight[:, at])

    def place(n):
        for m in range(2):
            c = 2 * n + m
            at = pl.ds(pl.multiple_of(c * LANES, LANES), LANES)
            res = jnp.concatenate(
                [left_ref[0:HALO, at], res_ref[:, at], right_ref[0:HALO, at]], axis=0
            ).astype(F32)
            block = res + proj[:, m * LANES : (m + 1) * LANES]
            block_in[c] = block
            masked[c] = jnp.where(valid, block, 0.0).astype(BF).astype(F32)
            cot[c] = jnp.concatenate(
                [
                    left_ref[HALO : HALO + NEAR, at],
                    cot_ref[:, at],
                    right_ref[HALO : HALO + NEAR, at],
                ],
                axis=0,
            ).astype(F32)

    for load in small:
        load.wait()
    chunk(0).wait()
    project(0)
    place(0)

    def channels(c):
        at = pl.ds(pl.multiple_of(c * LANES, LANES), LANES)
        acc = jnp.zeros((mid, LANES), F32)
        for r in range(TAPS):
            acc = acc + taps_ref[r : r + 1, at] * masked[c, 1 + r : 1 + r + mid, :]
        gate = jax.nn.sigmoid(acc)
        cg = (cot[c] * (gate * (1.0 + acc * (1.0 - gate)))).astype(BF).astype(F32)
        grad[...] = cg
        out_ref[:, at] = (
            block_in[c, HALO : HALO + rows, :] + (acc * gate)[16 : 16 + rows, :]
        ).astype(BF)
        own = cg[16 : 16 + rows, :]
        back = jnp.zeros((rows, LANES), F32)
        for r in range(TAPS):
            back = back + taps_ref[r : r + 1, at] * grad[31 - r : 31 - r + rows, :]
            prod = own * masked[c, 17 + r : 17 + r + rows, :]
            prod = jnp.sum(prod.reshape(rows // 8, 8, LANES), axis=0)
            taps_sum[r // 2, pl.ds((r % 2) * cols + c, 1), :] = jnp.sum(prod, axis=0, keepdims=True)
        own_valid = valid[HALO : HALO + rows, :]
        bg_ref[:, at] = (cot[c, 16 : 16 + rows, :] + jnp.where(own_valid, back, 0.0)).astype(BF)

    @pl.loop(0, pieces)
    def _(n):
        @pl.when(n < pieces - 1)
        def _():
            chunk(n + 1).wait()

        after = lax.rem(n + 1, pieces)
        project(after)
        channels(2 * n)
        channels(2 * n + 1)
        place(after)

    taps_sum[HEADS - 1, pl.ds(cols, cols), :] = jnp.zeros((cols, LANES), F32)
    taps_sum[:, pl.ds(2 * cols, 8), :] = jnp.zeros((HEADS, 8, LANES), F32)
    half = width // 2
    mine = pl.ds(pl.multiple_of(zbit * half, LANES), half)
    other = pl.ds(pl.multiple_of((1 - zbit) * half, LANES), half)
    stores = [
        pltpu.make_async_copy(src, dst, sems.at[pieces + 5 + n])
        for n, (src, dst) in enumerate(
            (
                (bg_ref.at[:, other], send_hbm),
                (bg_ref.at[:, mine], keep_hbm),
                (out_ref, out_hbm),
            )
        )
    ]
    for store in stores:
        store.start()
    pay_ref[:, HEAD:LANES, :] = taps_sum[...].astype(BF)
    bg = bg_ref[...]
    for h in range(0, HEADS, 2):
        mixed = lax.dot_general(
            weight[h * HEAD : (h + 2) * HEAD, :], bg, (((1,), (1,)), ((), ())),
            preferred_element_type=F32,
        ).astype(BF)
        pay_ref[h, 0:HEAD, :] = mixed[0:HEAD]
        pay_ref[h + 1, 0:HEAD, :] = mixed[HEAD : 2 * HEAD]
        if h % 4 == 2:
            at = pl.ds(h - 2, 4)
            store = pltpu.make_async_copy(
                pay_ref.at[at], pay_hbm.at[at], sems.at[pieces + 8 + h // 4]
            )
            store.start()
            stores.append(store)
    for store in stores:
        store.wait()


def conv(info, att, res, cot, left, right, w, taps):
    rows, width = res.shape
    cols = width // LANES
    span = rows + 2 * HALO
    vm = pl.BlockSpec()
    return pl.pallas_call(
        conv_kernel_body,
        out_shape=(
            pltpu.HBM((rows, width), BF),
            pltpu.HBM((HEADS, LANES, LANES), BF),
            pltpu.HBM((rows, width // 2), BF),
            pltpu.HBM((rows, width // 2), BF),
        ),
        in_specs=[pl.BlockSpec(memory_space=pltpu.SMEM)]
        + [vm]
        + [pl.BlockSpec(memory_space=pl.ANY)] * 6,
        out_specs=(
            pl.BlockSpec(memory_space=pl.ANY),
        )
        * 4,
        scratch_shapes=[
            pltpu.VMEM((span, width), BF),
            pltpu.VMEM((cols, span, LANES), F32),
            pltpu.VMEM((cols, span, LANES), F32),
            pltpu.VMEM((cols, rows + 32, LANES), F32),
            pltpu.VMEM((rows + 32, LANES), F32),
            pltpu.VMEM((HEADS, 32, LANES), F32),
            pltpu.VMEM((rows, width), BF),
            pltpu.VMEM((rows, width), BF),
            pltpu.VMEM((rows, width), BF),
            pltpu.VMEM((HALO + NEAR, width), BF),
            pltpu.VMEM((HALO + NEAR, width), BF),
            pltpu.VMEM((width, width), BF),
            pltpu.VMEM((TAPS, width), F32),
            pltpu.VMEM((span, 2 * LANES), F32),
            pltpu.VMEM((rows, width), BF),
            pltpu.VMEM((HEADS, LANES, LANES), BF),
            pltpu.SemaphoreType.DMA((cols // 2 + 12,)),
        ],
        compiler_params=params(20),
        cost_estimate=cost(9e9, 1e7),
        name="convolve",
    )(info, att, res, cot, left, right, w, taps)


def outer_kernel(info_ref, *refs):
    o_ref = refs[-1]
    core = info_ref[2]
    tall, wide = refs[0:4], refs[4:8]
    part = wide[0].shape[1] // 2
    at = pl.ds(pl.multiple_of(core * part, LANES), part)
    rhs = jnp.concatenate([ref[:, at] for ref in wide], axis=0)
    for h in range(0, HEADS, 4):
        lhs = jnp.concatenate(
            [
                jnp.concatenate([ref[g, 0:HEAD, :] for ref in tall], axis=1)
                for g in range(h, h + 4)
            ],
            axis=0,
        )
        full = dot(lhs, rhs).astype(BF)
        for g in range(4):
            for c in range(part // LANES):
                o_ref[h + g, c * HEAD : (c + 1) * HEAD, :] = full[
                    g * HEAD : (g + 1) * HEAD, c * LANES : (c + 1) * LANES
                ]


def outer(info, tall, wide):
    part = wide[0].shape[1] // 2
    return pl.pallas_call(
        outer_kernel,
        out_shape=pltpu.HBM((HEADS, part // LANES * HEAD + 32, LANES), BF),
        in_specs=[pl.BlockSpec(memory_space=pltpu.SMEM)] + [pl.BlockSpec()] * 8,
        compiler_params=params(20),
        cost_estimate=cost(1e9, 4e6),
        name="outer",
    )(info, *tall, *wide)


def tail_kernel(g_ref, w_ref, o_ref, taps, sems):
    taps[...] = jnp.sum(g_ref[:, HEAD:LANES, :].astype(F32), axis=0).astype(BF)
    base = o_ref.shape[1] - 32
    copies = [
        pltpu.make_async_copy(taps, o_ref.at[h, pl.ds(base, 32), :], sems.at[h])
        for h in range(HEADS)
    ]
    for copy in copies:
        copy.start()
    for copy in copies:
        copy.wait()


def tail(g, w):
    return pl.pallas_call(
        tail_kernel,
        out_shape=pltpu.HBM(w.shape, BF),
        in_specs=[pl.BlockSpec(), pl.BlockSpec(memory_space=pl.ANY)],
        out_specs=pl.BlockSpec(memory_space=pl.ANY),
        scratch_shapes=[pltpu.VMEM((32, LANES), BF), pltpu.SemaphoreType.DMA((HEADS,))],
        input_output_aliases={1: 0},
        compiler_params=params(8),
        cost_estimate=cost(1e6, 1e6),
        name="tail",
    )(g, w)


def bwd_kernel(x_ref, g_ref, e_ref, o_ref, inv_ref, pay_ref, vaug, kt, dk, dv):
    step = pl.program_id(0)
    blocks = x_ref.shape[0]
    scale = 1.0 / math.sqrt(HEAD)

    @pl.when(step == 0)
    def _():
        ones = jnp.where(row_iota((32, LANES)) < 3, 1.0, 0.0).astype(BF)
        for j in range(blocks):
            rows = pl.ds(j * LANES, LANES)
            turned = jnp.concatenate([x_ref[j, 2 * HEAD : 3 * HEAD, :], ones], axis=0).T
            vaug[rows, 0:LANES] = turned
            vaug[rows, LANES : 2 * LANES] = turned
            kt[:, rows] = x_ref[j, HEAD : 2 * HEAD, :]
        dk[...] = jnp.zeros_like(dk)
        dv[...] = jnp.zeros_like(dv)

    per = QT // LANES
    gt = jnp.concatenate([g_ref[step * per + p, 0:HEAD, :] for p in range(per)], axis=1).astype(F32)
    qt = jnp.concatenate([x_ref[step * per + p, 0:HEAD, :] for p in range(per)], axis=1)
    inv = inv_ref[0:1, :]
    centre = jnp.sum(gt * o_ref[...], axis=0, keepdims=True)
    ginv = gt * inv
    sg = ginv * scale
    hi = sg.astype(BF)
    lo = (sg - hi.astype(F32)).astype(BF)
    rest = centre * inv * (-scale)
    c0 = rest.astype(BF).astype(F32)
    c1 = (rest - c0).astype(BF).astype(F32)
    c2 = rest - c0 - c1
    at = row_iota((32, QT))
    crows = jnp.where(at == 0, c0, jnp.where(at == 1, c1, jnp.where(at == 2, c2, 0.0))).astype(BF)
    zeros = jnp.zeros((32, QT), BF)
    gaug = jnp.concatenate([hi, crows, lo, zeros], axis=0)
    gn = jnp.concatenate([ginv.astype(BF), zeros], axis=0).T
    qn = jnp.concatenate([qt, zeros], axis=0).T
    dq = jnp.zeros((HEAD, QT), F32)
    for t in range(kt.shape[1] // KT):
        rows = slice(t * KT, (t + 1) * KT)
        slope = dot(vaug[rows, :], gaug)
        e = e_ref[0, rows, :]
        ds = (e.astype(F32) * slope).astype(BF)
        dv[rows, :] += dot(e, gn)
        dk[rows, :] += dot(ds, qn)
        dq = dq + dot(kt[:, rows], ds)
    dq = dq.astype(BF)
    for p in range(per):
        pay_ref[step * per + p, 0:HEAD, :] = dq[:, p * LANES : (p + 1) * LANES]

    @pl.when(step == pl.num_programs(0) - 1)
    def _():
        for j in range(blocks):
            rows = pl.ds(j * LANES, LANES)
            pay_ref[j, HEAD : 2 * HEAD, :] = dk[rows, :].T[0:HEAD].astype(BF)
            pay_ref[j, 2 * HEAD : 3 * HEAD, :] = dv[rows, :].T[0:HEAD].astype(BF)


def bwd(x, g, e, o, inv):
    blocks = x.shape[0]
    frames = blocks * LANES
    steps = frames // QT
    return pl.pallas_call(
        bwd_kernel,
        grid=(steps,),
        out_shape=pltpu.HBM((blocks, 3 * HEAD, LANES), BF),
        in_specs=[
            pl.BlockSpec((blocks, 3 * HEAD, LANES), lambda i: (0, 0, 0)),
            pl.BlockSpec((blocks, LANES, LANES), lambda i: (0, 0, 0)),
            pl.BlockSpec((1, frames, QT), lambda i: (i, 0, 0)),
            pl.BlockSpec((HEAD, QT), lambda i: (0, i)),
            pl.BlockSpec((8, QT), lambda i: (0, i)),
        ],
        out_specs=pl.BlockSpec((blocks, 3 * HEAD, LANES), lambda i: (0, 0, 0)),
        scratch_shapes=[
            pltpu.VMEM((frames, 2 * LANES), BF),
            pltpu.VMEM((HEAD, frames), BF),
            pltpu.VMEM((frames, LANES), F32),
            pltpu.VMEM((frames, LANES), F32),
        ],
        compiler_params=params(30),
        cost_estimate=cost(2e10, 1e7),
        name="attend_back",
    )(x, g, e, o, inv)


def post_kernel(x_ref, q_ref, k_ref, v_ref):
    for part, ref in enumerate((q_ref, k_ref, v_ref)):
        rows = slice(part * HEAD, (part + 1) * HEAD)
        ref[...] = jnp.concatenate([x_ref[h, rows, :] for h in range(HEADS)], axis=0).T


def post(x):
    shape = jax.ShapeDtypeStruct((LANES, HEADS * HEAD), BF)
    return pl.pallas_call(
        post_kernel,
        out_shape=(shape,) * 3,
        compiler_params=params(12),
        cost_estimate=cost(1e6, 3e6),
        name="post",
    )(x)


GROUP = 8
PIECE = 120


def pack_kernel(info_ref, x_ref, *refs):
    outs, buf = refs[:-1], refs[-1]
    cols = x_ref.shape[1] // HEAD
    below = cols * HEAD
    for r in range(HEAD // 16):
        for c in range(2 * cols):
            at = (c % cols) * HEAD + 16 * r
            tiles = [x_ref[2 * i + c // cols, at : at + 16, :].astype(F32) for i in range(HEADS // 2)]
            both = sum(tiles[1:], tiles[0])
            for e in range(2):
                n = (2 * r + e) * 2 * cols + c
                buf[8 * n : 8 * n + 8, :] = both[8 * e : 8 * e + 8, :]
    share = buf.shape[0] // GROUP
    for k in range(GROUP):
        j = jnp.bitwise_xor(info_ref[4], k)
        taps = [x_ref[2 * j + e, below : below + 32, :].astype(F32)[0:24] for e in range(2)]
        outs[k // 2][k % 2] = jnp.concatenate(
            [buf[pl.ds(pl.multiple_of(share * j, 8), share), :]] + taps, axis=0
        ).astype(BF)


def pack(info, x):
    units = x.shape[1] // HEAD * HEAD * 2
    return pl.pallas_call(
        pack_kernel,
        out_shape=(pltpu.HBM((2, PIECE, LANES), BF),) * (GROUP // 2),
        in_specs=[pl.BlockSpec(memory_space=pltpu.SMEM), pl.BlockSpec()],
        scratch_shapes=[pltpu.VMEM((units, LANES), F32)],
        compiler_params=params(12),
        cost_estimate=cost(1e6, 3e6),
        name="pack",
    )(info, x)


def merge_kernel(*refs):
    keep_ref, send_ref = refs[-2:]
    both = sum([ref[...].astype(F32) for ref in refs[1:-2]], refs[0][...].astype(F32))
    keep_ref[...] = both[0].astype(BF)
    send_ref[...] = both[1].astype(BF)


def merge(xs):
    return pl.pallas_call(
        merge_kernel,
        out_shape=(pltpu.HBM(xs[0].shape[1:], BF),) * 2,
        compiler_params=params(8),
        cost_estimate=cost(1e6, 1e6),
        name="merge",
    )(*xs)


def total_kernel(*refs):
    o_ref = refs[-1]
    total = sum([ref[...].astype(F32) for ref in refs[1:-1]], refs[0][...].astype(F32))
    total = total * (1.0 / o_ref.shape[0])
    o_ref[...] = jnp.broadcast_to(total.astype(BF)[None], o_ref.shape)


def total(xs, batch):
    return pl.pallas_call(
        total_kernel,
        out_shape=pltpu.HBM((batch,) + xs[0].shape, BF),
        compiler_params=params(12),
        cost_estimate=cost(1e6, 1e6),
        name="total",
    )(*xs)


def unpack_kernel(x_ref, w_ref, k_ref):
    width = w_ref.shape[1]
    cols = width // LANES
    share = HEAD // 8 * cols // 2 // GROUP
    for z in range(2):
        for j in range(GROUP):
            x = x_ref[4 * (j // 2) + 2 * z + j % 2].astype(F32)
            for i in range(share):
                n = j * share + i
                r, c = 8 * (n // (cols // 2)), width // 2 * z + LANES * (n % (cols // 2))
                w_ref[r : r + 8, c : c + LANES] = x[8 * i : 8 * i + 8, :]
    for j in range(GROUP):
        x = x_ref[4 * (j // 2) + j % 2].astype(F32) + x_ref[4 * (j // 2) + 2 + j % 2].astype(F32)
        for i in range(4):
            if 4 * j + i < TAPS:
                for c in range(cols):
                    at = 8 * share + cols * i + c
                    k_ref[4 * j + i : 4 * j + i + 1, c * LANES : (c + 1) * LANES] = x[at : at + 1, :]


def unpack(x, width):
    return pl.pallas_call(
        unpack_kernel,
        out_shape=(
            jax.ShapeDtypeStruct((HEAD, width), F32),
            jax.ShapeDtypeStruct((TAPS, width), F32),
        ),
        compiler_params=params(12),
        cost_estimate=cost(1e6, 1e6),
        name="unpack",
    )(x)


def in_hbm(x):
    return pltpu.with_memory_space_constraint(x, pltpu.HBM)


def exchange(x, axis, groups=None):
    return lax.all_to_all(
        x, axis, split_axis=0, concat_axis=0, tiled=True, axis_index_groups=groups
    )


def shards(query_proj, key_proj, value_proj, residual, lengths, out_weight, conv_kernel, cotangent):
    rows, width = query_proj.shape[1:]
    count = lax.axis_size("seq")
    me = lax.axis_index("seq")
    res, cot = residual[0], cotangent[0]
    up = [(i, i + 1) for i in range(count - 1)]
    down = [(i + 1, i) for i in range(count - 1)]
    cores = [(i, i ^ 1) for i in range(count)]
    batch = lax.axis_size("dp")
    depth = lax.axis_index("dp")
    levels = [(i, i ^ 2) for i in range(batch)]

    def hop(k):
        return [(i, i ^ (4 * (k // 2) + k % 2)) for i in range(batch)]

    query, key, value, res, cot, out_weight, conv_kernel = (
        in_hbm(x)
        for x in (query_proj[0], key_proj[0], value_proj[0], res, cot, out_weight, conv_kernel)
    )
    payload, edge_up, edge_down = pre(query, key, value, res, cot)
    heads = exchange(payload, "seq")
    left = lax.ppermute(edge_up, "seq", up)
    right = lax.ppermute(edge_down, "seq", down)
    heads, left, right = lax.optimization_barrier((heads, left, right))
    weights, mixed, inv, payload = fwd(lengths, heads)
    attended = exchange(payload, "seq")
    own = attended[:, 0:HEAD]
    att_level = lax.ppermute(own, "dp", levels)
    att_core = lax.ppermute(own, "seq", cores)
    member = depth // 4 * 2 + depth % 2
    info = jnp.stack([lengths[0], me * rows, me % 2, depth // 2 % 2, member]).astype(jnp.int32)
    block_out, payload, keep, send = conv(
        info, attended, res, cot, in_hbm(left), in_hbm(right), out_weight, conv_kernel
    )
    att_level, payload = lax.optimization_barrier((att_level, payload))
    att_both = lax.ppermute(att_level, "seq", cores)
    grads = exchange(payload, "seq")
    level = lax.ppermute(send, "dp", levels)
    partner = lax.ppermute(keep, "seq", cores)
    both = lax.ppermute(level, "seq", cores)
    partial = outer(
        info, (own, att_core, att_level, att_both), (in_hbm(keep), partner, level, both)
    )
    partial = exchange(tail(grads, partial), "seq")
    payload = bwd(heads, grads, in_hbm(weights), in_hbm(mixed), inv)
    payload, partial = lax.optimization_barrier((payload, partial))
    back = exchange(payload, "seq")
    packed = pack(info, partial)
    level_parts = [in_hbm(packed[0])] + [
        lax.ppermute(packed[k], "dp", hop(2 * k)) for k in range(1, GROUP // 2)
    ]
    keep, send = merge(level_parts)
    packed = [in_hbm(keep), lax.ppermute(send, "dp", hop(1))]
    summed, back = lax.optimization_barrier((total(packed, batch), back))
    final = exchange(summed, "dp")
    query_grad, key_grad, value_grad = post(back)
    weight_grad, kernel_grad = unpack(final, width)
    return (
        block_out[None],
        query_grad[None],
        key_grad[None],
        value_grad[None],
        weight_grad,
        kernel_grad,
    )


def solution(mesh):
    split = P("dp", "seq", None)
    return jax.shard_map(
        shards,
        mesh=mesh,
        in_specs=(split, split, split, split, P("dp"), P(), P(), split),
        out_specs=(split, split, split, split, P("seq", None), P()),
        check_vma=False,
    )
```

```python
import math

import jax
import jax.numpy as jnp
from jax import lax
from jax.experimental import pallas as pl
from jax.experimental.pallas import tpu as pltpu
from jax.sharding import PartitionSpec as P

HEADS = 16
HEAD = 96
LANES = 128
TAPS = 31
HALF = 15
HALO = 32
NEAR = 16
QT = 512
KT = 256
BF = jnp.bfloat16
F32 = jnp.float32
MIB = 2**20


def params(mib):
    return pltpu.CompilerParams(vmem_limit_bytes=mib * MIB)


def cost(flops, moved):
    return pl.CostEstimate(flops=int(flops), bytes_accessed=int(moved), transcendentals=0)


def lane_iota(shape):
    return lax.broadcasted_iota(jnp.int32, shape, len(shape) - 1)


def row_iota(shape):
    return lax.broadcasted_iota(jnp.int32, shape, 0)


def dot(a, b):
    return jnp.dot(a, b, preferred_element_type=F32)


def pre_kernel(q_hbm, k_hbm, v_hbm, res_hbm, cot_hbm, o_ref, up_ref, down_ref, buf, sems):
    rows = q_hbm.shape[0]
    loads = [
        pltpu.make_async_copy(ref, buf.at[i], sems.at[i])
        for i, ref in enumerate((q_hbm, k_hbm, v_hbm))
    ]
    edges = [
        pltpu.make_async_copy(ref.at[pl.ds(lo, size)], out.at[pl.ds(at, size)], sems.at[n])
        for n, ref, lo, size, out, at in (
            (3, res_hbm, rows - HALO, HALO, up_ref, 0),
            (4, cot_hbm, rows - NEAR, NEAR, up_ref, HALO),
            (5, res_hbm, 0, HALO, down_ref, 0),
            (6, cot_hbm, 0, NEAR, down_ref, HALO),
        )
    ]
    for copy in loads + edges:
        copy.start()
    for part, copy in enumerate(loads):
        copy.wait()
        turned = buf[part].T
        for h in range(HEADS):
            o_ref[h, part * HEAD : (part + 1) * HEAD, :] = turned[h * HEAD : (h + 1) * HEAD, :]
    for copy in edges:
        copy.wait()


def pre(q, k, v, res, cot):
    edge = jax.ShapeDtypeStruct((HALO + NEAR, q.shape[1]), BF)
    return pl.pallas_call(
        pre_kernel,
        out_shape=(jax.ShapeDtypeStruct((HEADS, 3 * HEAD, LANES), BF), edge, edge),
        in_specs=[pl.BlockSpec(memory_space=pltpu.HBM)] * 5,
        scratch_shapes=[pltpu.VMEM((3,) + q.shape, BF), pltpu.SemaphoreType.DMA((7,))],
        compiler_params=params(8),
        cost_estimate=cost(1e6, 3e6),
        name="pre",
    )(q, k, v, res, cot)


def fwd_kernel(len_ref, x_ref, e_hbm, o_ref, inv_ref, pay_ref, kaug, vaug, even, odd, ebuf, sems):
    blocks = x_ref.shape[0]
    frames = blocks * LANES
    scale = math.log2(math.e) / math.sqrt(HEAD)
    length = len_ref[0]
    for j in range(blocks):
        rows = slice(j * LANES, (j + 1) * LANES)
        bias = jnp.where(j * LANES + lane_iota((32, LANES)) < length, 0.0, -1e30)
        bias = jnp.where(row_iota((32, LANES)) == 0, bias, 0.0)
        turned = jnp.concatenate([x_ref[j, HEAD : 2 * HEAD, :], bias.astype(BF)], axis=0).T
        kaug[rows, 0:LANES] = turned
        kaug[rows, LANES : 2 * LANES] = turned
        vaug[0:HEAD, rows] = x_ref[j, 2 * HEAD : 3 * HEAD, :]
        vaug[HEAD : HEAD + 16, rows] = jnp.where(row_iota((16, LANES)) == 0, 1.0, 0.0).astype(BF)
    per = QT // LANES
    count = frames // QT
    tiles = frames // KT
    one = jnp.where(row_iota((32, QT)) == 0, 1.0, 0.0).astype(BF)

    def queries(i):
        qt = jnp.concatenate([x_ref[i * per + p, 0:HEAD, :] for p in range(per)], axis=1)
        qs = qt.astype(F32) * scale
        hi = qs.astype(BF)
        lo = (qs - hi.astype(F32)).astype(BF)
        return jnp.concatenate([hi, one, lo, jnp.zeros((32, QT), BF)], axis=0)

    def score(buf, t, qaug, top):
        s = dot(kaug[t * KT : (t + 1) * KT, :], qaug)
        buf[t * KT : (t + 1) * KT, :] = s
        part = jnp.max(s.reshape(KT // 8, 8, QT), axis=0)
        return part if top is None else jnp.maximum(top, part)

    def out_copy(i, t):
        at = pl.ds(t * KT, 2 * KT)
        return pltpu.make_async_copy(ebuf.at[i, at], e_hbm.at[i, at], sems.at[i, t // 2])

    bufs = (even, odd)
    top = None
    qaug = queries(0)
    for t in range(tiles):
        top = score(bufs[0], t, qaug, top)
    for i in range(count):
        peak = jnp.max(top, axis=0, keepdims=True)
        top = None
        if i + 1 < count:
            qaug = queries(i + 1)
        acc = jnp.zeros((HEAD + 16, QT), F32)
        for t in range(tiles):
            rows = slice(t * KT, (t + 1) * KT)
            if i + 1 < count:
                top = score(bufs[(i + 1) % 2], t, qaug, top)
            e = jnp.exp2(bufs[i % 2][rows, :] - peak).astype(BF)
            ebuf[i, rows, :] = e
            acc = acc + dot(vaug[:, rows], e)
            if t % 2 == 1:
                out_copy(i, t - 1).start()
        inv = 1.0 / acc[HEAD : HEAD + 1, :]
        out = acc[0:HEAD, :] * inv
        at = slice(i * QT, (i + 1) * QT)
        o_ref[:, at] = out
        inv_ref[:, at] = jnp.broadcast_to(inv, (8, QT))
        rounded = out.astype(BF)
        for p in range(per):
            pay_ref[i * per + p, 0:HEAD, :] = rounded[:, p * LANES : (p + 1) * LANES]
    low = HEAD // 2
    lane = lane_iota((low, LANES))
    left = lane < LANES // 2
    outer_lanes = jnp.logical_or(lane < HALO, lane >= LANES - HALO)
    for j in range(blocks):
        after = pay_ref[min(j + 1, blocks - 1), 0:HEAD, :].astype(F32)
        before = pay_ref[max(j - 1, 0), 0:HEAD, :].astype(F32)
        first = jnp.where(left, after[0:low], before[0:low])
        second = jnp.where(left, after[low:HEAD], before[low:HEAD])
        second = pltpu.roll(second, LANES // 2, 1)
        pay_ref[j, HEAD : HEAD + low, :] = jnp.where(outer_lanes, first, second).astype(BF)
    for i in range(count):
        for t in range(0, tiles, 2):
            out_copy(i, t).wait()


def fwd(length, x):
    blocks = x.shape[0]
    frames = blocks * LANES
    steps = frames // QT
    return pl.pallas_call(
        fwd_kernel,
        out_shape=(
            pltpu.HBM((steps, frames, QT), BF),
            pltpu.HBM((HEAD, frames), F32),
            jax.ShapeDtypeStruct((8, frames), F32),
            jax.ShapeDtypeStruct((blocks, HEAD + HEAD // 2, LANES), BF),
        ),
        in_specs=[pl.BlockSpec(memory_space=pltpu.SMEM), pl.BlockSpec()],
        out_specs=(
            pl.BlockSpec(memory_space=pl.ANY),
            pl.BlockSpec(),
            pl.BlockSpec(),
            pl.BlockSpec(),
        ),
        scratch_shapes=[
            pltpu.VMEM((frames, 2 * LANES), BF),
            pltpu.VMEM((HEAD + 16, frames), BF),
            pltpu.VMEM((frames, QT), F32),
            pltpu.VMEM((frames, QT), F32),
            pltpu.VMEM((steps, frames, QT), BF),
            pltpu.SemaphoreType.DMA((steps, frames // KT // 2)),
        ],
        compiler_params=params(30),
        cost_estimate=cost(9e9, 1e7),
        name="attend",
    )(length, x)


def conv_kernel_body(
    info_ref, att_ref, res_hbm, cot_hbm, left_hbm, right_hbm, w_hbm, taps_hbm,
    out_hbm, pay_hbm, keep_hbm, send_hbm,
    lhs, block_in, masked, cot, grad, taps_sum, bg_ref,
    res_ref, cot_ref, left_ref, right_ref, weight, taps_ref, proj, out_ref, pay_ref, sems,
):
    rows, width = res_ref.shape
    cols = width // LANES
    span = rows + 2 * HALO
    length = info_ref[0]
    first = info_ref[1]
    zbit = info_ref[3]
    pieces = cols // 2
    wide = 2 * LANES

    def chunk(n):
        at = pl.ds(pl.multiple_of(n * wide, wide), wide)
        return pltpu.make_async_copy(w_hbm.at[:, at], weight.at[:, at], sems.at[n])

    small = [
        pltpu.make_async_copy(src, dst, sems.at[pieces + n])
        for n, (src, dst) in enumerate(
            (
                (res_hbm, res_ref),
                (cot_hbm, cot_ref),
                (left_hbm, left_ref),
                (right_hbm, right_ref),
                (taps_hbm, taps_ref),
            )
        )
    ]
    chunk(0).start()
    for load in small:
        load.start()
    for n in range(1, pieces):
        chunk(n).start()
    main = jnp.concatenate([att_ref[h, 0:HEAD, :] for h in range(HEADS)], axis=0)
    packed = [att_ref[h, HEAD : HEAD + HEAD // 2, :].astype(F32) for h in range(HEADS)]
    halo = jnp.concatenate(
        [part for p in packed for part in (p, pltpu.roll(p, LANES // 2, 1))], axis=0
    ).astype(BF)
    halo = halo.T
    lhs[0:HALO, :] = halo[LANES - HALO : LANES, :]
    lhs[HALO : HALO + rows, :] = main.T
    lhs[HALO + rows : span, :] = halo[0:HALO, :]
    frame = first - HALO + row_iota((span, LANES))
    valid = jnp.logical_and(frame >= 0, frame < length)
    mid = rows + 32

    def project(n):
        at = pl.ds(pl.multiple_of(n * wide, wide), wide)
        proj[...] = dot(lhs[...], weight[:, at])

    def place(n):
        for m in range(2):
            c = 2 * n + m
            at = pl.ds(pl.multiple_of(c * LANES, LANES), LANES)
            res = jnp.concatenate(
                [left_ref[0:HALO, at], res_ref[:, at], right_ref[0:HALO, at]], axis=0
            ).astype(F32)
            block = res + proj[:, m * LANES : (m + 1) * LANES]
            block_in[c] = block
            masked[c] = jnp.where(valid, block, 0.0).astype(BF).astype(F32)
            cot[c] = jnp.concatenate(
                [
                    left_ref[HALO : HALO + NEAR, at],
                    cot_ref[:, at],
                    right_ref[HALO : HALO + NEAR, at],
                ],
                axis=0,
            ).astype(F32)

    for load in small:
        load.wait()
    chunk(0).wait()
    project(0)
    place(0)

    def channels(c):
        at = pl.ds(pl.multiple_of(c * LANES, LANES), LANES)
        acc = jnp.zeros((mid, LANES), F32)
        for r in range(TAPS):
            acc = acc + taps_ref[r : r + 1, at] * masked[c, 1 + r : 1 + r + mid, :]
        gate = jax.nn.sigmoid(acc)
        cg = (cot[c] * (gate * (1.0 + acc * (1.0 - gate)))).astype(BF).astype(F32)
        grad[...] = cg
        out_ref[:, at] = (
            block_in[c, HALO : HALO + rows, :] + (acc * gate)[16 : 16 + rows, :]
        ).astype(BF)
        own = cg[16 : 16 + rows, :]
        back = jnp.zeros((rows, LANES), F32)
        for r in range(TAPS):
            back = back + taps_ref[r : r + 1, at] * grad[31 - r : 31 - r + rows, :]
            prod = own * masked[c, 17 + r : 17 + r + rows, :]
            prod = jnp.sum(prod.reshape(rows // 8, 8, LANES), axis=0)
            taps_sum[r // 2, pl.ds((r % 2) * cols + c, 1), :] = jnp.sum(prod, axis=0, keepdims=True)
        own_valid = valid[HALO : HALO + rows, :]
        bg_ref[:, at] = (cot[c, 16 : 16 + rows, :] + jnp.where(own_valid, back, 0.0)).astype(BF)

    @pl.loop(0, pieces)
    def _(n):
        @pl.when(n < pieces - 1)
        def _():
            chunk(n + 1).wait()

        after = lax.rem(n + 1, pieces)
        project(after)
        channels(2 * n)
        channels(2 * n + 1)
        place(after)

    taps_sum[HEADS - 1, pl.ds(cols, cols), :] = jnp.zeros((cols, LANES), F32)
    taps_sum[:, pl.ds(2 * cols, 8), :] = jnp.zeros((HEADS, 8, LANES), F32)
    half = width // 2
    mine = pl.ds(pl.multiple_of(zbit * half, LANES), half)
    other = pl.ds(pl.multiple_of((1 - zbit) * half, LANES), half)
    stores = [
        pltpu.make_async_copy(src, dst, sems.at[pieces + 5 + n])
        for n, (src, dst) in enumerate(
            (
                (bg_ref.at[:, other], send_hbm),
                (bg_ref.at[:, mine], keep_hbm),
                (out_ref, out_hbm),
            )
        )
    ]
    for store in stores:
        store.start()
    pay_ref[:, HEAD:LANES, :] = taps_sum[...].astype(BF)
    bg = bg_ref[...]
    for h in range(0, HEADS, 2):
        mixed = lax.dot_general(
            weight[h * HEAD : (h + 2) * HEAD, :], bg, (((1,), (1,)), ((), ())),
            preferred_element_type=F32,
        ).astype(BF)
        pay_ref[h, 0:HEAD, :] = mixed[0:HEAD]
        pay_ref[h + 1, 0:HEAD, :] = mixed[HEAD : 2 * HEAD]
        if h % 4 == 2:
            at = pl.ds(h - 2, 4)
            store = pltpu.make_async_copy(
                pay_ref.at[at], pay_hbm.at[at], sems.at[pieces + 8 + h // 4]
            )
            store.start()
            stores.append(store)
    for store in stores:
        store.wait()


def conv(info, att, res, cot, left, right, w, taps):
    rows, width = res.shape
    cols = width // LANES
    span = rows + 2 * HALO
    vm = pl.BlockSpec()
    return pl.pallas_call(
        conv_kernel_body,
        out_shape=(
            pltpu.HBM((rows, width), BF),
            pltpu.HBM((HEADS, LANES, LANES), BF),
            pltpu.HBM((rows, width // 2), BF),
            pltpu.HBM((rows, width // 2), BF),
        ),
        in_specs=[pl.BlockSpec(memory_space=pltpu.SMEM)]
        + [vm]
        + [pl.BlockSpec(memory_space=pl.ANY)] * 6,
        out_specs=(
            pl.BlockSpec(memory_space=pl.ANY),
        )
        * 4,
        scratch_shapes=[
            pltpu.VMEM((span, width), BF),
            pltpu.VMEM((cols, span, LANES), F32),
            pltpu.VMEM((cols, span, LANES), F32),
            pltpu.VMEM((cols, rows + 32, LANES), F32),
            pltpu.VMEM((rows + 32, LANES), F32),
            pltpu.VMEM((HEADS, 32, LANES), F32),
            pltpu.VMEM((rows, width), BF),
            pltpu.VMEM((rows, width), BF),
            pltpu.VMEM((rows, width), BF),
            pltpu.VMEM((HALO + NEAR, width), BF),
            pltpu.VMEM((HALO + NEAR, width), BF),
            pltpu.VMEM((width, width), BF),
            pltpu.VMEM((TAPS, width), F32),
            pltpu.VMEM((span, 2 * LANES), F32),
            pltpu.VMEM((rows, width), BF),
            pltpu.VMEM((HEADS, LANES, LANES), BF),
            pltpu.SemaphoreType.DMA((cols // 2 + 12,)),
        ],
        compiler_params=params(20),
        cost_estimate=cost(9e9, 1e7),
        name="convolve",
    )(info, att, res, cot, left, right, w, taps)


def outer_kernel(info_ref, *refs):
    o_ref = refs[-1]
    core = info_ref[2]
    tall, wide = refs[0:4], refs[4:8]
    part = wide[0].shape[1] // 2
    at = pl.ds(pl.multiple_of(core * part, LANES), part)
    rhs = jnp.concatenate([ref[:, at] for ref in wide], axis=0)
    for h in range(0, HEADS, 4):
        lhs = jnp.concatenate(
            [
                jnp.concatenate([ref[g, 0:HEAD, :] for ref in tall], axis=1)
                for g in range(h, h + 4)
            ],
            axis=0,
        )
        full = dot(lhs, rhs).astype(BF)
        for g in range(4):
            for c in range(part // LANES):
                o_ref[h + g, c * HEAD : (c + 1) * HEAD, :] = full[
                    g * HEAD : (g + 1) * HEAD, c * LANES : (c + 1) * LANES
                ]


def outer(info, tall, wide):
    part = wide[0].shape[1] // 2
    return pl.pallas_call(
        outer_kernel,
        out_shape=pltpu.HBM((HEADS, part // LANES * HEAD + 32, LANES), BF),
        in_specs=[pl.BlockSpec(memory_space=pltpu.SMEM)] + [pl.BlockSpec()] * 8,
        compiler_params=params(20),
        cost_estimate=cost(1e9, 4e6),
        name="outer",
    )(info, *tall, *wide)


def tail_kernel(g_ref, w_ref, o_ref, taps, sems):
    taps[...] = jnp.sum(g_ref[:, HEAD:LANES, :].astype(F32), axis=0).astype(BF)
    base = o_ref.shape[1] - 32
    copies = [
        pltpu.make_async_copy(taps, o_ref.at[h, pl.ds(base, 32), :], sems.at[h])
        for h in range(HEADS)
    ]
    for copy in copies:
        copy.start()
    for copy in copies:
        copy.wait()


def tail(g, w):
    return pl.pallas_call(
        tail_kernel,
        out_shape=pltpu.HBM(w.shape, BF),
        in_specs=[pl.BlockSpec(), pl.BlockSpec(memory_space=pl.ANY)],
        out_specs=pl.BlockSpec(memory_space=pl.ANY),
        scratch_shapes=[pltpu.VMEM((32, LANES), BF), pltpu.SemaphoreType.DMA((HEADS,))],
        input_output_aliases={1: 0},
        compiler_params=params(8),
        cost_estimate=cost(1e6, 1e6),
        name="tail",
    )(g, w)


def bwd_kernel(x_ref, g_ref, e_ref, o_ref, inv_ref, pay_ref, vaug, kt, dk, dv):
    step = pl.program_id(0)
    blocks = x_ref.shape[0]
    scale = 1.0 / math.sqrt(HEAD)

    @pl.when(step == 0)
    def _():
        ones = jnp.where(row_iota((32, LANES)) < 3, 1.0, 0.0).astype(BF)
        for j in range(blocks):
            rows = pl.ds(j * LANES, LANES)
            turned = jnp.concatenate([x_ref[j, 2 * HEAD : 3 * HEAD, :], ones], axis=0).T
            vaug[rows, 0:LANES] = turned
            vaug[rows, LANES : 2 * LANES] = turned
            kt[:, rows] = x_ref[j, HEAD : 2 * HEAD, :]
        dk[...] = jnp.zeros_like(dk)
        dv[...] = jnp.zeros_like(dv)

    per = QT // LANES
    gt = jnp.concatenate([g_ref[step * per + p, 0:HEAD, :] for p in range(per)], axis=1).astype(F32)
    qt = jnp.concatenate([x_ref[step * per + p, 0:HEAD, :] for p in range(per)], axis=1)
    inv = inv_ref[0:1, :]
    centre = jnp.sum(gt * o_ref[...], axis=0, keepdims=True)
    ginv = gt * inv
    sg = ginv * scale
    hi = sg.astype(BF)
    lo = (sg - hi.astype(F32)).astype(BF)
    rest = centre * inv * (-scale)
    c0 = rest.astype(BF).astype(F32)
    c1 = (rest - c0).astype(BF).astype(F32)
    c2 = rest - c0 - c1
    at = row_iota((32, QT))
    crows = jnp.where(at == 0, c0, jnp.where(at == 1, c1, jnp.where(at == 2, c2, 0.0))).astype(BF)
    zeros = jnp.zeros((32, QT), BF)
    gaug = jnp.concatenate([hi, crows, lo, zeros], axis=0)
    gn = jnp.concatenate([ginv.astype(BF), zeros], axis=0).T
    qn = jnp.concatenate([qt, zeros], axis=0).T
    dq = jnp.zeros((HEAD, QT), F32)
    for t in range(kt.shape[1] // KT):
        rows = slice(t * KT, (t + 1) * KT)
        slope = dot(vaug[rows, :], gaug)
        e = e_ref[0, rows, :]
        ds = (e.astype(F32) * slope).astype(BF)
        dv[rows, :] += dot(e, gn)
        dk[rows, :] += dot(ds, qn)
        dq = dq + dot(kt[:, rows], ds)
    dq = dq.astype(BF)
    for p in range(per):
        pay_ref[step * per + p, 0:HEAD, :] = dq[:, p * LANES : (p + 1) * LANES]

    @pl.when(step == pl.num_programs(0) - 1)
    def _():
        for j in range(blocks):
            rows = pl.ds(j * LANES, LANES)
            pay_ref[j, HEAD : 2 * HEAD, :] = dk[rows, :].T[0:HEAD].astype(BF)
            pay_ref[j, 2 * HEAD : 3 * HEAD, :] = dv[rows, :].T[0:HEAD].astype(BF)


def bwd(x, g, e, o, inv):
    blocks = x.shape[0]
    frames = blocks * LANES
    steps = frames // QT
    return pl.pallas_call(
        bwd_kernel,
        grid=(steps,),
        out_shape=pltpu.HBM((blocks, 3 * HEAD, LANES), BF),
        in_specs=[
            pl.BlockSpec((blocks, 3 * HEAD, LANES), lambda i: (0, 0, 0)),
            pl.BlockSpec((blocks, LANES, LANES), lambda i: (0, 0, 0)),
            pl.BlockSpec((1, frames, QT), lambda i: (i, 0, 0)),
            pl.BlockSpec((HEAD, QT), lambda i: (0, i)),
            pl.BlockSpec((8, QT), lambda i: (0, i)),
        ],
        out_specs=pl.BlockSpec((blocks, 3 * HEAD, LANES), lambda i: (0, 0, 0)),
        scratch_shapes=[
            pltpu.VMEM((frames, 2 * LANES), BF),
            pltpu.VMEM((HEAD, frames), BF),
            pltpu.VMEM((frames, LANES), F32),
            pltpu.VMEM((frames, LANES), F32),
        ],
        compiler_params=params(30),
        cost_estimate=cost(2e10, 1e7),
        name="attend_back",
    )(x, g, e, o, inv)


def post_kernel(x_ref, q_ref, k_ref, v_ref):
    for part, ref in enumerate((q_ref, k_ref, v_ref)):
        rows = slice(part * HEAD, (part + 1) * HEAD)
        ref[...] = jnp.concatenate([x_ref[h, rows, :] for h in range(HEADS)], axis=0).T


def post(x):
    shape = jax.ShapeDtypeStruct((LANES, HEADS * HEAD), BF)
    return pl.pallas_call(
        post_kernel,
        out_shape=(shape,) * 3,
        compiler_params=params(12),
        cost_estimate=cost(1e6, 3e6),
        name="post",
    )(x)


GROUP = 8
PIECE = 120


def pack_kernel(info_ref, x_ref, *refs):
    outs, buf = refs[:-1], refs[-1]
    cols = x_ref.shape[1] // HEAD
    below = cols * HEAD
    for r in range(HEAD // 16):
        for c in range(2 * cols):
            at = (c % cols) * HEAD + 16 * r
            tiles = [x_ref[2 * i + c // cols, at : at + 16, :].astype(F32) for i in range(HEADS // 2)]
            both = sum(tiles[1:], tiles[0])
            for e in range(2):
                n = (2 * r + e) * 2 * cols + c
                buf[8 * n : 8 * n + 8, :] = both[8 * e : 8 * e + 8, :]
    share = buf.shape[0] // GROUP
    for k in range(GROUP):
        j = 2 * jnp.bitwise_xor(info_ref[4], k // 2) + k % 2
        taps = [x_ref[2 * j + e, below : below + 32, :].astype(F32)[0:24] for e in range(2)]
        outs[k // 2][k % 2] = jnp.concatenate(
            [buf[pl.ds(pl.multiple_of(share * j, 8), share), :]] + taps, axis=0
        ).astype(BF)


def pack(info, x):
    units = x.shape[1] // HEAD * HEAD * 2
    return pl.pallas_call(
        pack_kernel,
        out_shape=(pltpu.HBM((2, PIECE, LANES), BF),) * (GROUP // 2),
        in_specs=[pl.BlockSpec(memory_space=pltpu.SMEM), pl.BlockSpec()],
        scratch_shapes=[pltpu.VMEM((units, LANES), F32)],
        compiler_params=params(12),
        cost_estimate=cost(1e6, 3e6),
        name="pack",
    )(info, x)


def merge_kernel(*refs):
    o_ref = refs[-1]
    both = sum([ref[...].astype(F32) for ref in refs[1:-1]], refs[0][...].astype(F32))
    o_ref[...] = both.astype(BF)


def merge(xs):
    return pl.pallas_call(
        merge_kernel,
        out_shape=pltpu.HBM(xs[0].shape, BF),
        compiler_params=params(8),
        cost_estimate=cost(1e6, 1e6),
        name="merge",
    )(*xs)


def total_kernel(a_ref, b_ref, o_ref):
    both = (a_ref[...].astype(F32) + b_ref[...].astype(F32)) * (0.5 / o_ref.shape[0])
    o_ref[...] = jnp.broadcast_to(both.astype(BF)[None], o_ref.shape)


def total(a, b):
    return pl.pallas_call(
        total_kernel,
        out_shape=pltpu.HBM((GROUP,) + a.shape, BF),
        compiler_params=params(12),
        cost_estimate=cost(1e6, 1e6),
        name="total",
    )(a, b)


def unpack_kernel(x_ref, w_ref, k_ref):
    width = w_ref.shape[1]
    cols = width // LANES
    share = HEAD // 8 * cols // 2 // GROUP
    for z in range(2):
        for j in range(GROUP):
            x = x_ref[j // 2 * 2 + z, j % 2].astype(F32)
            for i in range(share):
                n = j * share + i
                r, c = 8 * (n // (cols // 2)), width // 2 * z + LANES * (n % (cols // 2))
                w_ref[r : r + 8, c : c + LANES] = x[8 * i : 8 * i + 8, :]
    for j in range(GROUP):
        x = x_ref[j // 2 * 2, j % 2].astype(F32) + x_ref[j // 2 * 2 + 1, j % 2].astype(F32)
        for i in range(4):
            if 4 * j + i < TAPS:
                for c in range(cols):
                    at = 8 * share + cols * i + c
                    k_ref[4 * j + i : 4 * j + i + 1, c * LANES : (c + 1) * LANES] = x[at : at + 1, :]


def unpack(x, width):
    return pl.pallas_call(
        unpack_kernel,
        out_shape=(
            jax.ShapeDtypeStruct((HEAD, width), F32),
            jax.ShapeDtypeStruct((TAPS, width), F32),
        ),
        compiler_params=params(12),
        cost_estimate=cost(1e6, 1e6),
        name="unpack",
    )(x)


def in_hbm(x):
    return pltpu.with_memory_space_constraint(x, pltpu.HBM)


def exchange(x, axis, groups=None):
    return lax.all_to_all(
        x, axis, split_axis=0, concat_axis=0, tiled=True, axis_index_groups=groups
    )


def shards(query_proj, key_proj, value_proj, residual, lengths, out_weight, conv_kernel, cotangent):
    rows, width = query_proj.shape[1:]
    count = lax.axis_size("seq")
    me = lax.axis_index("seq")
    res, cot = residual[0], cotangent[0]
    up = [(i, i + 1) for i in range(count - 1)]
    down = [(i + 1, i) for i in range(count - 1)]
    cores = [(i, i ^ 1) for i in range(count)]
    batch = lax.axis_size("dp")
    depth = lax.axis_index("dp")
    levels = [(i, i ^ 2) for i in range(batch)]

    def hop(k):
        return [(i, i ^ (4 * (k // 2) + k % 2)) for i in range(batch)]

    query, key, value, res, cot, out_weight, conv_kernel = (
        in_hbm(x)
        for x in (query_proj[0], key_proj[0], value_proj[0], res, cot, out_weight, conv_kernel)
    )
    payload, edge_up, edge_down = pre(query, key, value, res, cot)
    heads = exchange(payload, "seq")
    heads, edge_up, edge_down = lax.optimization_barrier((heads, edge_up, edge_down))
    left = lax.ppermute(edge_up, "seq", up)
    right = lax.ppermute(edge_down, "seq", down)
    weights, mixed, inv, payload = fwd(lengths, heads)
    payload, left, right = lax.optimization_barrier((payload, left, right))
    attended = exchange(payload, "seq")
    own = attended[:, 0:HEAD]
    att_level = lax.ppermute(own, "dp", levels)
    att_core = lax.ppermute(own, "seq", cores)
    member = depth // 4
    info = jnp.stack([lengths[0], me * rows, me % 2, depth // 2 % 2, member]).astype(jnp.int32)
    block_out, payload, keep, send = conv(
        info, attended, res, cot, in_hbm(left), in_hbm(right), out_weight, conv_kernel
    )
    att_level, payload = lax.optimization_barrier((att_level, payload))
    att_both = lax.ppermute(att_level, "seq", cores)
    grads = exchange(payload, "seq")
    level = lax.ppermute(send, "dp", levels)
    partner = lax.ppermute(keep, "seq", cores)
    both = lax.ppermute(level, "seq", cores)
    partial = outer(
        info, (own, att_core, att_level, att_both), (in_hbm(keep), partner, level, both)
    )
    partial = exchange(tail(grads, partial), "seq")
    payload = bwd(heads, grads, in_hbm(weights), in_hbm(mixed), inv)
    payload, partial = lax.optimization_barrier((payload, partial))
    back = exchange(payload, "seq")
    packed = pack(info, partial)
    level_parts = [in_hbm(packed[0])] + [
        lax.ppermute(packed[k], "dp", hop(2 * k)) for k in range(1, GROUP // 2)
    ]
    merged = merge(level_parts)
    summed = total(in_hbm(merged), lax.ppermute(merged, "dp", hop(1)))
    summed, back = lax.optimization_barrier((summed, back))
    column = [[i for i in range(batch) if i % 2 == y] for y in range(2)]
    final = exchange(summed, "dp", column)
    query_grad, key_grad, value_grad = post(back)
    weight_grad, kernel_grad = unpack(final, width)
    return (
        block_out[None],
        query_grad[None],
        key_grad[None],
        value_grad[None],
        weight_grad,
        kernel_grad,
    )


def solution(mesh):
    split = P("dp", "seq", None)
    return jax.shard_map(
        shards,
        mesh=mesh,
        in_specs=(split, split, split, split, P("dp"), P(), P(), split),
        out_specs=(split, split, split, split, P("seq", None), P()),
        check_vma=False,
    )
```

```python
import math

import jax
import jax.numpy as jnp
from jax import lax
from jax.experimental import pallas as pl
from jax.experimental.pallas import tpu as pltpu
from jax.sharding import PartitionSpec as P

HEADS = 16
HEAD = 96
LANES = 128
TAPS = 31
HALF = 15
HALO = 32
NEAR = 16
QT = 512
KT = 256
BF = jnp.bfloat16
F32 = jnp.float32
MIB = 2**20


def params(mib):
    return pltpu.CompilerParams(vmem_limit_bytes=mib * MIB)


def cost(flops, moved):
    return pl.CostEstimate(flops=int(flops), bytes_accessed=int(moved), transcendentals=0)


def lane_iota(shape):
    return lax.broadcasted_iota(jnp.int32, shape, len(shape) - 1)


def row_iota(shape):
    return lax.broadcasted_iota(jnp.int32, shape, 0)


def dot(a, b):
    return jnp.dot(a, b, preferred_element_type=F32)


def pre_kernel(q_hbm, k_hbm, v_hbm, res_hbm, cot_hbm, o_ref, up_ref, down_ref, buf, sems):
    rows = q_hbm.shape[0]
    loads = [
        pltpu.make_async_copy(ref, buf.at[i], sems.at[i])
        for i, ref in enumerate((q_hbm, k_hbm, v_hbm))
    ]
    edges = [
        pltpu.make_async_copy(ref.at[pl.ds(lo, size)], out.at[pl.ds(at, size)], sems.at[n])
        for n, ref, lo, size, out, at in (
            (3, res_hbm, rows - HALO, HALO, up_ref, 0),
            (4, cot_hbm, rows - NEAR, NEAR, up_ref, HALO),
            (5, res_hbm, 0, HALO, down_ref, 0),
            (6, cot_hbm, 0, NEAR, down_ref, HALO),
        )
    ]
    for copy in loads + edges:
        copy.start()
    for part, copy in enumerate(loads):
        copy.wait()
        turned = buf[part].T
        for h in range(HEADS):
            o_ref[h, part * HEAD : (part + 1) * HEAD, :] = turned[h * HEAD : (h + 1) * HEAD, :]
    for copy in edges:
        copy.wait()


def pre(q, k, v, res, cot):
    edge = jax.ShapeDtypeStruct((HALO + NEAR, q.shape[1]), BF)
    return pl.pallas_call(
        pre_kernel,
        out_shape=(jax.ShapeDtypeStruct((HEADS, 3 * HEAD, LANES), BF), edge, edge),
        in_specs=[pl.BlockSpec(memory_space=pltpu.HBM)] * 5,
        scratch_shapes=[pltpu.VMEM((3,) + q.shape, BF), pltpu.SemaphoreType.DMA((7,))],
        compiler_params=params(8),
        cost_estimate=cost(1e6, 3e6),
        name="pre",
    )(q, k, v, res, cot)


def fwd_kernel(len_ref, x_ref, e_hbm, o_ref, inv_ref, pay_ref, kaug, vaug, even, odd, ebuf, sems):
    blocks = x_ref.shape[0]
    frames = blocks * LANES
    scale = math.log2(math.e) / math.sqrt(HEAD)
    length = len_ref[0]
    for j in range(blocks):
        rows = slice(j * LANES, (j + 1) * LANES)
        bias = jnp.where(j * LANES + lane_iota((32, LANES)) < length, 0.0, -1e30)
        bias = jnp.where(row_iota((32, LANES)) == 0, bias, 0.0)
        turned = jnp.concatenate([x_ref[j, HEAD : 2 * HEAD, :], bias.astype(BF)], axis=0).T
        kaug[rows, 0:LANES] = turned
        kaug[rows, LANES : 2 * LANES] = turned
        vaug[0:HEAD, rows] = x_ref[j, 2 * HEAD : 3 * HEAD, :]
        vaug[HEAD : HEAD + 16, rows] = jnp.where(row_iota((16, LANES)) == 0, 1.0, 0.0).astype(BF)
    per = QT // LANES
    count = frames // QT
    tiles = frames // KT
    one = jnp.where(row_iota((32, QT)) == 0, 1.0, 0.0).astype(BF)

    def queries(i):
        qt = jnp.concatenate([x_ref[i * per + p, 0:HEAD, :] for p in range(per)], axis=1)
        qs = qt.astype(F32) * scale
        hi = qs.astype(BF)
        lo = (qs - hi.astype(F32)).astype(BF)
        return jnp.concatenate([hi, one, lo, jnp.zeros((32, QT), BF)], axis=0)

    def score(buf, t, qaug, top):
        s = dot(kaug[t * KT : (t + 1) * KT, :], qaug)
        buf[t * KT : (t + 1) * KT, :] = s
        part = jnp.max(s.reshape(KT // 8, 8, QT), axis=0)
        return part if top is None else jnp.maximum(top, part)

    def out_copy(i, t):
        at = pl.ds(t * KT, 2 * KT)
        return pltpu.make_async_copy(ebuf.at[i, at], e_hbm.at[i, at], sems.at[i, t // 2])

    bufs = (even, odd)
    top = None
    qaug = queries(0)
    for t in range(tiles):
        top = score(bufs[0], t, qaug, top)
    for i in range(count):
        peak = jnp.max(top, axis=0, keepdims=True)
        top = None
        if i + 1 < count:
            qaug = queries(i + 1)
        acc = jnp.zeros((HEAD + 16, QT), F32)
        for t in range(tiles):
            rows = slice(t * KT, (t + 1) * KT)
            if i + 1 < count:
                top = score(bufs[(i + 1) % 2], t, qaug, top)
            e = jnp.exp2(bufs[i % 2][rows, :] - peak).astype(BF)
            ebuf[i, rows, :] = e
            acc = acc + dot(vaug[:, rows], e)
            if t % 2 == 1:
                out_copy(i, t - 1).start()
        inv = 1.0 / acc[HEAD : HEAD + 1, :]
        out = acc[0:HEAD, :] * inv
        at = slice(i * QT, (i + 1) * QT)
        o_ref[:, at] = out
        inv_ref[:, at] = jnp.broadcast_to(inv, (8, QT))
        rounded = out.astype(BF)
        for p in range(per):
            pay_ref[i * per + p, 0:HEAD, :] = rounded[:, p * LANES : (p + 1) * LANES]
    low = HEAD // 2
    lane = lane_iota((low, LANES))
    left = lane < LANES // 2
    outer_lanes = jnp.logical_or(lane < HALO, lane >= LANES - HALO)
    for j in range(blocks):
        after = pay_ref[min(j + 1, blocks - 1), 0:HEAD, :].astype(F32)
        before = pay_ref[max(j - 1, 0), 0:HEAD, :].astype(F32)
        first = jnp.where(left, after[0:low], before[0:low])
        second = jnp.where(left, after[low:HEAD], before[low:HEAD])
        second = pltpu.roll(second, LANES // 2, 1)
        pay_ref[j, HEAD : HEAD + low, :] = jnp.where(outer_lanes, first, second).astype(BF)
    for i in range(count):
        for t in range(0, tiles, 2):
            out_copy(i, t).wait()


def fwd(length, x):
    blocks = x.shape[0]
    frames = blocks * LANES
    steps = frames // QT
    return pl.pallas_call(
        fwd_kernel,
        out_shape=(
            pltpu.HBM((steps, frames, QT), BF),
            pltpu.HBM((HEAD, frames), F32),
            jax.ShapeDtypeStruct((8, frames), F32),
            jax.ShapeDtypeStruct((blocks, HEAD + HEAD // 2, LANES), BF),
        ),
        in_specs=[pl.BlockSpec(memory_space=pltpu.SMEM), pl.BlockSpec()],
        out_specs=(
            pl.BlockSpec(memory_space=pl.ANY),
            pl.BlockSpec(),
            pl.BlockSpec(),
            pl.BlockSpec(),
        ),
        scratch_shapes=[
            pltpu.VMEM((frames, 2 * LANES), BF),
            pltpu.VMEM((HEAD + 16, frames), BF),
            pltpu.VMEM((frames, QT), F32),
            pltpu.VMEM((frames, QT), F32),
            pltpu.VMEM((steps, frames, QT), BF),
            pltpu.SemaphoreType.DMA((steps, frames // KT // 2)),
        ],
        compiler_params=params(30),
        cost_estimate=cost(9e9, 1e7),
        name="attend",
    )(length, x)


def conv_kernel_body(
    info_ref, att_ref, res_hbm, cot_hbm, left_hbm, right_hbm, w_hbm, taps_hbm,
    out_hbm, pay_hbm, keep_hbm, send_hbm,
    lhs, block_in, masked, cot, grad, taps_sum, bg_ref,
    res_ref, cot_ref, left_ref, right_ref, weight, taps_ref, proj, out_ref, pay_ref, sems,
):
    rows, width = res_ref.shape
    cols = width // LANES
    span = rows + 2 * HALO
    length = info_ref[0]
    first = info_ref[1]
    zbit = info_ref[3]
    pieces = cols // 2
    wide = 2 * LANES

    def chunk(n):
        at = pl.ds(pl.multiple_of(n * wide, wide), wide)
        return pltpu.make_async_copy(w_hbm.at[:, at], weight.at[:, at], sems.at[n])

    small = [
        pltpu.make_async_copy(src, dst, sems.at[pieces + n])
        for n, (src, dst) in enumerate(
            (
                (res_hbm, res_ref),
                (cot_hbm, cot_ref),
                (left_hbm, left_ref),
                (right_hbm, right_ref),
                (taps_hbm, taps_ref),
            )
        )
    ]
    chunk(0).start()
    for load in small:
        load.start()
    for n in range(1, pieces):
        chunk(n).start()
    main = jnp.concatenate([att_ref[h, 0:HEAD, :] for h in range(HEADS)], axis=0)
    packed = [att_ref[h, HEAD : HEAD + HEAD // 2, :].astype(F32) for h in range(HEADS)]
    halo = jnp.concatenate(
        [part for p in packed for part in (p, pltpu.roll(p, LANES // 2, 1))], axis=0
    ).astype(BF)
    halo = halo.T
    lhs[0:HALO, :] = halo[LANES - HALO : LANES, :]
    lhs[HALO : HALO + rows, :] = main.T
    lhs[HALO + rows : span, :] = halo[0:HALO, :]
    frame = first - HALO + row_iota((span, LANES))
    valid = jnp.logical_and(frame >= 0, frame < length)
    mid = rows + 32

    def project(n):
        at = pl.ds(pl.multiple_of(n * wide, wide), wide)
        proj[...] = dot(lhs[...], weight[:, at])

    def place(n):
        for m in range(2):
            c = 2 * n + m
            at = pl.ds(pl.multiple_of(c * LANES, LANES), LANES)
            res = jnp.concatenate(
                [left_ref[0:HALO, at], res_ref[:, at], right_ref[0:HALO, at]], axis=0
            ).astype(F32)
            block = res + proj[:, m * LANES : (m + 1) * LANES]
            block_in[c] = block
            masked[c] = jnp.where(valid, block, 0.0).astype(BF).astype(F32)
            cot[c] = jnp.concatenate(
                [
                    left_ref[HALO : HALO + NEAR, at],
                    cot_ref[:, at],
                    right_ref[HALO : HALO + NEAR, at],
                ],
                axis=0,
            ).astype(F32)

    for load in small:
        load.wait()
    chunk(0).wait()
    project(0)
    place(0)

    def channels(c):
        at = pl.ds(pl.multiple_of(c * LANES, LANES), LANES)
        acc = jnp.zeros((mid, LANES), F32)
        for r in range(TAPS):
            acc = acc + taps_ref[r : r + 1, at] * masked[c, 1 + r : 1 + r + mid, :]
        gate = jax.nn.sigmoid(acc)
        cg = (cot[c] * (gate * (1.0 + acc * (1.0 - gate)))).astype(BF).astype(F32)
        grad[...] = cg
        out_ref[:, at] = (
            block_in[c, HALO : HALO + rows, :] + (acc * gate)[16 : 16 + rows, :]
        ).astype(BF)
        own = cg[16 : 16 + rows, :]
        back = jnp.zeros((rows, LANES), F32)
        for r in range(TAPS):
            back = back + taps_ref[r : r + 1, at] * grad[31 - r : 31 - r + rows, :]
            prod = own * masked[c, 17 + r : 17 + r + rows, :]
            prod = jnp.sum(prod.reshape(rows // 8, 8, LANES), axis=0)
            taps_sum[r // 2, pl.ds((r % 2) * cols + c, 1), :] = jnp.sum(prod, axis=0, keepdims=True)
        own_valid = valid[HALO : HALO + rows, :]
        bg_ref[:, at] = (cot[c, 16 : 16 + rows, :] + jnp.where(own_valid, back, 0.0)).astype(BF)

    @pl.loop(0, pieces)
    def _(n):
        @pl.when(n < pieces - 1)
        def _():
            chunk(n + 1).wait()

        after = lax.rem(n + 1, pieces)
        project(after)
        channels(2 * n)
        channels(2 * n + 1)
        place(after)

    taps_sum[HEADS - 1, pl.ds(cols, cols), :] = jnp.zeros((cols, LANES), F32)
    taps_sum[:, pl.ds(2 * cols, 8), :] = jnp.zeros((HEADS, 8, LANES), F32)
    half = width // 2
    mine = pl.ds(pl.multiple_of(zbit * half, LANES), half)
    other = pl.ds(pl.multiple_of((1 - zbit) * half, LANES), half)
    stores = [
        pltpu.make_async_copy(src, dst, sems.at[pieces + 5 + n])
        for n, (src, dst) in enumerate(
            (
                (bg_ref.at[:, other], send_hbm),
                (bg_ref.at[:, mine], keep_hbm),
                (out_ref, out_hbm),
            )
        )
    ]
    for store in stores:
        store.start()
    pay_ref[:, HEAD:LANES, :] = taps_sum[...].astype(BF)
    bg = bg_ref[...]
    for h in range(0, HEADS, 2):
        mixed = lax.dot_general(
            weight[h * HEAD : (h + 2) * HEAD, :], bg, (((1,), (1,)), ((), ())),
            preferred_element_type=F32,
        ).astype(BF)
        pay_ref[h, 0:HEAD, :] = mixed[0:HEAD]
        pay_ref[h + 1, 0:HEAD, :] = mixed[HEAD : 2 * HEAD]
        if h % 4 == 2:
            at = pl.ds(h - 2, 4)
            store = pltpu.make_async_copy(
                pay_ref.at[at], pay_hbm.at[at], sems.at[pieces + 8 + h // 4]
            )
            store.start()
            stores.append(store)
    for store in stores:
        store.wait()


def conv(info, att, res, cot, left, right, w, taps):
    rows, width = res.shape
    cols = width // LANES
    span = rows + 2 * HALO
    vm = pl.BlockSpec()
    return pl.pallas_call(
        conv_kernel_body,
        out_shape=(
            pltpu.HBM((rows, width), BF),
            pltpu.HBM((HEADS, LANES, LANES), BF),
            pltpu.HBM((rows, width // 2), BF),
            pltpu.HBM((rows, width // 2), BF),
        ),
        in_specs=[pl.BlockSpec(memory_space=pltpu.SMEM)]
        + [vm]
        + [pl.BlockSpec(memory_space=pl.ANY)] * 6,
        out_specs=(
            pl.BlockSpec(memory_space=pl.ANY),
        )
        * 4,
        scratch_shapes=[
            pltpu.VMEM((span, width), BF),
            pltpu.VMEM((cols, span, LANES), F32),
            pltpu.VMEM((cols, span, LANES), F32),
            pltpu.VMEM((cols, rows + 32, LANES), F32),
            pltpu.VMEM((rows + 32, LANES), F32),
            pltpu.VMEM((HEADS, 32, LANES), F32),
            pltpu.VMEM((rows, width), BF),
            pltpu.VMEM((rows, width), BF),
            pltpu.VMEM((rows, width), BF),
            pltpu.VMEM((HALO + NEAR, width), BF),
            pltpu.VMEM((HALO + NEAR, width), BF),
            pltpu.VMEM((width, width), BF),
            pltpu.VMEM((TAPS, width), F32),
            pltpu.VMEM((span, 2 * LANES), F32),
            pltpu.VMEM((rows, width), BF),
            pltpu.VMEM((HEADS, LANES, LANES), BF),
            pltpu.SemaphoreType.DMA((cols // 2 + 12,)),
        ],
        compiler_params=params(20),
        cost_estimate=cost(9e9, 1e7),
        name="convolve",
    )(info, att, res, cot, left, right, w, taps)


def outer_kernel(info_ref, *refs):
    o_ref = refs[-1]
    core = info_ref[2]
    tall, wide = refs[0:4], refs[4:8]
    part = wide[0].shape[1] // 2
    at = pl.ds(pl.multiple_of(core * part, LANES), part)
    rhs = jnp.concatenate([ref[:, at] for ref in wide], axis=0)
    for h in range(0, HEADS, 4):
        lhs = jnp.concatenate(
            [
                jnp.concatenate([ref[g, 0:HEAD, :] for ref in tall], axis=1)
                for g in range(h, h + 4)
            ],
            axis=0,
        )
        full = dot(lhs, rhs).astype(BF)
        for g in range(4):
            for c in range(part // LANES):
                o_ref[h + g, c * HEAD : (c + 1) * HEAD, :] = full[
                    g * HEAD : (g + 1) * HEAD, c * LANES : (c + 1) * LANES
                ]


def outer(info, tall, wide):
    part = wide[0].shape[1] // 2
    return pl.pallas_call(
        outer_kernel,
        out_shape=pltpu.HBM((HEADS, part // LANES * HEAD + 32, LANES), BF),
        in_specs=[pl.BlockSpec(memory_space=pltpu.SMEM)] + [pl.BlockSpec()] * 8,
        compiler_params=params(20),
        cost_estimate=cost(1e9, 4e6),
        name="outer",
    )(info, *tall, *wide)


def tail_kernel(g_ref, w_ref, o_ref, taps, sems):
    taps[...] = jnp.sum(g_ref[:, HEAD:LANES, :].astype(F32), axis=0).astype(BF)
    base = o_ref.shape[1] - 32
    copies = [
        pltpu.make_async_copy(taps, o_ref.at[h, pl.ds(base, 32), :], sems.at[h])
        for h in range(HEADS)
    ]
    for copy in copies:
        copy.start()
    for copy in copies:
        copy.wait()


def tail(g, w):
    return pl.pallas_call(
        tail_kernel,
        out_shape=pltpu.HBM(w.shape, BF),
        in_specs=[pl.BlockSpec(), pl.BlockSpec(memory_space=pl.ANY)],
        out_specs=pl.BlockSpec(memory_space=pl.ANY),
        scratch_shapes=[pltpu.VMEM((32, LANES), BF), pltpu.SemaphoreType.DMA((HEADS,))],
        input_output_aliases={1: 0},
        compiler_params=params(8),
        cost_estimate=cost(1e6, 1e6),
        name="tail",
    )(g, w)


def bwd_kernel(x_ref, g_ref, e_ref, o_ref, inv_ref, pay_ref, vaug, kt, dk, dv):
    step = pl.program_id(0)
    blocks = x_ref.shape[0]
    scale = 1.0 / math.sqrt(HEAD)

    @pl.when(step == 0)
    def _():
        ones = jnp.where(row_iota((32, LANES)) < 3, 1.0, 0.0).astype(BF)
        for j in range(blocks):
            rows = pl.ds(j * LANES, LANES)
            turned = jnp.concatenate([x_ref[j, 2 * HEAD : 3 * HEAD, :], ones], axis=0).T
            vaug[rows, 0:LANES] = turned
            vaug[rows, LANES : 2 * LANES] = turned
            kt[:, rows] = x_ref[j, HEAD : 2 * HEAD, :]
        dk[...] = jnp.zeros_like(dk)
        dv[...] = jnp.zeros_like(dv)

    per = QT // LANES
    gt = jnp.concatenate([g_ref[step * per + p, 0:HEAD, :] for p in range(per)], axis=1).astype(F32)
    qt = jnp.concatenate([x_ref[step * per + p, 0:HEAD, :] for p in range(per)], axis=1)
    inv = inv_ref[0:1, :]
    centre = jnp.sum(gt * o_ref[...], axis=0, keepdims=True)
    ginv = gt * inv
    sg = ginv * scale
    hi = sg.astype(BF)
    lo = (sg - hi.astype(F32)).astype(BF)
    rest = centre * inv * (-scale)
    c0 = rest.astype(BF).astype(F32)
    c1 = (rest - c0).astype(BF).astype(F32)
    c2 = rest - c0 - c1
    at = row_iota((32, QT))
    crows = jnp.where(at == 0, c0, jnp.where(at == 1, c1, jnp.where(at == 2, c2, 0.0))).astype(BF)
    zeros = jnp.zeros((32, QT), BF)
    gaug = jnp.concatenate([hi, crows, lo, zeros], axis=0)
    gn = jnp.concatenate([ginv.astype(BF), zeros], axis=0).T
    qn = jnp.concatenate([qt, zeros], axis=0).T
    dq = jnp.zeros((HEAD, QT), F32)
    for t in range(kt.shape[1] // KT):
        rows = slice(t * KT, (t + 1) * KT)
        slope = dot(vaug[rows, :], gaug)
        e = e_ref[0, rows, :]
        ds = (e.astype(F32) * slope).astype(BF)
        dv[rows, :] += dot(e, gn)
        dk[rows, :] += dot(ds, qn)
        dq = dq + dot(kt[:, rows], ds)
    dq = dq.astype(BF)
    for p in range(per):
        pay_ref[step * per + p, 0:HEAD, :] = dq[:, p * LANES : (p + 1) * LANES]

    @pl.when(step == pl.num_programs(0) - 1)
    def _():
        for j in range(blocks):
            rows = pl.ds(j * LANES, LANES)
            pay_ref[j, HEAD : 2 * HEAD, :] = dk[rows, :].T[0:HEAD].astype(BF)
            pay_ref[j, 2 * HEAD : 3 * HEAD, :] = dv[rows, :].T[0:HEAD].astype(BF)


def bwd(x, g, e, o, inv):
    blocks = x.shape[0]
    frames = blocks * LANES
    steps = frames // QT
    return pl.pallas_call(
        bwd_kernel,
        grid=(steps,),
        out_shape=pltpu.HBM((blocks, 3 * HEAD, LANES), BF),
        in_specs=[
            pl.BlockSpec((blocks, 3 * HEAD, LANES), lambda i: (0, 0, 0)),
            pl.BlockSpec((blocks, LANES, LANES), lambda i: (0, 0, 0)),
            pl.BlockSpec((1, frames, QT), lambda i: (i, 0, 0)),
            pl.BlockSpec((HEAD, QT), lambda i: (0, i)),
            pl.BlockSpec((8, QT), lambda i: (0, i)),
        ],
        out_specs=pl.BlockSpec((blocks, 3 * HEAD, LANES), lambda i: (0, 0, 0)),
        scratch_shapes=[
            pltpu.VMEM((frames, 2 * LANES), BF),
            pltpu.VMEM((HEAD, frames), BF),
            pltpu.VMEM((frames, LANES), F32),
            pltpu.VMEM((frames, LANES), F32),
        ],
        compiler_params=params(30),
        cost_estimate=cost(2e10, 1e7),
        name="attend_back",
    )(x, g, e, o, inv)


def post_kernel(x_ref, q_ref, k_ref, v_ref):
    for part, ref in enumerate((q_ref, k_ref, v_ref)):
        rows = slice(part * HEAD, (part + 1) * HEAD)
        ref[...] = jnp.concatenate([x_ref[h, rows, :] for h in range(HEADS)], axis=0).T


def post(x):
    shape = jax.ShapeDtypeStruct((LANES, HEADS * HEAD), BF)
    return pl.pallas_call(
        post_kernel,
        out_shape=(shape,) * 3,
        compiler_params=params(12),
        cost_estimate=cost(1e6, 3e6),
        name="post",
    )(x)


GROUP = 8
PIECE = 120


def pack_kernel(info_ref, x_ref, *refs):
    outs, buf = refs[:-1], refs[-1]
    cols = x_ref.shape[1] // HEAD
    below = cols * HEAD
    for r in range(HEAD // 16):
        for c in range(2 * cols):
            at = (c % cols) * HEAD + 16 * r
            tiles = [x_ref[2 * i + c // cols, at : at + 16, :].astype(F32) for i in range(HEADS // 2)]
            both = sum(tiles[1:], tiles[0])
            for e in range(2):
                n = (2 * r + e) * 2 * cols + c
                buf[8 * n : 8 * n + 8, :] = both[8 * e : 8 * e + 8, :]
    share = buf.shape[0] // GROUP
    for k in range(GROUP):
        j = jnp.bitwise_xor(info_ref[4], k)
        taps = [x_ref[2 * j + e, below : below + 32, :].astype(F32)[0:24] for e in range(2)]
        outs[k // 2][k % 2] = jnp.concatenate(
            [buf[pl.ds(pl.multiple_of(share * j, 8), share), :]] + taps, axis=0
        ).astype(BF)


def pack(info, x):
    units = x.shape[1] // HEAD * HEAD * 2
    return pl.pallas_call(
        pack_kernel,
        out_shape=(jax.ShapeDtypeStruct((2, PIECE, LANES), BF),) * (GROUP // 2),
        in_specs=[pl.BlockSpec(memory_space=pltpu.SMEM), pl.BlockSpec()],
        scratch_shapes=[pltpu.VMEM((units, LANES), F32)],
        compiler_params=params(12),
        cost_estimate=cost(1e6, 3e6),
        name="pack",
    )(info, x)


def merge_kernel(*refs):
    keep_ref, send_ref = refs[-2:]
    both = sum([ref[...].astype(F32) for ref in refs[1:-2]], refs[0][...].astype(F32))
    keep_ref[...] = both[0].astype(BF)
    send_ref[...] = both[1].astype(BF)


def merge(xs):
    return pl.pallas_call(
        merge_kernel,
        out_shape=(jax.ShapeDtypeStruct(xs[0].shape[1:], BF),) * 2,
        compiler_params=params(8),
        cost_estimate=cost(1e6, 1e6),
        name="merge",
    )(*xs)


def total_kernel(*refs):
    o_ref = refs[-1]
    total = sum([ref[...].astype(F32) for ref in refs[1:-1]], refs[0][...].astype(F32))
    total = total * (1.0 / o_ref.shape[0])
    o_ref[...] = jnp.broadcast_to(total.astype(BF)[None], o_ref.shape)


def total(xs, batch):
    return pl.pallas_call(
        total_kernel,
        out_shape=jax.ShapeDtypeStruct((batch,) + xs[0].shape, BF),
        compiler_params=params(12),
        cost_estimate=cost(1e6, 1e6),
        name="total",
    )(*xs)


def unpack_kernel(x_ref, w_ref, k_ref):
    width = w_ref.shape[1]
    cols = width // LANES
    share = HEAD // 8 * cols // 2 // GROUP
    for z in range(2):
        for j in range(GROUP):
            x = x_ref[4 * (j // 2) + 2 * z + j % 2].astype(F32)
            for i in range(share):
                n = j * share + i
                r, c = 8 * (n // (cols // 2)), width // 2 * z + LANES * (n % (cols // 2))
                w_ref[r : r + 8, c : c + LANES] = x[8 * i : 8 * i + 8, :]
    for j in range(GROUP):
        x = x_ref[4 * (j // 2) + j % 2].astype(F32) + x_ref[4 * (j // 2) + 2 + j % 2].astype(F32)
        for i in range(4):
            if 4 * j + i < TAPS:
                for c in range(cols):
                    at = 8 * share + cols * i + c
                    k_ref[4 * j + i : 4 * j + i + 1, c * LANES : (c + 1) * LANES] = x[at : at + 1, :]


def unpack(x, width):
    return pl.pallas_call(
        unpack_kernel,
        out_shape=(
            jax.ShapeDtypeStruct((HEAD, width), F32),
            jax.ShapeDtypeStruct((TAPS, width), F32),
        ),
        compiler_params=params(12),
        cost_estimate=cost(1e6, 1e6),
        name="unpack",
    )(x)


def in_hbm(x):
    return pltpu.with_memory_space_constraint(x, pltpu.HBM)


def exchange(x, axis, groups=None):
    return lax.all_to_all(
        x, axis, split_axis=0, concat_axis=0, tiled=True, axis_index_groups=groups
    )


def shards(query_proj, key_proj, value_proj, residual, lengths, out_weight, conv_kernel, cotangent):
    rows, width = query_proj.shape[1:]
    count = lax.axis_size("seq")
    me = lax.axis_index("seq")
    res, cot = residual[0], cotangent[0]
    up = [(i, i + 1) for i in range(count - 1)]
    down = [(i + 1, i) for i in range(count - 1)]
    cores = [(i, i ^ 1) for i in range(count)]
    batch = lax.axis_size("dp")
    depth = lax.axis_index("dp")
    levels = [(i, i ^ 2) for i in range(batch)]

    def hop(k):
        return [(i, i ^ (4 * (k // 2) + k % 2)) for i in range(batch)]

    query, key, value, res, cot, out_weight, conv_kernel = (
        in_hbm(x)
        for x in (query_proj[0], key_proj[0], value_proj[0], res, cot, out_weight, conv_kernel)
    )
    payload, edge_up, edge_down = pre(query, key, value, res, cot)
    heads = exchange(payload, "seq")
    left = lax.ppermute(edge_up, "seq", up)
    right = lax.ppermute(edge_down, "seq", down)
    heads, left, right = lax.optimization_barrier((heads, left, right))
    weights, mixed, inv, payload = fwd(lengths, heads)
    attended = exchange(payload, "seq")
    own = attended[:, 0:HEAD]
    att_level = lax.ppermute(own, "dp", levels)
    att_core = lax.ppermute(own, "seq", cores)
    member = depth // 4 * 2 + depth % 2
    info = jnp.stack([lengths[0], me * rows, me % 2, depth // 2 % 2, member]).astype(jnp.int32)
    block_out, payload, keep, send = conv(
        info, attended, res, cot, in_hbm(left), in_hbm(right), out_weight, conv_kernel
    )
    att_level, payload = lax.optimization_barrier((att_level, payload))
    att_both = lax.ppermute(att_level, "seq", cores)
    grads = exchange(payload, "seq")
    level = lax.ppermute(send, "dp", levels)
    partner = lax.ppermute(keep, "seq", cores)
    both = lax.ppermute(level, "seq", cores)
    partial = outer(
        info, (own, att_core, att_level, att_both), (in_hbm(keep), partner, level, both)
    )
    partial = exchange(tail(grads, partial), "seq")
    payload = bwd(heads, grads, in_hbm(weights), in_hbm(mixed), inv)
    payload, partial = lax.optimization_barrier((payload, partial))
    back = exchange(payload, "seq")
    packed = pack(info, partial)
    level_parts = [packed[0]] + [
        lax.ppermute(packed[k], "dp", hop(2 * k)) for k in range(1, GROUP // 2)
    ]
    keep, send = merge(level_parts)
    packed = [keep, lax.ppermute(send, "dp", hop(1))]
    summed, back = lax.optimization_barrier((total(packed, batch), back))
    final = exchange(summed, "dp")
    query_grad, key_grad, value_grad = post(back)
    weight_grad, kernel_grad = unpack(final, width)
    return (
        block_out[None],
        query_grad[None],
        key_grad[None],
        value_grad[None],
        weight_grad,
        kernel_grad,
    )


def solution(mesh):
    split = P("dp", "seq", None)
    return jax.shard_map(
        shards,
        mesh=mesh,
        in_specs=(split, split, split, split, P("dp"), P(), P(), split),
        out_specs=(split, split, split, split, P("seq", None), P()),
        check_vma=False,
    )
```
